32 devices in a mesh: row: 8 (over y, x, core), col: 4 (over z).
Axes of the slice: x: 2, y: 2, z: 4, core: 2. Of those that a mesh axis runs over, the one named last changes fastest.
Arguments:
- inverse_front: float32 [16384, 16384], P('row', 'col'), may hold values from -0.09375 to 0.09375
- factor: float32 [4096, 1024], P('row'), may hold values from -1.2 to 1.2
- unit_lower: float32 [2, 512, 512], replicated, may hold values from -0.25 to 0.25
- pivot_inverse: float32 [2, 512], replicated, may hold values from 0.5 to 4
- tile_list: int32 [2, 16], replicated, may hold values from 0 to 63, as said below
- tile_valid: int32 [2, 16], replicated, may hold values from 0 to 1, as said below
Outputs:
- inverse_column: float32 [16384, 1024], P('row')
- diagonal_block: float32 [2, 512, 512], replicated
The draws below stay inside these ranges and needn't reach their ends.
Inputs may be any that keep to these rules, and one draw needn't show every extreme that they name: `tile_list`: each row names 16 different tile rows of the front in increasing order, exactly 2 of them among each aligned group of 8 tile rows, and the last tile row is always among them. `tile_valid`: each row holds at least one 1.
All inputs are finite; a program needn't handle non-finite values.
Results may differ from the reference program's by a relative error of at most 0.0001.
Values sent between devices are 32-bit elements; how exact they have to be, the bound alone decides.
No kernel may reach another device: no remote copies, remote signals or barrier semaphores. Data moves between devices by JAX's collectives and lax.ppermute only.
A program may use at most 256 MiB of HBM per device.

```python
import math
import jax
import jax.numpy as jnp
from jax import lax

F = 16384
B = 256
W = 512
NS = 2
NA = 16
R = 4096
N_ROW = 8


def draw_tile_list(key, part):
    group_tiles = F // (B * N_ROW)
    picks = NA // N_ROW
    local = jnp.arange(group_tiles, dtype=jnp.int32)
    noise = jax.random.randint(jax.random.fold_in(key, 11), (NS, N_ROW, group_tiles), 0, 1000, dtype=jnp.int32)
    scores = noise * group_tiles + local[None, None, :]
    last_group = jnp.arange(N_ROW, dtype=jnp.int32)[None, :, None] == N_ROW - 1
    last_tile = local[None, None, :] == group_tiles - 1
    scores = jnp.where(last_group & last_tile, 4000 * group_tiles, scores)
    picked = lax.top_k(scores, picks)[1]
    picked = jnp.sort(picked, axis=2)
    base = (jnp.arange(N_ROW, dtype=jnp.int32) * group_tiles)[None, :, None]
    return (picked + base).reshape(NS, NA).astype(jnp.int32)


def draw_tile_valid(key, part):
    mask = jax.random.randint(jax.random.fold_in(key, 21), (NS, NA), 0, 4, dtype=jnp.int32) < 3
    forced = jax.random.randint(jax.random.fold_in(key, 22), (NS, 1), 0, NA, dtype=jnp.int32)
    slot = jnp.arange(NA, dtype=jnp.int32)[None, :]
    return (mask | (slot == forced)).astype(jnp.int32)


def block_levels(stream_key, extent, split, low, largest):
    level, own = 1.0, jax.random.fold_in(stream_key, 6)
    for dim, blocks in split:
        draws = jnp.exp(jax.random.uniform(jax.random.fold_in(own, dim), (blocks,), jnp.float32, low / len(split), largest / len(split)))
        level = level * jnp.repeat(draws, extent[dim] // blocks).reshape([-1 if axis == dim else 1 for axis in range(len(extent))])
    return level


def centred(stream_key, shape, width, reach, shards=(), kind=jnp.bfloat16):
    level = block_levels(stream_key, shape, shards, -0.22, 0.18) if shards else 1.0
    entries = jax.random.normal(stream_key, shape, jnp.float32) * width * level
    return jnp.minimum(jnp.maximum(entries, -reach), reach).astype(kind)


def setup_inputs(seed: int = 0) -> dict:
    arg_keys = jax.random.split(jax.random.key(seed), 7)
    return {
        "inverse_front": centred(arg_keys[0], (F, F), (NA * B) ** -0.5, 0.09375, ((0, 8), (1, 4)), jnp.float32),
        "factor": centred(arg_keys[1], (R, NS * W), 0.2, 1.2, ((0, 8),), jnp.float32),
        "unit_lower": centred(arg_keys[2], (NS, W, W), W ** -0.5, 0.25, (), jnp.float32),
        "pivot_inverse": jnp.clip(jnp.exp(jax.random.uniform(arg_keys[3], (NS, W), jnp.float32, math.log(0.5), math.log(4.0))), 0.5, 4.0),
        "tile_list": draw_tile_list(jax.random.fold_in(arg_keys[6], 71), 0),
        "tile_valid": draw_tile_valid(jax.random.fold_in(arg_keys[6], 71), 0),
    }


def reference(inverse_front, factor, unit_lower, pivot_inverse, tile_list, tile_valid):
    identity = jnp.eye(W, dtype=jnp.float32)
    result = jnp.zeros((F, NS * W), jnp.float32)
    blocks = []
    for member in range(NS):
        inverse_s = jnp.tril(unit_lower[member], -1) + identity
        slab = factor[:, member * W:(member + 1) * W]
        normalized = jnp.dot(slab, inverse_s, precision=lax.Precision.HIGHEST, preferred_element_type=jnp.float32)
        row_keep = jnp.repeat(tile_valid[member].astype(jnp.float32), B)
        normalized = normalized * row_keep[:, None]
        row_global = (tile_list[member][:, None] * B + jnp.arange(B, dtype=jnp.int32)[None, :]).reshape(-1).astype(jnp.int32)
        picked_rows = jnp.take(inverse_front, row_global, axis=0)
        gathered = jnp.take(picked_rows, row_global, axis=1)
        symmetric = jnp.where(row_global[:, None] >= row_global[None, :], gathered, gathered.T)
        column = -jnp.dot(symmetric, normalized, precision=lax.Precision.HIGHEST, preferred_element_type=jnp.float32)
        column = column * row_keep[:, None]
        result = result.at[row_global, member * W:(member + 1) * W].set(column)
        base_block = jnp.dot(inverse_s.T * pivot_inverse[member][None, :], inverse_s, precision=lax.Precision.HIGHEST, preferred_element_type=jnp.float32)
        update = jnp.dot(normalized.T, column, precision=lax.Precision.HIGHEST, preferred_element_type=jnp.float32)
        blocks.append(base_block - update)
    return result, jnp.stack(blocks)
```

```python
import functools

import jax
import jax.numpy as jnp
from jax import lax
from jax.experimental import pallas as pl
from jax.experimental.pallas import tpu as pltpu
from jax.sharding import PartitionSpec as P

F32 = jnp.float32
BF16 = jnp.bfloat16
VMEM = pltpu.MemorySpace.VMEM
SMEM = pltpu.MemorySpace.SMEM
PARAMS = pltpu.CompilerParams(vmem_limit_bytes=48 * 1024 * 1024)


def vmem(count):
    return [pl.BlockSpec(memory_space=VMEM)] * count


def smem(count):
    return [pl.BlockSpec(memory_space=SMEM)] * count


def split(x):
    high = x.astype(BF16)
    return high, (x - high.astype(F32)).astype(BF16)


def product(left, right, contract=1):
    def one(a, b):
        return lax.dot_general(a, b, (((contract,), (0,)), ((), ())), preferred_element_type=F32)

    return one(left[0], right[1]) + one(left[1], right[0]) + one(left[0], right[0])


def unit_inverse(ref, member):
    lower = ref[member]
    row = lax.broadcasted_iota(jnp.int32, lower.shape, 0)
    col = lax.broadcasted_iota(jnp.int32, lower.shape, 1)
    return jnp.where(row > col, lower, jnp.where(row == col, 1.0, 0.0).astype(F32))


class Plan:
    def __init__(self, front, factor, unit_lower, tile_list):
        self.rows, self.cols = lax.axis_size("row"), lax.axis_size("col")
        self.lanes = self.rows // self.cols
        self.members, self.width, _ = unit_lower.shape
        self.na = tile_list.shape[1] // self.rows
        self.tile = factor.shape[0] // self.na
        self.nb = self.na * self.lanes
        self.row_tiles = front.shape[0] // self.tile
        self.col_tiles = front.shape[1] // self.tile
        self.depth = factor.shape[0]
        bits = [1 << i for i in range((self.cols - 1).bit_length())]
        self.orders = [
            bits[lane % len(bits):] + bits[:lane % len(bits)] for lane in range(self.lanes)
        ]
        self.steps = len(bits)

    def device(self, chip, lane, col):
        return (chip * self.lanes + lane) * self.cols + col

    def tree(self, step):
        pairs = []
        for col in range(self.cols):
            for lane, order in enumerate(self.orders):
                held, later = [0], [0]
                for bit in order[:step]:
                    held = held + [x ^ bit for x in held]
                for bit in order[step + 1:]:
                    later = later + [x ^ bit for x in later]
                for offset in held:
                    child = col ^ offset ^ order[step]
                    if any(child ^ x > col for x in later):
                        pairs.append(
                            (self.device(col ^ offset, lane, col), self.device(child, lane, col))
                        )
        return pairs

    def received(self, step):
        row, col = lax.axis_index("row"), lax.axis_index("col")
        offset = (row // self.lanes) ^ col
        got = False
        for lane, order in enumerate(self.orders):
            later = sum(order[step + 1:])
            here = ((offset & order[step]) != 0) & ((offset & later) == 0)
            got = got | (here & (row % self.lanes == lane))
        return got

    def swap(self, x, shift):
        pairs = []
        for row in range(self.rows):
            chip, lane = divmod(row, self.lanes)
            pairs.append((chip * self.lanes + (lane + shift) % self.lanes, row))
        return lax.ppermute(x, "row", pairs)

    def spread(self, x):
        for step in range(self.steps):
            got = lax.ppermute(x, ("row", "col"), self.tree(step))
            x = jnp.where(self.received(step), got, x)
        return x

    def collect(self, x):
        for step in reversed(range(self.steps)):
            pairs = [(child, parent) for parent, child in self.tree(step)]
            x = x + lax.ppermute(x, ("row", "col"), pairs)
        return x

    def line_sum(self, x):
        count, half = self.cols, self.cols // 2
        place = lax.axis_index("col")
        for i in range(half - 1):
            x = x + lax.ppermute(x, "col", [(i, i + 1), (count - 1 - i, count - 2 - i)])
        x = x + lax.ppermute(x, "col", [(half - 1, half), (half, half - 1)])
        for i in range(half - 1):
            got = lax.ppermute(x, "col", [(half - 1 - i, half - 2 - i), (half + i, half + i + 1)])
            x = jnp.where((place == half - 2 - i) | (place == half + i + 1), got, x)
        return x


def gather_kernel(plan, member, tiles_ref, valid_ref, front, factor, high, low, *rest):
    mirror, (buffer, sems) = rest[:plan.lanes], rest[plan.lanes:]
    size, na, nb = plan.tile, plan.na, plan.nb
    row, col = lax.axis_index("row"), lax.axis_index("col")
    lane = lax.rem(row, plan.lanes)
    row_slots = [row * na + a for a in range(na)]
    col_slots = [
        col * nb + lax.rem(lane + b // na, plan.lanes) * na + b % na for b in range(nb)
    ]
    copies = []
    for a in range(na):
        for b in range(nb):
            i = jnp.clip(tiles_ref[member, row_slots[a]] - row * plan.row_tiles, 0, plan.row_tiles - 1)
            j = jnp.clip(tiles_ref[member, col_slots[b]] - col * plan.col_tiles, 0, plan.col_tiles - 1)
            copy = pltpu.make_async_copy(
                front.at[
                    pl.ds(pl.multiple_of(i * size, size), size),
                    pl.ds(pl.multiple_of(j * size, size), size),
                ],
                buffer.at[a, b],
                sems.at[a, b],
            )
            copy.start()
            copies.append(copy)
    right = split(factor[...])
    local_row = lax.broadcasted_iota(jnp.int32, (size, size), 0)
    local_col = lax.broadcasted_iota(jnp.int32, (size, size), 1)
    for a in range(na):
        for b in range(nb):
            copies[a * nb + b].wait()
            live = (valid_ref[member, row_slots[a]] > 0) & (valid_ref[member, col_slots[b]] > 0)
            ahead = (tiles_ref[member, row_slots[a]] - tiles_ref[member, col_slots[b]]) * size
            gap = local_row - local_col + ahead
            x = buffer[a, b]
            x = jnp.where(gap > 0, x, jnp.where(gap == 0, 0.5 * x, 0.0))
            x = jnp.where(live, x, 0.0)
            x_high, x_low = split(x)
            high[a * size:(a + 1) * size, b * size:(b + 1) * size] = x_high
            low[a * size:(a + 1) * size, b * size:(b + 1) * size] = x_low
    for b in range(nb):
        left = (high[:, b * size:(b + 1) * size], low[:, b * size:(b + 1) * size])
        first = b % na * size
        mirror[b // na][first:first + size, :] = product(left, right, contract=0)


def forward_kernel(plan, high, low, factor, *rest):
    parts, (total, cross) = rest[:plan.lanes], rest[plan.lanes:]
    size, depth = plan.tile, plan.depth
    right = [split(part[...]) for part in parts]
    for a in range(plan.na):
        rows = slice(a * size, (a + 1) * size)
        total[rows, :] = sum(
            product(
                (high[rows, i * depth:(i + 1) * depth], low[rows, i * depth:(i + 1) * depth]),
                right[i],
            )
            for i in range(plan.lanes)
        )
    cross[...] = product(split(factor[...]), split(total[...]), contract=0)


def place_kernel(plan, tiles_ref, unit_ref, *rest):
    sums, (out, stack, sem) = rest[:plan.members], rest[plan.members:]
    size, width = plan.tile, plan.width
    row = lax.axis_index("row")
    for member in range(plan.members):
        right = split(unit_inverse(unit_ref, member))
        stack[member, plan.na] = jnp.zeros((size, width), F32)
        for a in range(plan.na):
            left = split(sums[member][a * size:(a + 1) * size, :])
            stack[member, a] = -product(left, right)
        copies = []
        for t in range(plan.row_tiles):
            slot = jnp.int32(plan.na)
            for a in range(plan.na):
                slot = jnp.where(
                    tiles_ref[member, row * plan.na + a] == row * plan.row_tiles + t, a, slot
                )
            copy = pltpu.make_async_copy(
                stack.at[member, slot],
                out.at[t * size:(t + 1) * size, member * width:(member + 1) * width],
                sem.at[member, t],
            )
            copy.start()
            copies.append(copy)
        if member == plan.members - 1:
            last = copies
        else:
            for copy in copies:
                copy.wait()
    for copy in last:
        copy.wait()


def diagonal_kernel(plan, cross, pivot, unit_ref, out):
    width = plan.width
    row = lax.broadcasted_iota(jnp.int32, (width, width), 0)
    col = lax.broadcasted_iota(jnp.int32, (width, width), 1)
    for member in range(plan.members):
        inverse = split(unit_inverse(unit_ref, member))
        x = cross[member]
        x = jnp.where(row == col, pivot[member:member + 1, :], 0.0) + x + x.T
        half = product(split(x), inverse)
        out[member] = product(inverse, split(half), contract=0)


def shards(inverse_front, factor, unit_lower, pivot_inverse, tile_list, tile_valid):
    plan = Plan(inverse_front, factor, unit_lower, tile_list)
    width, depth, lanes = plan.width, plan.depth, plan.lanes
    row, col = lax.axis_index("row"), lax.axis_index("col")
    on_diagonal = row // lanes == col
    flops = 6 * depth * depth * lanes * width
    sums, crosses = [], []
    for member in range(plan.members):
        own = factor[:, member * width:(member + 1) * width]
        high, low, *mirror = pl.pallas_call(
            functools.partial(gather_kernel, plan, member),
            in_specs=smem(2) + [pl.BlockSpec(memory_space=pl.ANY)] + vmem(1),
            out_specs=vmem(2 + lanes),
            out_shape=[jax.ShapeDtypeStruct((depth, depth * lanes), BF16)] * 2
            + [jax.ShapeDtypeStruct((depth, width), F32)] * lanes,
            scratch_shapes=[
                pltpu.VMEM((plan.na, plan.nb, plan.tile, plan.tile), F32),
                pltpu.SemaphoreType.DMA((plan.na, plan.nb)),
            ],
            compiler_params=PARAMS,
            cost_estimate=pl.CostEstimate(flops=flops, bytes_accessed=8 << 20, transcendentals=0),
            name="gather_mirror",
        )(tile_list, tile_valid, inverse_front, own)
        back = mirror[0]
        for shift in range(1, lanes):
            back = back + plan.swap(mirror[lanes - shift], shift)
        back = plan.collect(back)
        held = plan.spread(own)
        parts = [held] + [plan.swap(held, shift) for shift in range(1, lanes)]
        total, cross = pl.pallas_call(
            functools.partial(forward_kernel, plan),
            in_specs=vmem(3 + lanes),
            out_specs=vmem(2),
            out_shape=[
                jax.ShapeDtypeStruct((depth, width), F32),
                jax.ShapeDtypeStruct((width, width), F32),
            ],
            compiler_params=PARAMS,
            cost_estimate=pl.CostEstimate(flops=flops, bytes_accessed=8 << 20, transcendentals=0),
            name="forward",
        )(high, low, own, *parts)
        sums.append(plan.line_sum(total + jnp.where(on_diagonal, back, 0.0)))
        crosses.append(cross)
    column = pl.pallas_call(
        functools.partial(place_kernel, plan),
        in_specs=smem(1) + vmem(1 + plan.members),
        out_specs=pl.BlockSpec(memory_space=pl.ANY),
        out_shape=jax.ShapeDtypeStruct((inverse_front.shape[0], factor.shape[1]), F32),
        scratch_shapes=[
            pltpu.VMEM((plan.members, plan.na + 1, plan.tile, width), F32),
            pltpu.SemaphoreType.DMA((plan.members, plan.row_tiles)),
        ],
        compiler_params=PARAMS,
        name="place",
    )(tile_list, unit_lower, *sums)
    cross = lax.psum(jnp.stack(crosses), ("row", "col"))
    diagonal = pl.pallas_call(
        functools.partial(diagonal_kernel, plan),
        in_specs=vmem(3),
        out_specs=vmem(1)[0],
        out_shape=jax.ShapeDtypeStruct(unit_lower.shape, F32),
        compiler_params=PARAMS,
        name="diagonal",
    )(cross, pivot_inverse, unit_lower)
    return (column, diagonal)


def solution(mesh):
    in_specs = (P("row", "col"), P("row", None), P(), P(), P(), P())
    out_specs = (P("row", None), P())
    return jax.shard_map(shards, mesh=mesh, in_specs=in_specs, out_specs=out_specs, check_vma=False)
```

```python
import functools

import jax
import jax.numpy as jnp
from jax import lax
from jax.experimental import pallas as pl
from jax.experimental.pallas import tpu as pltpu
from jax.sharding import PartitionSpec as P

F32 = jnp.float32
BF16 = jnp.bfloat16
VMEM = pltpu.MemorySpace.VMEM
SMEM = pltpu.MemorySpace.SMEM
SPLIT = 2
PARAMS = pltpu.CompilerParams(vmem_limit_bytes=48 * 1024 * 1024)


def vmem(count):
    return [pl.BlockSpec(memory_space=VMEM)] * count


def smem(count):
    return [pl.BlockSpec(memory_space=SMEM)] * count


def split(x):
    high = x.astype(BF16)
    return high, (x - high.astype(F32)).astype(BF16)


def product(left, right, contract=1):
    def one(a, b):
        return lax.dot_general(a, b, (((contract,), (0,)), ((), ())), preferred_element_type=F32)

    return one(left[0], right[1]) + one(left[1], right[0]) + one(left[0], right[0])


def unit_inverse(ref, member):
    lower = ref[member]
    row = lax.broadcasted_iota(jnp.int32, lower.shape, 0)
    col = lax.broadcasted_iota(jnp.int32, lower.shape, 1)
    return jnp.where(row > col, lower, jnp.where(row == col, 1.0, 0.0).astype(F32))


class Plan:
    def __init__(self, front, factor, unit_lower, tile_list):
        self.rows, self.cols = lax.axis_size("row"), lax.axis_size("col")
        self.lanes = self.rows // self.cols
        self.members, self.width, _ = unit_lower.shape
        self.na = tile_list.shape[1] // self.rows
        self.tile = factor.shape[0] // self.na
        self.nb = self.na * self.lanes
        self.row_tiles = front.shape[0] // self.tile
        self.col_tiles = front.shape[1] // self.tile
        self.depth = factor.shape[0]
        bits = [1 << i for i in range((self.cols - 1).bit_length())]
        self.orders = [
            bits[lane % len(bits):] + bits[:lane % len(bits)] for lane in range(self.lanes)
        ]
        self.steps = len(bits)

    def device(self, chip, lane, col):
        return (chip * self.lanes + lane) * self.cols + col

    def tree(self, step):
        pairs = []
        for col in range(self.cols):
            for lane, order in enumerate(self.orders):
                held, later = [0], [0]
                for bit in order[:step]:
                    held = held + [x ^ bit for x in held]
                for bit in order[step + 1:]:
                    later = later + [x ^ bit for x in later]
                for offset in held:
                    child = col ^ offset ^ order[step]
                    if any(child ^ x > col for x in later):
                        pairs.append(
                            (self.device(col ^ offset, lane, col), self.device(child, lane, col))
                        )
        return pairs

    def received(self, step):
        row, col = lax.axis_index("row"), lax.axis_index("col")
        offset = (row // self.lanes) ^ col
        got = False
        for lane, order in enumerate(self.orders):
            later = sum(order[step + 1:])
            here = ((offset & order[step]) != 0) & ((offset & later) == 0)
            got = got | (here & (row % self.lanes == lane))
        return got

    def rounds(self):
        pairs = [[], []]
        for turn, col, chip, plane in (
            (0, 0, 1, 0), (1, 0, 2, 0), (0, 0, 3, 3), (0, 1, 3, 1), (1, 1, 2, 3), (0, 2, 3, 2),
        ):
            for lane in range(self.lanes):
                pairs[(turn + lane) % 2].append(
                    (self.device(col, lane, plane), self.device(chip, lane, col))
                )
        return pairs

    def swap(self, x, shift):
        pairs = []
        for row in range(self.rows):
            chip, lane = divmod(row, self.lanes)
            pairs.append((chip * self.lanes + (lane + shift) % self.lanes, row))
        return lax.ppermute(x, "row", pairs)

    def spread(self, x, on_diagonal):
        if self.cols == 4:
            first, second = (lax.ppermute(x, ("row", "col"), pairs) for pairs in self.rounds())
            return jnp.where(on_diagonal, x, first + second), (first, second)
        for step in range(self.steps):
            got = lax.ppermute(x, ("row", "col"), self.tree(step))
            x = jnp.where(self.received(step), got, x)
        return x, (x,)

    def collect(self, x, on_diagonal):
        if self.cols == 4:
            first, second = (
                lax.ppermute(x, ("row", "col"), [(child, parent) for parent, child in pairs])
                for pairs in self.rounds()
            )
            return jnp.where(on_diagonal, x, 0.0) + first + second, (first, second)
        for step in reversed(range(self.steps)):
            pairs = [(child, parent) for parent, child in self.tree(step)]
            x = x + lax.ppermute(x, ("row", "col"), pairs)
        return jnp.where(on_diagonal, x, 0.0), (x,)

    def line_sum(self, x):
        count, half = self.cols, self.cols // 2
        place = lax.axis_index("col")
        for i in range(half - 1):
            x = x + lax.ppermute(x, "col", [(i, i + 1), (count - 1 - i, count - 2 - i)])
        x = x + lax.ppermute(x, "col", [(half - 1, half), (half, half - 1)])
        got = x
        for i in range(half - 1):
            got = lax.ppermute(x, "col", [(half - 1 - i, half - 2 - i), (half + i, half + i + 1)])
            if i < half - 2:
                x = jnp.where((place == half - 2 - i) | (place == half + i + 1), got, x)
        return x, got

    def at_end(self):
        place = lax.axis_index("col")
        return (place == 0) | (place == self.cols - 1)

    def bit_pairs(self, step):
        return [
            (self.device(chip, lane, col), self.device(chip ^ order[step], lane, col))
            for chip in range(self.cols)
            for lane, order in enumerate(self.orders)
            for col in range(self.cols)
        ]

    def bit(self, step):
        row = lax.axis_index("row")
        chip, value = row // self.lanes, jnp.int32(0)
        for lane, order in enumerate(self.orders):
            value = jnp.where((row % self.lanes == lane) & ((chip & order[step]) != 0), 1, value)
        return value

    def sum_all(self, x):
        for step in range(self.steps):
            x = x.reshape(2, x.shape[0] // 2, x.shape[1])
            bit = self.bit(step)
            send = lax.dynamic_index_in_dim(x, 1 - bit, 0, keepdims=False)
            keep = lax.dynamic_index_in_dim(x, bit, 0, keepdims=False)
            x = keep + lax.ppermute(send, ("row", "col"), self.bit_pairs(step))
        x, got = self.line_sum(x)
        x = jnp.where(self.at_end(), got, x)
        for step in reversed(range(self.steps)):
            got = lax.ppermute(x, ("row", "col"), self.bit_pairs(step))
            bit = self.bit(step) == 1
            x = jnp.concatenate([jnp.where(bit, got, x), jnp.where(bit, x, got)])
        return x


def gather_kernel(plan, member, tiles_ref, valid_ref, front, factor, high, low, *rest):
    mirror, (buffer, sems) = rest[:plan.lanes], rest[plan.lanes:]
    size, na, nb = plan.tile, plan.na, plan.nb
    row, col = lax.axis_index("row"), lax.axis_index("col")
    lane = lax.rem(row, plan.lanes)
    row_slots = [row * na + a for a in range(na)]
    col_slots = [
        col * nb + lax.rem(lane + b // na, plan.lanes) * na + b % na for b in range(nb)
    ]
    copies = []
    for a in range(na):
        for b in range(nb):
            i = jnp.clip(tiles_ref[member, row_slots[a]] - row * plan.row_tiles, 0, plan.row_tiles - 1)
            j = jnp.clip(tiles_ref[member, col_slots[b]] - col * plan.col_tiles, 0, plan.col_tiles - 1)
            copy = pltpu.make_async_copy(
                front.at[
                    pl.ds(pl.multiple_of(i * size, size), size),
                    pl.ds(pl.multiple_of(j * size, size), size),
                ],
                buffer.at[a, b],
                sems.at[a, b],
            )
            copy.start()
            copies.append(copy)
    right = split(factor[...])
    local_row = lax.broadcasted_iota(jnp.int32, (size, size), 0)
    local_col = lax.broadcasted_iota(jnp.int32, (size, size), 1)
    for a in range(na):
        for b in range(nb):
            copies[a * nb + b].wait()
            live = (valid_ref[member, row_slots[a]] > 0) & (valid_ref[member, col_slots[b]] > 0)
            ahead = (tiles_ref[member, row_slots[a]] - tiles_ref[member, col_slots[b]]) * size
            gap = local_row - local_col + ahead
            x = buffer[a, b]
            x = jnp.where(gap > 0, x, jnp.where(gap == 0, 0.5 * x, 0.0))
            x = jnp.where(live, x, 0.0)
            x_high, x_low = split(x)
            high[a * size:(a + 1) * size, b * size:(b + 1) * size] = x_high
            low[a * size:(a + 1) * size, b * size:(b + 1) * size] = x_low
    for b in range(nb):
        left = (high[:, b * size:(b + 1) * size], low[:, b * size:(b + 1) * size])
        first = b % na * size
        mirror[b // na][first:first + size, :] = product(left, right, contract=0)


def forward_kernel(plan, high, low, factor, *rest):
    lanes, size, depth = plan.lanes, plan.tile, plan.depth
    parts, rest = rest[:lanes], rest[lanes:]
    totals, rest = rest[:SPLIT], rest[SPLIT:]
    cross, (total, whole) = rest[:lanes], rest[lanes:]
    right = [split(part[...]) for part in parts]
    for a in range(plan.na):
        rows = slice(a * size, (a + 1) * size)
        total[rows, :] = sum(
            product(
                (high[rows, i * depth:(i + 1) * depth], low[rows, i * depth:(i + 1) * depth]),
                right[i],
            )
            for i in range(lanes)
        )
    share = depth // SPLIT
    for i in range(SPLIT):
        totals[i][...] = total[i * share:(i + 1) * share, :]
    whole[...] = product(split(factor[...]), split(total[...]), contract=0)
    share = plan.width // lanes
    lane = lax.rem(lax.axis_index("row"), lanes)
    for i in range(lanes):
        first = pl.multiple_of(lax.rem(lane + i, lanes) * share, share)
        cross[i][...] = whole[pl.ds(first, share), :]


def place_kernel(plan, member, tiles_ref, unit_ref, *rest):
    sums, rest = rest[:2 * SPLIT], rest[2 * SPLIT:]
    out, stack, zeros, sems, zero_sems = rest[member > 0:]
    size, width = plan.tile, plan.width
    row, at_end = lax.axis_index("row"), plan.at_end()

    def zero_copies(act):
        for other in range(plan.members):
            for t in range(plan.row_tiles):
                taken = False
                for a in range(plan.na):
                    taken = taken | (
                        tiles_ref[other, row * plan.na + a] == row * plan.row_tiles + t
                    )
                copy = pltpu.make_async_copy(
                    zeros,
                    out.at[t * size:(t + 1) * size, other * width:(other + 1) * width],
                    zero_sems.at[other, t],
                )
                pl.when(jnp.logical_not(taken))(functools.partial(act, copy))

    if member == 0:
        zeros[...] = jnp.zeros_like(zeros)
        zero_copies(lambda copy: copy.start())
    right = split(unit_inverse(unit_ref, member))
    share = plan.depth // SPLIT
    for i in range(SPLIT):
        x = jnp.where(at_end, sums[2 * i + 1][...], sums[2 * i][...])
        stack[i * share:(i + 1) * share, :] = -product(split(x), right)
    copies = []
    for a in range(plan.na):
        t = jnp.clip(
            tiles_ref[member, row * plan.na + a] - row * plan.row_tiles, 0, plan.row_tiles - 1
        )
        copy = pltpu.make_async_copy(
            stack.at[a * size:(a + 1) * size, :],
            out.at[
                pl.ds(pl.multiple_of(t * size, size), size), member * width:(member + 1) * width
            ],
            sems.at[a],
        )
        copy.start()
        copies.append(copy)
    for copy in copies:
        copy.wait()
    if member == 0:
        zero_copies(lambda copy: copy.wait())


def diagonal_kernel(plan, pivot, unit_ref, *rest):
    parts, out = rest[:plan.lanes], rest[plan.lanes]
    width, lanes = plan.width, plan.lanes
    share = width // lanes
    lane = lax.rem(lax.axis_index("row"), lanes)
    row = lax.broadcasted_iota(jnp.int32, (width, width), 0)
    col = lax.broadcasted_iota(jnp.int32, (width, width), 1)
    for member in range(plan.members):
        rows = slice(member * share, (member + 1) * share)
        pieces = []
        for other in range(lanes):
            piece = parts[0][rows, :]
            for i in range(1, lanes):
                piece = jnp.where(lax.rem(lane + i, lanes) == other, parts[i][rows, :], piece)
            pieces.append(piece)
        x = jnp.concatenate(pieces)
        x = jnp.where(row == col, pivot[member:member + 1, :], 0.0) + x + x.T
        inverse = split(unit_inverse(unit_ref, member))
        half = product(split(x), inverse)
        out[member] = product(inverse, split(half), contract=0)


def shards(inverse_front, factor, unit_lower, pivot_inverse, tile_list, tile_valid):
    plan = Plan(inverse_front, factor, unit_lower, tile_list)
    width, depth, lanes = plan.width, plan.depth, plan.lanes
    row, col = lax.axis_index("row"), lax.axis_index("col")
    on_diagonal = row // lanes == col
    flops = 6 * depth * depth * lanes * width
    sums, crosses = [], []
    sent = returned = None
    for member in range(plan.members):
        own = factor[:, member * width:(member + 1) * width]
        high, low, *mirror = pl.pallas_call(
            functools.partial(gather_kernel, plan, member),
            in_specs=smem(2) + [pl.BlockSpec(memory_space=pl.ANY)] + vmem(1),
            out_specs=vmem(2 + lanes),
            out_shape=[jax.ShapeDtypeStruct((depth, depth * lanes), BF16)] * 2
            + [jax.ShapeDtypeStruct((depth, width), F32)] * lanes,
            scratch_shapes=[
                pltpu.VMEM((plan.na, plan.nb, plan.tile, plan.tile), F32),
                pltpu.SemaphoreType.DMA((plan.na, plan.nb)),
            ],
            compiler_params=PARAMS,
            cost_estimate=pl.CostEstimate(flops=flops, bytes_accessed=8 << 20, transcendentals=0),
            name="gather_mirror",
        )(tile_list, tile_valid, inverse_front, own)
        back = mirror[0]
        for shift in range(1, lanes):
            back = back + plan.swap(mirror[lanes - shift], shift)
        ready = own
        if member:
            ready, sent = lax.optimization_barrier((ready, sent))
            back, returned = lax.optimization_barrier((back, returned))
        back, returned = plan.collect(back, on_diagonal)
        held, sent = plan.spread(ready, on_diagonal)
        parts = [held] + [plan.swap(held, shift) for shift in range(1, lanes)]
        *totals_cross, = pl.pallas_call(
            functools.partial(forward_kernel, plan),
            in_specs=vmem(3 + lanes),
            out_specs=vmem(SPLIT + lanes),
            out_shape=[jax.ShapeDtypeStruct((depth // SPLIT, width), F32)] * SPLIT
            + [jax.ShapeDtypeStruct((width // lanes, width), F32)] * lanes,
            scratch_shapes=[
                pltpu.VMEM((depth, width), F32),
                pltpu.VMEM((width, width), F32),
            ],
            compiler_params=PARAMS,
            cost_estimate=pl.CostEstimate(flops=flops, bytes_accessed=8 << 20, transcendentals=0),
            name="forward",
        )(high, low, own, *parts)
        totals, cross = totals_cross[:SPLIT], totals_cross[SPLIT:]
        share = depth // SPLIT
        member_sums = []
        for i in range(SPLIT):
            member_sums += plan.line_sum(totals[i] + back[i * share:(i + 1) * share])
        sums.append(member_sums)
        reduced = cross[0]
        for shift in range(1, lanes):
            reduced = reduced + plan.swap(cross[lanes - shift], shift)
        crosses.append(reduced)
    column = None
    for member in range(plan.members):
        column = pl.pallas_call(
            functools.partial(place_kernel, plan, member),
            in_specs=smem(1) + vmem(1 + 2 * SPLIT)
            + [pl.BlockSpec(memory_space=pl.ANY)] * (member > 0),
            out_specs=pl.BlockSpec(memory_space=pl.ANY),
            out_shape=jax.ShapeDtypeStruct((inverse_front.shape[0], factor.shape[1]), F32),
            scratch_shapes=[
                pltpu.VMEM((depth, width), F32),
                pltpu.VMEM((plan.tile, width), F32),
                pltpu.SemaphoreType.DMA((plan.na,)),
                pltpu.SemaphoreType.DMA((plan.members, plan.row_tiles)),
            ],
            input_output_aliases={2 + 2 * SPLIT: 0} if member else {},
            compiler_params=PARAMS,
            cost_estimate=pl.CostEstimate(
                flops=6 * depth * width * width, bytes_accessed=8 << 20, transcendentals=0
            ),
            name="place",
        )(tile_list, unit_lower, *sums[member], *([column] if member else []))
    cross = plan.sum_all(jnp.concatenate(crosses))
    parts = [cross] + [plan.swap(cross, shift) for shift in range(1, lanes)]
    diagonal = pl.pallas_call(
        functools.partial(diagonal_kernel, plan),
        in_specs=vmem(2 + lanes),
        out_specs=vmem(1)[0],
        out_shape=jax.ShapeDtypeStruct(unit_lower.shape, F32),
        compiler_params=PARAMS,
        cost_estimate=pl.CostEstimate(
            flops=24 * width * width * width, bytes_accessed=8 << 20, transcendentals=0
        ),
        name="diagonal",
    )(pivot_inverse, unit_lower, *parts)
    return (column, diagonal)


def solution(mesh):
    in_specs = (P("row", "col"), P("row", None), P(), P(), P(), P())
    out_specs = (P("row", None), P())
    return jax.shard_map(shards, mesh=mesh, in_specs=in_specs, out_specs=out_specs, check_vma=False)
```

```python
import functools

import jax
import jax.numpy as jnp
from jax import lax
from jax.experimental import pallas as pl
from jax.experimental.pallas import tpu as pltpu
from jax.sharding import PartitionSpec as P

F32 = jnp.float32
BF16 = jnp.bfloat16
VMEM = pltpu.MemorySpace.VMEM
SMEM = pltpu.MemorySpace.SMEM
SPLIT = 2
PARAMS = pltpu.CompilerParams(vmem_limit_bytes=48 * 1024 * 1024)


def vmem(count):
    return [pl.BlockSpec(memory_space=VMEM)] * count


def smem(count):
    return [pl.BlockSpec(memory_space=SMEM)] * count


def split(x):
    high = x.astype(BF16)
    return high, (x - high.astype(F32)).astype(BF16)


def product(left, right, contract=1):
    def one(a, b):
        return lax.dot_general(a, b, (((contract,), (0,)), ((), ())), preferred_element_type=F32)

    return one(left[0], right[1]) + one(left[1], right[0]) + one(left[0], right[0])


def unit_inverse(ref, member):
    lower = ref[member]
    row = lax.broadcasted_iota(jnp.int32, lower.shape, 0)
    col = lax.broadcasted_iota(jnp.int32, lower.shape, 1)
    return jnp.where(row > col, lower, jnp.where(row == col, 1.0, 0.0).astype(F32))


class Plan:
    def __init__(self, front, factor, unit_lower, tile_list):
        self.rows, self.cols = lax.axis_size("row"), lax.axis_size("col")
        self.lanes = self.rows // self.cols
        self.members, self.width, _ = unit_lower.shape
        self.na = tile_list.shape[1] // self.rows
        self.tile = factor.shape[0] // self.na
        self.nb = self.na * self.lanes
        self.row_tiles = front.shape[0] // self.tile
        self.col_tiles = front.shape[1] // self.tile
        self.depth = factor.shape[0]
        bits = [1 << i for i in range((self.cols - 1).bit_length())]
        self.orders = [
            bits[lane % len(bits):] + bits[:lane % len(bits)] for lane in range(self.lanes)
        ]
        self.steps = len(bits)

    def device(self, chip, lane, col):
        return (chip * self.lanes + lane) * self.cols + col

    def tree(self, step):
        pairs = []
        for col in range(self.cols):
            for lane, order in enumerate(self.orders):
                held, later = [0], [0]
                for bit in order[:step]:
                    held = held + [x ^ bit for x in held]
                for bit in order[step + 1:]:
                    later = later + [x ^ bit for x in later]
                for offset in held:
                    child = col ^ offset ^ order[step]
                    if any(child ^ x > col for x in later):
                        pairs.append(
                            (self.device(col ^ offset, lane, col), self.device(child, lane, col))
                        )
        return pairs

    def received(self, step):
        row, col = lax.axis_index("row"), lax.axis_index("col")
        offset = (row // self.lanes) ^ col
        got = False
        for lane, order in enumerate(self.orders):
            later = sum(order[step + 1:])
            here = ((offset & order[step]) != 0) & ((offset & later) == 0)
            got = got | (here & (row % self.lanes == lane))
        return got

    def rounds(self):
        ways = (
            (0, ((0, 1), (0, 2)), ((0, 2), (0, 1)), ((1, 3), (2, 3))),
            (1, ((1, 3), (1, 0)), (None, (1, 3)), ((3, 2), (0, 2))),
            (2, ((2, 3), None), (None, (2, 3)), (None, None)),
        )
        pairs = [[], [], []]
        for col, *turns in ways:
            for turn, hops in enumerate(turns):
                for lane, hop in enumerate(hops):
                    if hop is not None:
                        pairs[turn].append(tuple(self.device(chip, lane, col) for chip in hop))
        return pairs

    def swap(self, x, shift):
        pairs = []
        for row in range(self.rows):
            chip, lane = divmod(row, self.lanes)
            pairs.append((chip * self.lanes + (lane + shift) % self.lanes, row))
        return lax.ppermute(x, "row", pairs)

    def line_hops(self):
        count, half = self.cols, self.cols // 2
        inward = [[(i, i + 1), (count - 1 - i, count - 2 - i)] for i in range(half - 1)]
        outward = [
            [(half - 1 - i, half - 2 - i), (half + i, half + i + 1)] for i in range(half - 1)
        ]
        return inward + [[(half - 1, half), (half, half - 1)]] + outward

    def line_step(self, hop, x, got):
        half = self.cols // 2
        if hop < half:
            return x + got
        place, i = lax.axis_index("col"), hop - half
        return jnp.where((place == half - 2 - i) | (place == half + i + 1), got, x)

    def at_end(self):
        place = lax.axis_index("col")
        return (place == 0) | (place == self.cols - 1)

    def bit_pairs(self, step):
        return [
            (self.device(chip, lane, col), self.device(chip ^ order[step], lane, col))
            for chip in range(self.cols)
            for lane, order in enumerate(self.orders)
            for col in range(self.cols)
        ]

    def bit(self, step):
        row = lax.axis_index("row")
        chip, value = row // self.lanes, jnp.int32(0)
        for lane, order in enumerate(self.orders):
            value = jnp.where((row % self.lanes == lane) & ((chip & order[step]) != 0), 1, value)
        return value


class Chain:
    def __init__(self):
        self.last = ()

    def issue(self, *requests):
        out = []
        for x, axis, pairs in requests:
            if self.last:
                x, _ = lax.optimization_barrier((x, self.last))
            out.append(lax.ppermute(x, axis, pairs))
        self.last = tuple(out)
        return out


def gather_kernel(plan, member, tiles_ref, valid_ref, front, factor, high, low, *rest):
    mirror, (buffer, sems) = rest[:plan.lanes], rest[plan.lanes:]
    size, na, nb = plan.tile, plan.na, plan.nb
    row, col = lax.axis_index("row"), lax.axis_index("col")
    lane = lax.rem(row, plan.lanes)
    row_slots = [row * na + a for a in range(na)]
    col_slots = [
        col * nb + lax.rem(lane + b // na, plan.lanes) * na + b % na for b in range(nb)
    ]
    copies = []
    for a in range(na):
        for b in range(nb):
            i = jnp.clip(tiles_ref[member, row_slots[a]] - row * plan.row_tiles, 0, plan.row_tiles - 1)
            j = jnp.clip(tiles_ref[member, col_slots[b]] - col * plan.col_tiles, 0, plan.col_tiles - 1)
            copy = pltpu.make_async_copy(
                front.at[
                    pl.ds(pl.multiple_of(i * size, size), size),
                    pl.ds(pl.multiple_of(j * size, size), size),
                ],
                buffer.at[a, b],
                sems.at[a, b],
            )
            copy.start()
            copies.append(copy)
    right = split(factor[...])
    local_row = lax.broadcasted_iota(jnp.int32, (size, size), 0)
    local_col = lax.broadcasted_iota(jnp.int32, (size, size), 1)
    for a in range(na):
        for b in range(nb):
            copies[a * nb + b].wait()
            live = (valid_ref[member, row_slots[a]] > 0) & (valid_ref[member, col_slots[b]] > 0)
            ahead = (tiles_ref[member, row_slots[a]] - tiles_ref[member, col_slots[b]]) * size
            gap = local_row - local_col + ahead
            x = buffer[a, b]
            x = jnp.where(gap > 0, x, jnp.where(gap == 0, 0.5 * x, 0.0))
            x = jnp.where(live, x, 0.0)
            x_high, x_low = split(x)
            high[a * size:(a + 1) * size, b * size:(b + 1) * size] = x_high
            low[a * size:(a + 1) * size, b * size:(b + 1) * size] = x_low
    for b in range(nb):
        left = (high[:, b * size:(b + 1) * size], low[:, b * size:(b + 1) * size])
        first = b % na * size
        mirror[b // na][first:first + size, :] = product(left, right, contract=0)


def forward_kernel(plan, high, low, factor, *rest):
    lanes, size, depth = plan.lanes, plan.tile, plan.depth
    parts, rest = rest[:lanes], rest[lanes:]
    totals, rest = rest[:SPLIT], rest[SPLIT:]
    cross, (total, whole) = rest[:lanes], rest[lanes:]
    right = [split(part[...]) for part in parts]
    for a in range(plan.na):
        rows = slice(a * size, (a + 1) * size)
        total[rows, :] = sum(
            product(
                (high[rows, i * depth:(i + 1) * depth], low[rows, i * depth:(i + 1) * depth]),
                right[i],
            )
            for i in range(lanes)
        )
    share = depth // SPLIT
    for i in range(SPLIT):
        totals[i][...] = total[i * share:(i + 1) * share, :]
    whole[...] = product(split(factor[...]), split(total[...]), contract=0)
    share = plan.width // lanes
    lane = lax.rem(lax.axis_index("row"), lanes)
    for i in range(lanes):
        first = pl.multiple_of(lax.rem(lane + i, lanes) * share, share)
        cross[i][...] = whole[pl.ds(first, share), :]


def place_kernel(plan, member, tiles_ref, unit_ref, *rest):
    sums, rest = rest[:2 * SPLIT], rest[2 * SPLIT:]
    out, stack, zeros, sems, zero_sems = rest[member > 0:]
    size, width = plan.tile, plan.width
    row, at_end = lax.axis_index("row"), plan.at_end()

    def zero_copies(act):
        for other in range(plan.members):
            for t in range(plan.row_tiles):
                taken = False
                for a in range(plan.na):
                    taken = taken | (
                        tiles_ref[other, row * plan.na + a] == row * plan.row_tiles + t
                    )
                copy = pltpu.make_async_copy(
                    zeros,
                    out.at[t * size:(t + 1) * size, other * width:(other + 1) * width],
                    zero_sems.at[other, t],
                )
                pl.when(jnp.logical_not(taken))(functools.partial(act, copy))

    if member == 0:
        zeros[...] = jnp.zeros_like(zeros)
        zero_copies(lambda copy: copy.start())
    right = split(unit_inverse(unit_ref, member))
    share = plan.depth // SPLIT
    for i in range(SPLIT):
        x = jnp.where(at_end, sums[2 * i + 1][...], sums[2 * i][...])
        stack[i * share:(i + 1) * share, :] = -product(split(x), right)
    copies = []
    for a in range(plan.na):
        t = jnp.clip(
            tiles_ref[member, row * plan.na + a] - row * plan.row_tiles, 0, plan.row_tiles - 1
        )
        copy = pltpu.make_async_copy(
            stack.at[a * size:(a + 1) * size, :],
            out.at[
                pl.ds(pl.multiple_of(t * size, size), size), member * width:(member + 1) * width
            ],
            sems.at[a],
        )
        copy.start()
        copies.append(copy)
    for copy in copies:
        copy.wait()
    if member == 0:
        zero_copies(lambda copy: copy.wait())


def diagonal_kernel(plan, pivot, unit_ref, *rest):
    parts, out = rest[:plan.lanes], rest[plan.lanes]
    width, lanes = plan.width, plan.lanes
    share = width // lanes
    lane = lax.rem(lax.axis_index("row"), lanes)
    row = lax.broadcasted_iota(jnp.int32, (width, width), 0)
    col = lax.broadcasted_iota(jnp.int32, (width, width), 1)
    for member in range(plan.members):
        rows = slice(member * share, (member + 1) * share)
        pieces = []
        for other in range(lanes):
            piece = parts[0][rows, :]
            for i in range(1, lanes):
                piece = jnp.where(lax.rem(lane + i, lanes) == other, parts[i][rows, :], piece)
            pieces.append(piece)
        x = jnp.concatenate(pieces)
        x = jnp.where(row == col, pivot[member:member + 1, :], 0.0) + x + x.T
        inverse = split(unit_inverse(unit_ref, member))
        half = product(split(x), inverse)
        out[member] = product(inverse, split(half), contract=0)


def reverse(pairs):
    return [(receiver, sender) for sender, receiver in pairs]


def exchange(plan, factors, mirrors):
    row, col = lax.axis_index("row"), lax.axis_index("col")
    on_diagonal = row // plan.lanes == col
    both = ("row", "col")
    plane = Chain()
    held, back = [], []
    if plan.cols == 4 and plan.lanes == 2:
        a, b, c = plan.rounds()
        first, relayed = plane.issue((factors[0], both, a)) + [None]
        for member in range(plan.members):
            own, mirror = factors[member], mirrors(member)
            second, third, near, far = plane.issue(
                (own, both, b), (first, both, c),
                (mirror, both, reverse(b)), (mirror, both, reverse(c)),
            )
            held.append(jnp.where(on_diagonal, own, first + second + third))
            last = (mirror + far, both, reverse(a))
            if member + 1 < plan.members:
                first, relayed = plane.issue((factors[member + 1], both, a), last)
            else:
                relayed, = plane.issue(last)
            back.append(jnp.where(on_diagonal, mirror, 0.0) + near + relayed)
        return plane, held, back
    for member in range(plan.members):
        x, mirror = factors[member], mirrors(member)
        for step in range(plan.steps):
            got, = plane.issue((x, both, plan.tree(step)))
            x = jnp.where(plan.received(step), got, x)
        for step in reversed(range(plan.steps)):
            got, = plane.issue((mirror, both, reverse(plan.tree(step))))
            mirror = mirror + got
        held.append(x)
        back.append(jnp.where(on_diagonal, mirror, 0.0))
    return plane, held, back


def shards(inverse_front, factor, unit_lower, pivot_inverse, tile_list, tile_valid):
    plan = Plan(inverse_front, factor, unit_lower, tile_list)
    width, depth, lanes = plan.width, plan.depth, plan.lanes
    flops = 6 * depth * depth * lanes * width
    factors = [factor[:, member * width:(member + 1) * width] for member in range(plan.members)]
    halves = {}

    def lane_sum(parts):
        out = parts[0]
        for shift in range(1, lanes):
            out = out + plan.swap(parts[lanes - shift], shift)
        return out

    def mirrors(member):
        high, low, *mirror = pl.pallas_call(
            functools.partial(gather_kernel, plan, member),
            in_specs=smem(2) + [pl.BlockSpec(memory_space=pl.ANY)] + vmem(1),
            out_specs=vmem(2 + lanes),
            out_shape=[jax.ShapeDtypeStruct((depth, depth * lanes), BF16)] * 2
            + [jax.ShapeDtypeStruct((depth, width), F32)] * lanes,
            scratch_shapes=[
                pltpu.VMEM((plan.na, plan.nb, plan.tile, plan.tile), F32),
                pltpu.SemaphoreType.DMA((plan.na, plan.nb)),
            ],
            compiler_params=PARAMS,
            cost_estimate=pl.CostEstimate(flops=flops, bytes_accessed=8 << 20, transcendentals=0),
            name="gather_mirror",
        )(tile_list, tile_valid, inverse_front, factors[member])
        halves[member] = (high, low)
        return lane_sum(mirror)

    plane, held, back = exchange(plan, factors, mirrors)
    share = depth // SPLIT
    chunks, crosses = [], []
    for member in range(plan.members):
        parts = [held[member]] + [plan.swap(held[member], shift) for shift in range(1, lanes)]
        *outs, = pl.pallas_call(
            functools.partial(forward_kernel, plan),
            in_specs=vmem(3 + lanes),
            out_specs=vmem(SPLIT + lanes),
            out_shape=[jax.ShapeDtypeStruct((share, width), F32)] * SPLIT
            + [jax.ShapeDtypeStruct((width // lanes, width), F32)] * lanes,
            scratch_shapes=[
                pltpu.VMEM((depth, width), F32),
                pltpu.VMEM((width, width), F32),
            ],
            compiler_params=PARAMS,
            cost_estimate=pl.CostEstimate(flops=flops, bytes_accessed=8 << 20, transcendentals=0),
            name="forward",
        )(*halves[member], factors[member], *parts)
        for i in range(SPLIT):
            chunks.append(outs[i] + back[member][i * share:(i + 1) * share])
        crosses.append(lane_sum(outs[SPLIT:]))

    x = jnp.concatenate(crosses)
    for step in range(plan.steps):
        x = x.reshape(2, x.shape[0] // 2, x.shape[1])
        bit = plan.bit(step)
        send = lax.dynamic_index_in_dim(x, 1 - bit, 0, keepdims=False)
        keep = lax.dynamic_index_in_dim(x, bit, 0, keepdims=False)
        got, = plane.issue((send, ("row", "col"), plan.bit_pairs(step)))
        x = keep + got
    chunks.append(x)

    line, hops = Chain(), plan.line_hops()
    ends = [None] * len(chunks)
    for phase in range(len(chunks) + len(hops) - 1):
        live = [i for i in range(len(chunks)) if 0 <= phase - i < len(hops)]
        brought = line.issue(*((chunks[i], "col", hops[phase - i]) for i in live))
        for i, got in zip(live, brought):
            if phase - i < len(hops) - 1 or len(hops) == 1:
                chunks[i] = plan.line_step(phase - i, chunks[i], got)
            ends[i] = got if len(hops) > 1 else chunks[i]

    column = None
    for member in range(plan.members):
        sums = []
        for i in range(member * SPLIT, (member + 1) * SPLIT):
            sums += [chunks[i], ends[i]]
        column = pl.pallas_call(
            functools.partial(place_kernel, plan, member),
            in_specs=smem(1) + vmem(1 + 2 * SPLIT)
            + [pl.BlockSpec(memory_space=pl.ANY)] * (member > 0),
            out_specs=pl.BlockSpec(memory_space=pl.ANY),
            out_shape=jax.ShapeDtypeStruct((inverse_front.shape[0], factor.shape[1]), F32),
            scratch_shapes=[
                pltpu.VMEM((depth, width), F32),
                pltpu.VMEM((plan.tile, width), F32),
                pltpu.SemaphoreType.DMA((plan.na,)),
                pltpu.SemaphoreType.DMA((plan.members, plan.row_tiles)),
            ],
            input_output_aliases={2 + 2 * SPLIT: 0} if member else {},
            compiler_params=PARAMS,
            cost_estimate=pl.CostEstimate(
                flops=6 * depth * width * width, bytes_accessed=8 << 20, transcendentals=0
            ),
            name="place",
        )(tile_list, unit_lower, *sums, *([column] if member else []))

    x = jnp.where(plan.at_end(), ends[-1], chunks[-1])
    for step in reversed(range(plan.steps)):
        got, = plane.issue((x, ("row", "col"), plan.bit_pairs(step)))
        bit = plan.bit(step) == 1
        x = jnp.concatenate([jnp.where(bit, got, x), jnp.where(bit, x, got)])
    parts = [x] + [plan.swap(x, shift) for shift in range(1, lanes)]
    diagonal = pl.pallas_call(
        functools.partial(diagonal_kernel, plan),
        in_specs=vmem(2 + lanes),
        out_specs=vmem(1)[0],
        out_shape=jax.ShapeDtypeStruct(unit_lower.shape, F32),
        compiler_params=PARAMS,
        cost_estimate=pl.CostEstimate(
            flops=24 * width * width * width, bytes_accessed=8 << 20, transcendentals=0
        ),
        name="diagonal",
    )(pivot_inverse, unit_lower, *parts)
    return (column, diagonal)


def solution(mesh):
    in_specs = (P("row", "col"), P("row", None), P(), P(), P(), P())
    out_specs = (P("row", None), P())
    return jax.shard_map(shards, mesh=mesh, in_specs=in_specs, out_specs=out_specs, check_vma=False)
```

```python
import functools

import jax
import jax.numpy as jnp
from jax import lax
from jax.experimental import pallas as pl
from jax.experimental.pallas import tpu as pltpu
from jax.sharding import PartitionSpec as P

F32 = jnp.float32
BF16 = jnp.bfloat16
VMEM = pltpu.MemorySpace.VMEM
SMEM = pltpu.MemorySpace.SMEM
SPLIT = 2
PARAMS = pltpu.CompilerParams(vmem_limit_bytes=48 * 1024 * 1024)


def vmem(count):
    return [pl.BlockSpec(memory_space=VMEM)] * count


def smem(count):
    return [pl.BlockSpec(memory_space=SMEM)] * count


def split(x):
    high = x.astype(BF16)
    return high, (x - high.astype(F32)).astype(BF16)


def product(left, right, contract=1):
    def one(a, b):
        return lax.dot_general(a, b, (((contract,), (0,)), ((), ())), preferred_element_type=F32)

    return one(left[0], right[1]) + one(left[1], right[0]) + one(left[0], right[0])


def unit_inverse(ref, member):
    lower = ref[member]
    row = lax.broadcasted_iota(jnp.int32, lower.shape, 0)
    col = lax.broadcasted_iota(jnp.int32, lower.shape, 1)
    return jnp.where(row > col, lower, jnp.where(row == col, 1.0, 0.0).astype(F32))


class Plan:
    def __init__(self, front, factor, unit_lower, tile_list):
        self.rows, self.cols = lax.axis_size("row"), lax.axis_size("col")
        self.lanes = self.rows // self.cols
        self.members, self.width, _ = unit_lower.shape
        self.na = tile_list.shape[1] // self.rows
        self.tile = factor.shape[0] // self.na
        self.nb = self.na * self.lanes
        self.row_tiles = front.shape[0] // self.tile
        self.col_tiles = front.shape[1] // self.tile
        self.depth = factor.shape[0]
        bits = [1 << i for i in range((self.cols - 1).bit_length())]
        self.orders = [
            bits[lane % len(bits):] + bits[:lane % len(bits)] for lane in range(self.lanes)
        ]
        self.steps = len(bits)

    def device(self, chip, lane, col):
        return (chip * self.lanes + lane) * self.cols + col

    def tree(self, step):
        pairs = []
        for col in range(self.cols):
            for lane, order in enumerate(self.orders):
                held, later = [0], [0]
                for bit in order[:step]:
                    held = held + [x ^ bit for x in held]
                for bit in order[step + 1:]:
                    later = later + [x ^ bit for x in later]
                for offset in held:
                    child = col ^ offset ^ order[step]
                    if any(child ^ x > col for x in later):
                        pairs.append(
                            (self.device(col ^ offset, lane, col), self.device(child, lane, col))
                        )
        return pairs

    def swap(self, x, shift):
        pairs = []
        for row in range(self.rows):
            chip, lane = divmod(row, self.lanes)
            pairs.append((chip * self.lanes + (lane + shift) % self.lanes, row))
        return lax.ppermute(x, "row", pairs)

    def line_hops(self):
        count, half = self.cols, self.cols // 2
        inward = [[(i, i + 1), (count - 1 - i, count - 2 - i)] for i in range(half - 1)]
        outward = [
            [(half - 1 - i, half - 2 - i), (half + i, half + i + 1)] for i in range(half - 1)
        ]
        return inward + [[(half - 1, half), (half, half - 1)]] + outward

    def line_step(self, hop, x, got):
        half = self.cols // 2
        if hop < half:
            return x + got
        place, i = lax.axis_index("col"), hop - half
        return jnp.where((place == half - 2 - i) | (place == half + i + 1), got, x)

    def on_diagonal(self):
        return lax.axis_index("row") // self.lanes == lax.axis_index("col")

    def at_end(self):
        place = lax.axis_index("col")
        return (place == 0) | (place == self.cols - 1)

    def bit_pairs(self, step):
        return [
            (self.device(chip, lane, col), self.device(chip ^ order[step], lane, col))
            for chip in range(self.cols)
            for lane, order in enumerate(self.orders)
            for col in range(self.cols)
        ]

    def bit(self, step):
        row = lax.axis_index("row")
        chip, value = row // self.lanes, jnp.int32(0)
        for lane, order in enumerate(self.orders):
            value = jnp.where((row % self.lanes == lane) & ((chip & order[step]) != 0), 1, value)
        return value


class Chain:
    def __init__(self):
        self.last = ()

    def issue(self, *requests, after=()):
        out = []
        for x, axis, pairs in requests:
            if self.last or after:
                x, _ = lax.optimization_barrier((x, self.last + tuple(after)))
            out.append(lax.ppermute(x, axis, pairs))
        self.last = tuple(out)
        return out


def gather_kernel(plan, member, tiles_ref, valid_ref, front, factor, high, low, *rest):
    mirror, (buffer, sems) = rest[:plan.lanes], rest[plan.lanes:]
    size, na, nb = plan.tile, plan.na, plan.nb
    row, col = lax.axis_index("row"), lax.axis_index("col")
    lane = lax.rem(row, plan.lanes)
    row_slots = [row * na + a for a in range(na)]
    col_slots = [
        col * nb + lax.rem(lane + b // na, plan.lanes) * na + b % na for b in range(nb)
    ]
    copies = []
    for a in range(na):
        for b in range(nb):
            i = jnp.clip(tiles_ref[member, row_slots[a]] - row * plan.row_tiles, 0, plan.row_tiles - 1)
            j = jnp.clip(tiles_ref[member, col_slots[b]] - col * plan.col_tiles, 0, plan.col_tiles - 1)
            copy = pltpu.make_async_copy(
                front.at[
                    pl.ds(pl.multiple_of(i * size, size), size),
                    pl.ds(pl.multiple_of(j * size, size), size),
                ],
                buffer.at[a, b],
                sems.at[a, b],
            )
            copy.start()
            copies.append(copy)
    right = split(factor[...])
    local_row = lax.broadcasted_iota(jnp.int32, (size, size), 0)
    local_col = lax.broadcasted_iota(jnp.int32, (size, size), 1)
    for a in range(na):
        for b in range(nb):
            copies[a * nb + b].wait()
            live = (valid_ref[member, row_slots[a]] > 0) & (valid_ref[member, col_slots[b]] > 0)
            ahead = (tiles_ref[member, row_slots[a]] - tiles_ref[member, col_slots[b]]) * size
            gap = local_row - local_col + ahead
            x = buffer[a, b]
            x = jnp.where(gap > 0, x, jnp.where(gap == 0, 0.5 * x, 0.0))
            x = jnp.where(live, x, 0.0)
            x_high, x_low = split(x)
            high[a * size:(a + 1) * size, b * size:(b + 1) * size] = x_high
            low[a * size:(a + 1) * size, b * size:(b + 1) * size] = x_low
    for b in range(nb):
        left = (high[:, b * size:(b + 1) * size], low[:, b * size:(b + 1) * size])
        first = b % na * size
        mirror[b // na][first:first + size, :] = product(left, right, contract=0)


def forward_kernel(plan, high, low, factor, mirror, *rest):
    lanes, size, depth = plan.lanes, plan.tile, plan.depth
    parts, rest = rest[:lanes], rest[lanes:]
    totals, rest = rest[:SPLIT], rest[SPLIT:]
    cross, (total, whole) = rest[:lanes], rest[lanes:]
    right = [split(part[...]) for part in parts]
    for a in range(plan.na):
        rows = slice(a * size, (a + 1) * size)
        total[rows, :] = sum(
            product(
                (high[rows, i * depth:(i + 1) * depth], low[rows, i * depth:(i + 1) * depth]),
                right[i],
            )
            for i in range(lanes)
        )
    share = depth // SPLIT
    on_diagonal = plan.on_diagonal()
    for i in range(SPLIT):
        rows = slice(i * share, (i + 1) * share)
        totals[i][...] = total[rows, :] + jnp.where(on_diagonal, mirror[rows, :], 0.0)
    whole[...] = product(split(factor[...]), split(total[...]), contract=0)
    share = plan.width // lanes
    lane = lax.rem(lax.axis_index("row"), lanes)
    for i in range(lanes):
        first = pl.multiple_of(lax.rem(lane + i, lanes) * share, share)
        cross[i][...] = whole[pl.ds(first, share), :]


def place_kernel(plan, member, tiles_ref, unit_ref, *rest):
    sums, rest = rest[:2 * SPLIT], rest[2 * SPLIT:]
    out, stack, zeros, sems, zero_sems = rest[member > 0:]
    size, width = plan.tile, plan.width
    row, at_end = lax.axis_index("row"), plan.at_end()

    def zero_copies(act):
        for other in range(plan.members):
            for t in range(plan.row_tiles):
                taken = False
                for a in range(plan.na):
                    taken = taken | (
                        tiles_ref[other, row * plan.na + a] == row * plan.row_tiles + t
                    )
                copy = pltpu.make_async_copy(
                    zeros,
                    out.at[t * size:(t + 1) * size, other * width:(other + 1) * width],
                    zero_sems.at[other, t],
                )
                pl.when(jnp.logical_not(taken))(functools.partial(act, copy))

    if member == 0:
        zeros[...] = jnp.zeros_like(zeros)
        zero_copies(lambda copy: copy.start())
    right = split(unit_inverse(unit_ref, member))
    share = plan.depth // SPLIT
    for i in range(SPLIT):
        x = jnp.where(at_end, sums[2 * i + 1][...], sums[2 * i][...])
        stack[i * share:(i + 1) * share, :] = -product(split(x), right)
    copies = []
    for a in range(plan.na):
        t = jnp.clip(
            tiles_ref[member, row * plan.na + a] - row * plan.row_tiles, 0, plan.row_tiles - 1
        )
        copy = pltpu.make_async_copy(
            stack.at[a * size:(a + 1) * size, :],
            out.at[
                pl.ds(pl.multiple_of(t * size, size), size), member * width:(member + 1) * width
            ],
            sems.at[a],
        )
        copy.start()
        copies.append(copy)
    for copy in copies:
        copy.wait()
    if member == 0:
        zero_copies(lambda copy: copy.wait())


def diagonal_kernel(plan, pivot, unit_ref, *rest):
    parts, out = rest[:plan.lanes], rest[plan.lanes]
    width, lanes = plan.width, plan.lanes
    share = width // lanes
    lane = lax.rem(lax.axis_index("row"), lanes)
    row = lax.broadcasted_iota(jnp.int32, (width, width), 0)
    col = lax.broadcasted_iota(jnp.int32, (width, width), 1)
    for member in range(plan.members):
        rows = slice(member * share, (member + 1) * share)
        pieces = []
        for other in range(lanes):
            piece = parts[0][rows, :]
            for i in range(1, lanes):
                piece = jnp.where(lax.rem(lane + i, lanes) == other, parts[i][rows, :], piece)
            pieces.append(piece)
        x = jnp.concatenate(pieces)
        x = jnp.where(row == col, pivot[member:member + 1, :], 0.0) + x + x.T
        inverse = split(unit_inverse(unit_ref, member))
        half = product(split(x), inverse)
        out[member] = product(inverse, split(half), contract=0)


def reverse(pairs):
    return [(receiver, sender) for sender, receiver in pairs]


def shards(inverse_front, factor, unit_lower, pivot_inverse, tile_list, tile_valid):
    plan = Plan(inverse_front, factor, unit_lower, tile_list)
    width, depth, lanes, members, steps = plan.width, plan.depth, plan.lanes, plan.members, plan.steps
    both = ("row", "col")
    share = depth // SPLIT
    flops = 6 * depth * depth * lanes * width
    factors = [factor[:, member * width:(member + 1) * width] for member in range(members)]

    def lane_sum(parts):
        out = parts[0]
        for shift in range(1, lanes):
            out = out + plan.swap(parts[lanes - shift], shift)
        return out

    def gather(member):
        return pl.pallas_call(
            functools.partial(gather_kernel, plan, member),
            in_specs=smem(2) + [pl.BlockSpec(memory_space=pl.ANY)] + vmem(1),
            out_specs=vmem(2 + lanes),
            out_shape=[jax.ShapeDtypeStruct((depth, depth * lanes), BF16)] * 2
            + [jax.ShapeDtypeStruct((depth, width), F32)] * lanes,
            scratch_shapes=[
                pltpu.VMEM((plan.na, plan.nb, plan.tile, plan.tile), F32),
                pltpu.SemaphoreType.DMA((plan.na, plan.nb)),
            ],
            compiler_params=PARAMS,
            cost_estimate=pl.CostEstimate(flops=flops, bytes_accessed=8 << 20, transcendentals=0),
            name="gather_mirror",
        )(tile_list, tile_valid, inverse_front, factors[member])

    def forward(high, low, own, mirror, held):
        parts = [held] + [plan.swap(held, shift) for shift in range(1, lanes)]
        outs = pl.pallas_call(
            functools.partial(forward_kernel, plan),
            in_specs=vmem(4 + lanes),
            out_specs=vmem(SPLIT + lanes),
            out_shape=[jax.ShapeDtypeStruct((share, width), F32)] * SPLIT
            + [jax.ShapeDtypeStruct((width // lanes, width), F32)] * lanes,
            scratch_shapes=[
                pltpu.VMEM((depth, width), F32),
                pltpu.VMEM((width, width), F32),
            ],
            compiler_params=PARAMS,
            cost_estimate=pl.CostEstimate(flops=flops, bytes_accessed=8 << 20, transcendentals=0),
            name="forward",
        )(high, low, own, mirror, *parts)
        return outs[:SPLIT], outs[SPLIT:]

    line, hops = Chain(), plan.line_hops()
    chunks, ends, phase_now = [], [], [0]

    def line_phase(after=(), beside=()):
        phase = phase_now[0]
        live = [i for i in range(len(chunks)) if 0 <= phase - i < len(hops)]
        brought = line.issue(
            *((chunks[i], "col", hops[phase - i]) for i in live), after=after
        )
        brought, beside = lax.optimization_barrier((brought, beside))
        line.last = tuple(brought)
        ends.extend([None] * (len(chunks) - len(ends)))
        for i, got in zip(live, brought):
            if phase - i < len(hops) - 1 or len(hops) == 1:
                chunks[i] = plan.line_step(phase - i, chunks[i], got)
            ends[i] = got if len(hops) > 1 else chunks[i]
        phase_now[0] += 1
        return beside

    plane = Chain()
    count = members * steps
    tiles, held, mirror, crosses = {}, {}, {}, []
    after = ()
    for phase in range(count + 1):
        requests = []
        if phase < count:
            out, step = divmod(phase, steps)
            x = factors[out] if step == 0 else held[out]
            requests.append((x, both, plan.tree(step)))
        if phase:
            back, turn = divmod(phase - 1, steps)
            requests.append((mirror[back], both, reverse(plan.tree(steps - 1 - turn))))
        brought = plane.issue(*requests, after=after)
        if chunks:
            brought = line_phase(beside=brought)
            plane.last = tuple(brought)
        after = ()
        if phase % steps == 0 and phase < count:
            high, low, *parts = gather(out) if out == 0 else tiles[out]
            tiles[out] = (high, low)
            mirror[out] = lane_sum(parts)
        if phase % steps == 1 % steps and phase < count and out + 1 < members:
            tiles[out + 1] = gather(out + 1)
            after = (tiles[out + 1][0],)
        if phase < count:
            got = brought[0]
            held[out] = jnp.where(plan.on_diagonal(), x, got) if step == 0 else x + got
        if phase:
            if turn < steps - 1:
                mirror[back] = mirror[back] + brought[-1]
            else:
                sums, cross = forward(*tiles[back], factors[back], mirror[back], held[back])
                new = [
                    part + brought[-1][i * share:(i + 1) * share] for i, part in enumerate(sums)
                ]
                chunks += new
                after = tuple(new)
                crosses.append(cross)

    x = jnp.concatenate([lane_sum(cross) for cross in crosses])
    for step in range(steps):
        x = x.reshape(2, x.shape[0] // 2, x.shape[1])
        bit = plan.bit(step)
        send = lax.dynamic_index_in_dim(x, 1 - bit, 0, keepdims=False)
        keep = lax.dynamic_index_in_dim(x, bit, 0, keepdims=False)
        got, = plane.issue((send, both, plan.bit_pairs(step)))
        x = keep + got
    chunks.append(x)

    def place(member, column):
        sums = []
        for i in range(member * SPLIT, (member + 1) * SPLIT):
            sums += [chunks[i], ends[i]]
        return pl.pallas_call(
            functools.partial(place_kernel, plan, member),
            in_specs=smem(1) + vmem(1 + 2 * SPLIT)
            + [pl.BlockSpec(memory_space=pl.ANY)] * (member > 0),
            out_specs=pl.BlockSpec(memory_space=pl.ANY),
            out_shape=jax.ShapeDtypeStruct((inverse_front.shape[0], factor.shape[1]), F32),
            scratch_shapes=[
                pltpu.VMEM((depth, width), F32),
                pltpu.VMEM((plan.tile, width), F32),
                pltpu.SemaphoreType.DMA((plan.na,)),
                pltpu.SemaphoreType.DMA((members, plan.row_tiles)),
            ],
            input_output_aliases={2 + 2 * SPLIT: 0} if member else {},
            compiler_params=PARAMS,
            cost_estimate=pl.CostEstimate(
                flops=6 * depth * width * width, bytes_accessed=8 << 20, transcendentals=0
            ),
            name="place",
        )(tile_list, unit_lower, *sums, *([column] if member else []))

    column, placed, after = None, 0, ()
    while phase_now[0] < len(chunks) + len(hops) - 1:
        line_phase(after)
        after = ()
        if phase_now[0] > (placed + 1) * SPLIT + len(hops) - 1 and placed < members - 1:
            column = place(placed, column)
            placed += 1
            after = (column,)
    for member in range(placed, members):
        column = place(member, column)

    x = jnp.where(plan.at_end(), ends[-1], chunks[-1])
    for step in reversed(range(steps)):
        got, = plane.issue(
            (x, both, plan.bit_pairs(step)), after=(column,) if step < steps - 1 else ()
        )
        bit = plan.bit(step) == 1
        x = jnp.concatenate([jnp.where(bit, got, x), jnp.where(bit, x, got)])
    parts = [x] + [plan.swap(x, shift) for shift in range(1, lanes)]
    diagonal = pl.pallas_call(
        functools.partial(diagonal_kernel, plan),
        in_specs=vmem(2 + lanes),
        out_specs=vmem(1)[0],
        out_shape=jax.ShapeDtypeStruct(unit_lower.shape, F32),
        compiler_params=PARAMS,
        cost_estimate=pl.CostEstimate(
            flops=24 * width * width * width, bytes_accessed=8 << 20, transcendentals=0
        ),
        name="diagonal",
    )(pivot_inverse, unit_lower, *parts)
    return (column, diagonal)


def solution(mesh):
    in_specs = (P("row", "col"), P("row", None), P(), P(), P(), P())
    out_specs = (P("row", None), P())
    return jax.shard_map(shards, mesh=mesh, in_specs=in_specs, out_specs=out_specs, check_vma=False)
```

```python
import functools

import jax
import jax.numpy as jnp
from jax import lax
from jax.experimental import pallas as pl
from jax.experimental.pallas import tpu as pltpu
from jax.sharding import PartitionSpec as P

F32 = jnp.float32
BF16 = jnp.bfloat16
VMEM = pltpu.MemorySpace.VMEM
SMEM = pltpu.MemorySpace.SMEM
SPLIT = 2
PARAMS = pltpu.CompilerParams(vmem_limit_bytes=48 * 1024 * 1024)


def vmem(count):
    return [pl.BlockSpec(memory_space=VMEM)] * count


def smem(count):
    return [pl.BlockSpec(memory_space=SMEM)] * count


def split(x):
    high = x.astype(BF16)
    return high, (x - high.astype(F32)).astype(BF16)


def product(left, right, contract=1):
    def one(a, b):
        return lax.dot_general(a, b, (((contract,), (0,)), ((), ())), preferred_element_type=F32)

    return one(left[0], right[1]) + one(left[1], right[0]) + one(left[0], right[0])


def unit_inverse(ref, member):
    lower = ref[member]
    row = lax.broadcasted_iota(jnp.int32, lower.shape, 0)
    col = lax.broadcasted_iota(jnp.int32, lower.shape, 1)
    return jnp.where(row > col, lower, jnp.where(row == col, 1.0, 0.0).astype(F32))


class Plan:
    def __init__(self, front, factor, unit_lower, tile_list):
        self.rows, self.cols = lax.axis_size("row"), lax.axis_size("col")
        self.lanes = self.rows // self.cols
        self.members, self.width, _ = unit_lower.shape
        self.na = tile_list.shape[1] // self.rows
        self.tile = factor.shape[0] // self.na
        self.nb = self.na * self.lanes
        self.row_tiles = front.shape[0] // self.tile
        self.col_tiles = front.shape[1] // self.tile
        self.depth = factor.shape[0]
        bits = [1 << i for i in range((self.cols - 1).bit_length())]
        self.orders = [
            bits[lane % len(bits):] + bits[:lane % len(bits)] for lane in range(self.lanes)
        ]
        self.steps = len(bits)

    def device(self, chip, lane, col):
        return (chip * self.lanes + lane) * self.cols + col

    def tree(self, step):
        pairs = []
        for col in range(self.cols):
            for lane, order in enumerate(self.orders):
                held, later = [0], [0]
                for bit in order[:step]:
                    held = held + [x ^ bit for x in held]
                for bit in order[step + 1:]:
                    later = later + [x ^ bit for x in later]
                for offset in held:
                    child = col ^ offset ^ order[step]
                    if any(child ^ x > col for x in later):
                        pairs.append(
                            (self.device(col ^ offset, lane, col), self.device(child, lane, col))
                        )
        return pairs

    def swap(self, x, shift):
        pairs = []
        for row in range(self.rows):
            chip, lane = divmod(row, self.lanes)
            pairs.append((chip * self.lanes + (lane + shift) % self.lanes, row))
        return lax.ppermute(x, "row", pairs)

    def line_hops(self):
        count, half = self.cols, self.cols // 2
        inward = [[(i, i + 1), (count - 1 - i, count - 2 - i)] for i in range(half - 1)]
        outward = [
            [(half - 1 - i, half - 2 - i), (half + i, half + i + 1)] for i in range(half - 1)
        ]
        return inward + [[(half - 1, half), (half, half - 1)]] + outward

    def line_step(self, hop, x, got):
        half = self.cols // 2
        if hop < half:
            return x + got
        place, i = lax.axis_index("col"), hop - half
        return jnp.where((place == half - 2 - i) | (place == half + i + 1), got, x)

    def on_diagonal(self):
        return lax.axis_index("row") // self.lanes == lax.axis_index("col")

    def at_end(self):
        place = lax.axis_index("col")
        return (place == 0) | (place == self.cols - 1)

    def bit_pairs(self, step):
        return [
            (self.device(chip, lane, col), self.device(chip ^ order[step], lane, col))
            for chip in range(self.cols)
            for lane, order in enumerate(self.orders)
            for col in range(self.cols)
        ]

    def offset_pairs(self, offset):
        pairs = []
        for lane, order in enumerate(self.orders):
            flip = sum(
                bit for step, bit in enumerate(order) if offset >> (self.steps - 1 - step) & 1
            )
            for chip in range(self.cols):
                for col in range(self.cols):
                    pairs.append(
                        (self.device(chip, lane, col), self.device(chip ^ flip, lane, col))
                    )
        return pairs

    def place_of(self, lane):
        chip, place = lax.axis_index("row") // self.lanes, jnp.int32(0)
        for step, bit in enumerate(self.orders[lane]):
            place = jnp.where((chip & bit) != 0, place + (1 << (self.steps - 1 - step)), place)
        return place

    def bit(self, step):
        row = lax.axis_index("row")
        chip, value = row // self.lanes, jnp.int32(0)
        for lane, order in enumerate(self.orders):
            value = jnp.where((row % self.lanes == lane) & ((chip & order[step]) != 0), 1, value)
        return value


class Chain:
    def __init__(self):
        self.last = ()

    def issue(self, *requests, after=()):
        out = []
        for x, axis, pairs in requests:
            if self.last or after:
                x, _ = lax.optimization_barrier((x, self.last + tuple(after)))
            out.append(lax.ppermute(x, axis, pairs))
        self.last = tuple(out)
        return out


def gather_kernel(plan, member, tiles_ref, valid_ref, front, factor, high, low, *rest):
    mirror, (buffer, sems) = rest[:plan.lanes], rest[plan.lanes:]
    size, na, nb = plan.tile, plan.na, plan.nb
    row, col = lax.axis_index("row"), lax.axis_index("col")
    lane = lax.rem(row, plan.lanes)
    row_slots = [row * na + a for a in range(na)]
    col_slots = [
        col * nb + lax.rem(lane + b // na, plan.lanes) * na + b % na for b in range(nb)
    ]
    copies = []
    for a in range(na):
        for b in range(nb):
            i = jnp.clip(tiles_ref[member, row_slots[a]] - row * plan.row_tiles, 0, plan.row_tiles - 1)
            j = jnp.clip(tiles_ref[member, col_slots[b]] - col * plan.col_tiles, 0, plan.col_tiles - 1)
            copy = pltpu.make_async_copy(
                front.at[
                    pl.ds(pl.multiple_of(i * size, size), size),
                    pl.ds(pl.multiple_of(j * size, size), size),
                ],
                buffer.at[a, b],
                sems.at[a, b],
            )
            copy.start()
            copies.append(copy)
    right = split(factor[...])
    local_row = lax.broadcasted_iota(jnp.int32, (size, size), 0)
    local_col = lax.broadcasted_iota(jnp.int32, (size, size), 1)
    for a in range(na):
        for b in range(nb):
            copies[a * nb + b].wait()
            live = (valid_ref[member, row_slots[a]] > 0) & (valid_ref[member, col_slots[b]] > 0)
            ahead = (tiles_ref[member, row_slots[a]] - tiles_ref[member, col_slots[b]]) * size
            gap = local_row - local_col + ahead
            x = buffer[a, b]
            x = jnp.where(gap > 0, x, jnp.where(gap == 0, 0.5 * x, 0.0))
            x = jnp.where(live, x, 0.0)
            x_high, x_low = split(x)
            high[a * size:(a + 1) * size, b * size:(b + 1) * size] = x_high
            low[a * size:(a + 1) * size, b * size:(b + 1) * size] = x_low
    for b in range(nb):
        left = (high[:, b * size:(b + 1) * size], low[:, b * size:(b + 1) * size])
        first = b % na * size
        mirror[b // na][first:first + size, :] = product(left, right, contract=0)


def forward_kernel(plan, member, high, low, factor, mirror, *rest):
    lanes, size, depth = plan.lanes, plan.tile, plan.depth
    parts, rest = rest[:lanes], rest[lanes:]
    earlier, rest = rest[:lanes * bool(member)], rest[lanes * bool(member):]
    totals, rest = rest[:SPLIT], rest[SPLIT:]
    cross, (total, whole) = rest[:lanes], rest[lanes:]
    right = [split(part[...]) for part in parts]
    for a in range(plan.na):
        rows = slice(a * size, (a + 1) * size)
        total[rows, :] = sum(
            product(
                (high[rows, i * depth:(i + 1) * depth], low[rows, i * depth:(i + 1) * depth]),
                right[i],
            )
            for i in range(lanes)
        )
    share = depth // SPLIT
    on_diagonal = plan.on_diagonal()
    for i in range(SPLIT):
        rows = slice(i * share, (i + 1) * share)
        totals[i][...] = total[rows, :] + jnp.where(on_diagonal, mirror[rows, :], 0.0)
    whole[...] = product(split(factor[...]), split(total[...]), contract=0)
    share = plan.width // lanes
    lane = lax.rem(lax.axis_index("row"), lanes)
    for i in range(lanes):
        first = pl.multiple_of(lax.rem(lane + i, lanes) * share, share)
        cross[i][member * share:, :] = whole[pl.ds(first, share), :]
        if member:
            cross[i][:member * share, :] = earlier[i][...]


def place_kernel(plan, member, tiles_ref, unit_ref, *rest):
    sums, rest = rest[:2 * SPLIT], rest[2 * SPLIT:]
    out, stack, zeros, sems, zero_sems = rest[member > 0:]
    size, width = plan.tile, plan.width
    row, at_end = lax.axis_index("row"), plan.at_end()

    def zero_copies(act):
        for other in range(plan.members):
            for t in range(plan.row_tiles):
                taken = False
                for a in range(plan.na):
                    taken = taken | (
                        tiles_ref[other, row * plan.na + a] == row * plan.row_tiles + t
                    )
                copy = pltpu.make_async_copy(
                    zeros,
                    out.at[t * size:(t + 1) * size, other * width:(other + 1) * width],
                    zero_sems.at[other, t],
                )
                pl.when(jnp.logical_not(taken))(functools.partial(act, copy))

    if member == 0:
        zeros[...] = jnp.zeros_like(zeros)
        zero_copies(lambda copy: copy.start())
    right = split(unit_inverse(unit_ref, member))
    share = plan.depth // SPLIT
    for i in range(SPLIT):
        x = jnp.where(at_end, sums[2 * i + 1][...], sums[2 * i][...])
        stack[i * share:(i + 1) * share, :] = -product(split(x), right)
    copies = []
    for a in range(plan.na):
        t = jnp.clip(
            tiles_ref[member, row * plan.na + a] - row * plan.row_tiles, 0, plan.row_tiles - 1
        )
        copy = pltpu.make_async_copy(
            stack.at[a * size:(a + 1) * size, :],
            out.at[
                pl.ds(pl.multiple_of(t * size, size), size), member * width:(member + 1) * width
            ],
            sems.at[a],
        )
        copy.start()
        copies.append(copy)
    for copy in copies:
        copy.wait()
    if member == 0:
        zero_copies(lambda copy: copy.wait())


def diagonal_kernel(plan, pivot, unit_ref, *rest):
    parts, (out, cross) = rest[:plan.lanes], rest[plan.lanes:]
    width, lanes, members = plan.width, plan.lanes, plan.members
    lane = lax.rem(lax.axis_index("row"), lanes)
    count = 1 << plan.steps
    size = members * width // (lanes * count)
    for other in range(lanes):
        mine = plan.place_of(other)
        for place in range(count):
            first = pl.multiple_of((mine ^ place) * size, size)
            piece = parts[0][pl.ds(first, size), :]
            for i in range(1, lanes):
                piece = jnp.where(
                    lax.rem(lane + i, lanes) == other, parts[i][pl.ds(first, size), :], piece
                )
            cross[other, place * size:(place + 1) * size, :] = piece
    share = width // lanes
    row = lax.broadcasted_iota(jnp.int32, (width, width), 0)
    col = lax.broadcasted_iota(jnp.int32, (width, width), 1)
    for member in range(members):
        rows = slice(member * share, (member + 1) * share)
        x = jnp.concatenate([cross[other, rows, :] for other in range(lanes)])
        x = jnp.where(row == col, pivot[member:member + 1, :], 0.0) + x + x.T
        inverse = split(unit_inverse(unit_ref, member))
        half = product(split(x), inverse)
        out[member] = product(inverse, split(half), contract=0)


def reverse(pairs):
    return [(receiver, sender) for sender, receiver in pairs]


def shards(inverse_front, factor, unit_lower, pivot_inverse, tile_list, tile_valid):
    plan = Plan(inverse_front, factor, unit_lower, tile_list)
    width, depth, lanes, members, steps = plan.width, plan.depth, plan.lanes, plan.members, plan.steps
    both = ("row", "col")
    share = depth // SPLIT
    flops = 6 * depth * depth * lanes * width
    factors = [factor[:, member * width:(member + 1) * width] for member in range(members)]

    def lane_sum(parts):
        out = parts[0]
        for shift in range(1, lanes):
            out = out + plan.swap(parts[lanes - shift], shift)
        return out

    def gather(member):
        return pl.pallas_call(
            functools.partial(gather_kernel, plan, member),
            in_specs=smem(2) + [pl.BlockSpec(memory_space=pl.ANY)] + vmem(1),
            out_specs=vmem(2 + lanes),
            out_shape=[jax.ShapeDtypeStruct((depth, depth * lanes), BF16)] * 2
            + [jax.ShapeDtypeStruct((depth, width), F32)] * lanes,
            scratch_shapes=[
                pltpu.VMEM((plan.na, plan.nb, plan.tile, plan.tile), F32),
                pltpu.SemaphoreType.DMA((plan.na, plan.nb)),
            ],
            compiler_params=PARAMS,
            cost_estimate=pl.CostEstimate(flops=flops, bytes_accessed=8 << 20, transcendentals=0),
            name="gather_mirror",
        )(tile_list, tile_valid, inverse_front, factors[member])

    def forward(member, high, low, mirror, held, earlier):
        parts = [held] + [plan.swap(held, shift) for shift in range(1, lanes)]
        outs = pl.pallas_call(
            functools.partial(forward_kernel, plan, member),
            in_specs=vmem(4 + lanes + len(earlier)),
            out_specs=vmem(SPLIT + lanes),
            out_shape=[jax.ShapeDtypeStruct((share, width), F32)] * SPLIT
            + [jax.ShapeDtypeStruct(((member + 1) * width // lanes, width), F32)] * lanes,
            scratch_shapes=[
                pltpu.VMEM((depth, width), F32),
                pltpu.VMEM((width, width), F32),
            ],
            compiler_params=PARAMS,
            cost_estimate=pl.CostEstimate(flops=flops, bytes_accessed=8 << 20, transcendentals=0),
            name="forward",
        )(high, low, factors[member], mirror, *parts, *earlier)
        return outs[:SPLIT], outs[SPLIT:], parts[-1]

    hops = plan.line_hops()

    def enter(x, after=()):
        if after:
            x, _ = lax.optimization_barrier((x, tuple(after)))
        return lax.ppermute(x, "col", hops[0])

    def run(x, got, before_last=()):
        for hop in range(1, len(hops)):
            x = plan.line_step(hop - 1, x, got)
            sent = x
            if hop == len(hops) - 1 and before_last:
                sent, _ = lax.optimization_barrier((x, tuple(before_last)))
            got = lax.ppermute(sent, "col", hops[hop])
        if len(hops) == 1:
            got = x = x + got
        return x, got

    spread, collect = Chain(), Chain()
    count = members * steps
    tiles, held, mirror, chunks, entered = {}, {}, {}, [], {}
    after, cross, last_swap = (), [], None
    for phase in range(count + 1):
        if phase < count:
            out, step = divmod(phase, steps)
            x = factors[out] if step == 0 else held[out]
            got_out, = spread.issue((x, both, plan.tree(step)), after=after)
        if phase:
            back, turn = divmod(phase - 1, steps)
            got_back, = collect.issue(
                (mirror[back], both, reverse(plan.tree(steps - 1 - turn))), after=after
            )
        if chunks and 0 not in entered:
            entered[0] = enter(chunks[0])
            entered[0], got_out, got_back = lax.optimization_barrier(
                (entered[0], got_out, got_back)
            )
        after = ()
        if phase % steps == 0 and phase < count:
            high, low, *parts = gather(out) if out == 0 else tiles[out]
            tiles[out] = (high, low)
            mirror[out] = lane_sum(parts)
        if phase % steps == 1 % steps and phase < count and out + 1 < members:
            tiles[out + 1] = gather(out + 1)
            after = (tiles[out + 1][0],)
        if phase < count:
            held[out] = jnp.where(plan.on_diagonal(), x, got_out) if step == 0 else x + got_out
        if phase:
            if turn < steps - 1:
                mirror[back] = mirror[back] + got_back
            else:
                sums, cross, last_swap = forward(
                    back, *tiles[back], mirror[back], held[back], cross
                )
                chunks += [
                    part + got_back[i * share:(i + 1) * share] for i, part in enumerate(sums)
                ]
                after = tuple(chunks[-SPLIT:])

    x, _ = lax.optimization_barrier((lane_sum(cross), tuple(chunks[-SPLIT:])))
    for step in range(steps):
        x = x.reshape(2, x.shape[0] // 2, x.shape[1])
        bit = plan.bit(step)
        send = lax.dynamic_index_in_dim(x, 1 - bit, 0, keepdims=False)
        keep = lax.dynamic_index_in_dim(x, bit, 0, keepdims=False)
        x = keep + lax.ppermute(send, both, plan.bit_pairs(step))
    update = x

    def place(member, column):
        sums = []
        for i in range(member * SPLIT, (member + 1) * SPLIT):
            sums += [chunks[i], ends[i]]
        return pl.pallas_call(
            functools.partial(place_kernel, plan, member),
            in_specs=smem(1) + vmem(1 + 2 * SPLIT)
            + [pl.BlockSpec(memory_space=pl.ANY)] * (member > 0),
            out_specs=pl.BlockSpec(memory_space=pl.ANY),
            out_shape=jax.ShapeDtypeStruct((inverse_front.shape[0], factor.shape[1]), F32),
            scratch_shapes=[
                pltpu.VMEM((depth, width), F32),
                pltpu.VMEM((plan.tile, width), F32),
                pltpu.SemaphoreType.DMA((plan.na,)),
                pltpu.SemaphoreType.DMA((members, plan.row_tiles)),
            ],
            input_output_aliases={2 + 2 * SPLIT: 0} if member else {},
            compiler_params=PARAMS,
            cost_estimate=pl.CostEstimate(
                flops=6 * depth * width * width, bytes_accessed=8 << 20, transcendentals=0
            ),
            name="place",
        )(tile_list, unit_lower, *sums, *([column] if member else []))

    ends, column = {}, None
    for i in range(len(chunks)):
        if i + 1 < len(chunks):
            if i + 1 < SPLIT:
                wait = (last_swap, entered[i])
            elif (i + 1) % SPLIT and i >= SPLIT:
                wait = (ends[i - SPLIT],)
            else:
                wait = ()
            entered[i + 1] = enter(chunks[i + 1], wait)
            wait = (entered[i + 1],)
        else:
            wait = () if column is None else (column,)
        chunks[i], ends[i] = run(chunks[i], entered[i], wait)
        if i % SPLIT == SPLIT - 1:
            column = place(i // SPLIT, column)

    x, got = run(update, enter(update))
    x = jnp.where(plan.at_end(), got, x)
    pieces = [x] + [lax.ppermute(x, both, plan.offset_pairs(r)) for r in range(1, 1 << steps)]
    x, _ = lax.optimization_barrier((jnp.concatenate(pieces), column))
    parts = [x] + [plan.swap(x, shift) for shift in range(1, lanes)]
    diagonal = pl.pallas_call(
        functools.partial(diagonal_kernel, plan),
        in_specs=vmem(2 + lanes),
        out_specs=vmem(1)[0],
        out_shape=jax.ShapeDtypeStruct(unit_lower.shape, F32),
        scratch_shapes=[pltpu.VMEM((lanes, members * width // lanes, width), F32)],
        compiler_params=PARAMS,
        cost_estimate=pl.CostEstimate(
            flops=24 * width * width * width, bytes_accessed=8 << 20, transcendentals=0
        ),
        name="diagonal",
    )(pivot_inverse, unit_lower, *parts)
    return (column, diagonal)


def solution(mesh):
    in_specs = (P("row", "col"), P("row", None), P(), P(), P(), P())
    out_specs = (P("row", None), P())
    return jax.shard_map(shards, mesh=mesh, in_specs=in_specs, out_specs=out_specs, check_vma=False)
```

```python
import functools

import jax
import jax.numpy as jnp
from jax import lax
from jax.experimental import pallas as pl
from jax.experimental.pallas import tpu as pltpu
from jax.sharding import PartitionSpec as P

F32 = jnp.float32
BF16 = jnp.bfloat16
VMEM = pltpu.MemorySpace.VMEM
SMEM = pltpu.MemorySpace.SMEM
SMALL = pl.CostEstimate(flops=1 << 20, bytes_accessed=1 << 16, transcendentals=0)
PARAMS = pltpu.CompilerParams(vmem_limit_bytes=48 * 1024 * 1024)


def vmem(count):
    return [pl.BlockSpec(memory_space=VMEM)] * count


def smem(count):
    return [pl.BlockSpec(memory_space=SMEM)] * count


def split(x):
    high = x.astype(BF16)
    return high, (x - high.astype(F32)).astype(BF16)


def product(left, right, contract=1):
    def one(a, b):
        return lax.dot_general(a, b, (((contract,), (0,)), ((), ())), preferred_element_type=F32)

    return one(left[0], right[1]) + one(left[1], right[0]) + one(left[0], right[0])


def unit_inverse(ref, member):
    lower = ref[member]
    row = lax.broadcasted_iota(jnp.int32, lower.shape, 0)
    col = lax.broadcasted_iota(jnp.int32, lower.shape, 1)
    return jnp.where(row > col, lower, jnp.where(row == col, 1.0, 0.0).astype(F32))


class Plan:
    def __init__(self, front, factor, unit_lower, tile_list):
        self.rows, self.cols = lax.axis_size("row"), lax.axis_size("col")
        self.lanes = self.rows // self.cols
        self.members, self.width, _ = unit_lower.shape
        self.na = tile_list.shape[1] // self.rows
        self.tile = factor.shape[0] // self.na
        self.nb = self.na * self.lanes
        self.row_tiles = front.shape[0] // self.tile
        self.col_tiles = front.shape[1] // self.tile
        self.depth = factor.shape[0]
        bits = [1 << i for i in range((self.cols - 1).bit_length())]
        self.orders = [
            bits[lane % len(bits):] + bits[:lane % len(bits)] for lane in range(self.lanes)
        ]
        self.steps = len(bits)
        self.splits = [1] + [2] * (self.members - 1)

    def device(self, chip, lane, col):
        return (chip * self.lanes + lane) * self.cols + col

    def tree(self, step):
        pairs = []
        for col in range(self.cols):
            for lane, order in enumerate(self.orders):
                held, later = [0], [0]
                for bit in order[:step]:
                    held = held + [x ^ bit for x in held]
                for bit in order[step + 1:]:
                    later = later + [x ^ bit for x in later]
                for offset in held:
                    child = col ^ offset ^ order[step]
                    if any(child ^ x > col for x in later):
                        pairs.append(
                            (self.device(col ^ offset, lane, col), self.device(child, lane, col))
                        )
        return pairs

    def swap(self, x, shift):
        pairs = []
        for row in range(self.rows):
            chip, lane = divmod(row, self.lanes)
            pairs.append((chip * self.lanes + (lane + shift) % self.lanes, row))
        return lax.ppermute(x, "row", pairs)

    def line_hops(self):
        count, half = self.cols, self.cols // 2
        inward = [[(i, i + 1), (count - 1 - i, count - 2 - i)] for i in range(half - 1)]
        outward = [
            [(half - 1 - i, half - 2 - i), (half + i, half + i + 1)] for i in range(half - 1)
        ]
        return inward + [[(half - 1, half), (half, half - 1)]] + outward

    def line_step(self, hop, x, got):
        half = self.cols // 2
        if hop < half:
            return x + got
        place, i = lax.axis_index("col"), hop - half
        return jnp.where((place == half - 2 - i) | (place == half + i + 1), got, x)

    def on_diagonal(self):
        return lax.axis_index("row") // self.lanes == lax.axis_index("col")

    def at_end(self):
        place = lax.axis_index("col")
        return (place == 0) | (place == self.cols - 1)

    def bit_pairs(self, step):
        return [
            (self.device(chip, lane, col), self.device(chip ^ order[step], lane, col))
            for chip in range(self.cols)
            for lane, order in enumerate(self.orders)
            for col in range(self.cols)
        ]

    def offset_pairs(self, offset):
        pairs = []
        for lane, order in enumerate(self.orders):
            flip = sum(
                bit for step, bit in enumerate(order) if offset >> (self.steps - 1 - step) & 1
            )
            for chip in range(self.cols):
                for col in range(self.cols):
                    pairs.append(
                        (self.device(chip, lane, col), self.device(chip ^ flip, lane, col))
                    )
        return pairs

    def place_of(self, lane):
        chip, place = lax.axis_index("row") // self.lanes, jnp.int32(0)
        for step, bit in enumerate(self.orders[lane]):
            place = jnp.where((chip & bit) != 0, place + (1 << (self.steps - 1 - step)), place)
        return place

    def bit(self, step):
        row = lax.axis_index("row")
        chip, value = row // self.lanes, jnp.int32(0)
        for lane, order in enumerate(self.orders):
            value = jnp.where((row % self.lanes == lane) & ((chip & order[step]) != 0), 1, value)
        return value


class Chain:
    def __init__(self):
        self.last = ()

    def issue(self, *requests, after=()):
        out = []
        for x, axis, pairs in requests:
            if self.last or after:
                x, _ = lax.optimization_barrier((x, self.last + tuple(after)))
            out.append(lax.ppermute(x, axis, pairs))
        self.last = tuple(out)
        return out


def gather_kernel(plan, member, tiles_ref, valid_ref, front, factor, high, low, *rest):
    mirror, (buffer, sems) = rest[:plan.lanes], rest[plan.lanes:]
    size, na, nb = plan.tile, plan.na, plan.nb
    row, col = lax.axis_index("row"), lax.axis_index("col")
    lane = lax.rem(row, plan.lanes)
    row_slots = [row * na + a for a in range(na)]
    col_slots = [
        col * nb + lax.rem(lane + b // na, plan.lanes) * na + b % na for b in range(nb)
    ]
    copies = []
    for a in range(na):
        for b in range(nb):
            i = jnp.clip(tiles_ref[member, row_slots[a]] - row * plan.row_tiles, 0, plan.row_tiles - 1)
            j = jnp.clip(tiles_ref[member, col_slots[b]] - col * plan.col_tiles, 0, plan.col_tiles - 1)
            copy = pltpu.make_async_copy(
                front.at[
                    pl.ds(pl.multiple_of(i * size, size), size),
                    pl.ds(pl.multiple_of(j * size, size), size),
                ],
                buffer.at[a, b],
                sems.at[a, b],
            )
            copy.start()
            copies.append(copy)
    right = split(factor[...])
    local_row = lax.broadcasted_iota(jnp.int32, (size, size), 0)
    local_col = lax.broadcasted_iota(jnp.int32, (size, size), 1)
    for a in range(na):
        for b in range(nb):
            copies[a * nb + b].wait()
            live = (valid_ref[member, row_slots[a]] > 0) & (valid_ref[member, col_slots[b]] > 0)
            ahead = (tiles_ref[member, row_slots[a]] - tiles_ref[member, col_slots[b]]) * size
            gap = local_row - local_col + ahead
            x = buffer[a, b]
            x = jnp.where(gap > 0, x, jnp.where(gap == 0, 0.5 * x, 0.0))
            x = jnp.where(live, x, 0.0)
            x_high, x_low = split(x)
            high[a * size:(a + 1) * size, b * size:(b + 1) * size] = x_high
            low[a * size:(a + 1) * size, b * size:(b + 1) * size] = x_low
    for b in range(nb):
        left = (high[:, b * size:(b + 1) * size], low[:, b * size:(b + 1) * size])
        first = b % na * size
        mirror[b // na][first:first + size, :] = product(left, right, contract=0)


def forward_kernel(plan, member, high, low, factor, mirror, *rest):
    lanes, size, depth = plan.lanes, plan.tile, plan.depth
    parts, rest = rest[:lanes], rest[lanes:]
    earlier, rest = rest[:lanes * bool(member)], rest[lanes * bool(member):]
    splits = plan.splits[member]
    totals, rest = rest[:splits], rest[splits:]
    cross, (total, whole) = rest[:lanes], rest[lanes:]
    right = [split(part[...]) for part in parts]
    for a in range(plan.na):
        rows = slice(a * size, (a + 1) * size)
        total[rows, :] = sum(
            product(
                (high[rows, i * depth:(i + 1) * depth], low[rows, i * depth:(i + 1) * depth]),
                right[i],
            )
            for i in range(lanes)
        )
    share = depth // splits
    on_diagonal = plan.on_diagonal()
    for i in range(splits):
        rows = slice(i * share, (i + 1) * share)
        totals[i][...] = total[rows, :] + jnp.where(on_diagonal, mirror[rows, :], 0.0)
    whole[...] = product(split(factor[...]), split(total[...]), contract=0)
    share = plan.width // lanes
    lane = lax.rem(lax.axis_index("row"), lanes)
    for i in range(lanes):
        first = pl.multiple_of(lax.rem(lane + i, lanes) * share, share)
        cross[i][member * share:, :] = whole[pl.ds(first, share), :]
        if member:
            cross[i][:member * share, :] = earlier[i][...]


def place_kernel(plan, member, tiles_ref, unit_ref, *rest):
    splits = plan.splits[member]
    sums, rest = rest[:2 * splits], rest[2 * splits:]
    out, stack, zeros, sems, zero_sems = rest[member > 0:]
    size, width = plan.tile, plan.width
    row, at_end = lax.axis_index("row"), plan.at_end()

    def zero_copies(act):
        for other in range(plan.members):
            for t in range(plan.row_tiles):
                taken = False
                for a in range(plan.na):
                    taken = taken | (
                        tiles_ref[other, row * plan.na + a] == row * plan.row_tiles + t
                    )
                copy = pltpu.make_async_copy(
                    zeros,
                    out.at[t * size:(t + 1) * size, other * width:(other + 1) * width],
                    zero_sems.at[other, t],
                )
                pl.when(jnp.logical_not(taken))(functools.partial(act, copy))

    if member == 0:
        zeros[...] = jnp.zeros_like(zeros)
        zero_copies(lambda copy: copy.start())
    right = split(unit_inverse(unit_ref, member))
    share = plan.depth // splits
    for i in range(splits):
        x = jnp.where(at_end, sums[2 * i + 1][...], sums[2 * i][...])
        stack[i * share:(i + 1) * share, :] = -product(split(x), right)
    copies = []
    for a in range(plan.na):
        t = jnp.clip(
            tiles_ref[member, row * plan.na + a] - row * plan.row_tiles, 0, plan.row_tiles - 1
        )
        copy = pltpu.make_async_copy(
            stack.at[a * size:(a + 1) * size, :],
            out.at[
                pl.ds(pl.multiple_of(t * size, size), size), member * width:(member + 1) * width
            ],
            sems.at[a],
        )
        copy.start()
        copies.append(copy)
    for copy in copies:
        copy.wait()
    if member == 0:
        zero_copies(lambda copy: copy.wait())


def diagonal_kernel(plan, pivot, unit_ref, *rest):
    parts, (out, cross) = rest[:plan.lanes], rest[plan.lanes:]
    width, lanes, members = plan.width, plan.lanes, plan.members
    lane = lax.rem(lax.axis_index("row"), lanes)
    count = 1 << plan.steps
    size = members * width // (lanes * count)
    for other in range(lanes):
        mine = plan.place_of(other)
        for place in range(count):
            first = pl.multiple_of((mine ^ place) * size, size)
            piece = parts[0][pl.ds(first, size), :]
            for i in range(1, lanes):
                piece = jnp.where(
                    lax.rem(lane + i, lanes) == other, parts[i][pl.ds(first, size), :], piece
                )
            cross[other, place * size:(place + 1) * size, :] = piece
    share = width // lanes
    row = lax.broadcasted_iota(jnp.int32, (width, width), 0)
    col = lax.broadcasted_iota(jnp.int32, (width, width), 1)
    for member in range(members):
        rows = slice(member * share, (member + 1) * share)
        x = jnp.concatenate([cross[other, rows, :] for other in range(lanes)])
        x = jnp.where(row == col, pivot[member:member + 1, :], 0.0) + x + x.T
        inverse = split(unit_inverse(unit_ref, member))
        half = product(split(x), inverse)
        out[member] = product(inverse, split(half), contract=0)


def reverse(pairs):
    return [(receiver, sender) for sender, receiver in pairs]


def shards(inverse_front, factor, unit_lower, pivot_inverse, tile_list, tile_valid):
    plan = Plan(inverse_front, factor, unit_lower, tile_list)
    width, depth, lanes, members, steps = plan.width, plan.depth, plan.lanes, plan.members, plan.steps
    both = ("row", "col")
    factors = [factor[:, member * width:(member + 1) * width] for member in range(members)]

    def lane_sum(parts):
        out = parts[0]
        for shift in range(1, lanes):
            out = out + plan.swap(parts[lanes - shift], shift)
        return out

    def gather(member):
        return pl.pallas_call(
            functools.partial(gather_kernel, plan, member),
            in_specs=smem(2) + [pl.BlockSpec(memory_space=pl.ANY)] + vmem(1),
            out_specs=vmem(2 + lanes),
            out_shape=[jax.ShapeDtypeStruct((depth, depth * lanes), BF16)] * 2
            + [jax.ShapeDtypeStruct((depth, width), F32)] * lanes,
            scratch_shapes=[
                pltpu.VMEM((plan.na, plan.nb, plan.tile, plan.tile), F32),
                pltpu.SemaphoreType.DMA((plan.na, plan.nb)),
            ],
            compiler_params=PARAMS,
            cost_estimate=SMALL,
            name="gather_mirror",
        )(tile_list, tile_valid, inverse_front, factors[member])

    def forward(member, high, low, mirror, held, earlier):
        parts = [held] + [plan.swap(held, shift) for shift in range(1, lanes)]
        splits = plan.splits[member]
        outs = pl.pallas_call(
            functools.partial(forward_kernel, plan, member),
            in_specs=vmem(4 + lanes + len(earlier)),
            out_specs=vmem(splits + lanes),
            out_shape=[jax.ShapeDtypeStruct((depth // splits, width), F32)] * splits
            + [jax.ShapeDtypeStruct(((member + 1) * width // lanes, width), F32)] * lanes,
            scratch_shapes=[
                pltpu.VMEM((depth, width), F32),
                pltpu.VMEM((width, width), F32),
            ],
            compiler_params=PARAMS,
            cost_estimate=SMALL,
            name="forward",
        )(high, low, factors[member], mirror, *parts, *earlier)
        return outs[:splits], outs[splits:]

    hops = plan.line_hops()

    def enter(x, after=()):
        if after:
            x, _ = lax.optimization_barrier((x, tuple(after)))
        return lax.ppermute(x, "col", hops[0])

    def run(x, got, ties=(), second=None):
        sent, brought = [], []
        for hop in range(1, len(hops)):
            x = plan.line_step(hop - 1, x, got)
            sent.append(x)
            tie = ties[hop - 1] if hop <= len(ties) else ()
            y = lax.optimization_barrier((x, tuple(tie)))[0] if tie else x
            if hop == 1 and second is not None:
                got = second
            else:
                got = lax.ppermute(y, "col", hops[hop])
            brought.append(got)
        if len(hops) == 1:
            got = x = x + got
        return x, got, sent, brought

    spread, collect = Chain(), Chain()
    count = members * steps
    tiles, held, mirror, chunks, entered = {}, {}, {}, [], {}
    after, cross, second = (), [], None
    for phase in range(count + 1):
        if phase < count:
            out, step = divmod(phase, steps)
            x = factors[out] if step == 0 else held[out]
            got_out, = spread.issue((x, both, plan.tree(step)), after=after)
        if phase:
            back, turn = divmod(phase - 1, steps)
            got_back, = collect.issue(
                (mirror[back], both, reverse(plan.tree(steps - 1 - turn))), after=after
            )
        if chunks and 0 not in entered:
            entered[0] = enter(chunks[0])
            entered[0], got_out, got_back = lax.optimization_barrier(
                (entered[0], got_out, got_back)
            )
        if phase == count and chunks and len(hops) > 1:
            second = lax.ppermute(plan.line_step(0, chunks[0], entered[0]), "col", hops[1])
            second, got_back = lax.optimization_barrier((second, got_back))
        after = ()
        if phase % steps == 0 and phase < count:
            high, low, *parts = gather(out) if out == 0 else tiles[out]
            tiles[out] = (high, low)
            mirror[out] = lane_sum(parts)
        if phase % steps == 1 % steps and phase < count and out + 1 < members:
            tiles[out + 1] = gather(out + 1)
            after = (tiles[out + 1][0],)
        if phase < count:
            held[out] = jnp.where(plan.on_diagonal(), x, got_out) if step == 0 else x + got_out
        if phase:
            if turn < steps - 1:
                mirror[back] = mirror[back] + got_back
            else:
                x = mirror[back]
                if chunks:
                    x, _ = lax.optimization_barrier(
                        (x, plan.line_step(0, chunks[0], entered[0]))
                    )
                sums, cross = forward(back, *tiles[back], x, held[back], cross)
                share = sums[0].shape[0]
                after = tuple(
                    part + got_back[i * share:(i + 1) * share] for i, part in enumerate(sums)
                )
                chunks += after

    x = lane_sum(cross)
    for step in range(steps):
        x = x.reshape(2, x.shape[0] // 2, x.shape[1])
        bit = plan.bit(step)
        send = lax.dynamic_index_in_dim(x, 1 - bit, 0, keepdims=False)
        keep = lax.dynamic_index_in_dim(x, bit, 0, keepdims=False)
        x = keep + lax.ppermute(send, both, plan.bit_pairs(step))
    update = x

    def place(member, column):
        sums, splits = [], plan.splits[member]
        first = sum(plan.splits[:member])
        for i in range(first, first + splits):
            sums += [chunks[i], ends[i]]
        return pl.pallas_call(
            functools.partial(place_kernel, plan, member),
            in_specs=smem(1) + vmem(1 + 2 * splits)
            + [pl.BlockSpec(memory_space=pl.ANY)] * (member > 0),
            out_specs=pl.BlockSpec(memory_space=pl.ANY),
            out_shape=jax.ShapeDtypeStruct((inverse_front.shape[0], factor.shape[1]), F32),
            scratch_shapes=[
                pltpu.VMEM((depth, width), F32),
                pltpu.VMEM((plan.tile, width), F32),
                pltpu.SemaphoreType.DMA((plan.na,)),
                pltpu.SemaphoreType.DMA((members, plan.row_tiles)),
            ],
            input_output_aliases={2 + 2 * splits: 0} if member else {},
            compiler_params=PARAMS,
            cost_estimate=SMALL,
            name="place",
        )(tile_list, unit_lower, *sums, *([column] if member else []))

    ends, sent, column, last = {}, {}, None, len(chunks) - 1
    middle = len(hops) - 1
    for i in range(1, last + 1):
        entered[i] = enter(chunks[i], (entered[i - 1],) if i > 1 else ())
    for i in range(last + 1):
        ties = [()] * (middle - 1) + [(ends[0],)] if i == 1 and middle else ()
        chunks[i], ends[i], sent[i], _ = run(
            chunks[i], entered[i], ties, second if i == 0 else None
        )
    ties = [tuple(sent[max(last - 1, 0)][-1:]), tuple(sent[last][-1:])][:middle]
    update, got, _, _ = run(update, enter(update), ties)
    for member in range(members):
        column = place(member, column)
        if member == 0:
            got, _ = lax.optimization_barrier((got, column))

    x = update
    x = jnp.where(plan.at_end(), got, x)
    pieces = [x] + [lax.ppermute(x, both, plan.offset_pairs(r)) for r in range(1, 1 << steps)]
    x, _ = lax.optimization_barrier((jnp.concatenate(pieces), column))
    parts = [x] + [plan.swap(x, shift) for shift in range(1, lanes)]
    diagonal = pl.pallas_call(
        functools.partial(diagonal_kernel, plan),
        in_specs=vmem(2 + lanes),
        out_specs=vmem(1)[0],
        out_shape=jax.ShapeDtypeStruct(unit_lower.shape, F32),
        scratch_shapes=[pltpu.VMEM((lanes, members * width // lanes, width), F32)],
        compiler_params=PARAMS,
        cost_estimate=SMALL,
        name="diagonal",
    )(pivot_inverse, unit_lower, *parts)
    return (column, diagonal)


def solution(mesh):
    in_specs = (P("row", "col"), P("row", None), P(), P(), P(), P())
    out_specs = (P("row", None), P())
    return jax.shard_map(shards, mesh=mesh, in_specs=in_specs, out_specs=out_specs, check_vma=False)
```

```python
import functools

import jax
import jax.numpy as jnp
from jax import lax
from jax.experimental import pallas as pl
from jax.experimental.pallas import tpu as pltpu
from jax.sharding import PartitionSpec as P

F32 = jnp.float32
BF16 = jnp.bfloat16
VMEM = pltpu.MemorySpace.VMEM
SMEM = pltpu.MemorySpace.SMEM
COST = pl.CostEstimate(flops=1600 << 20, bytes_accessed=8 << 20, transcendentals=0)
PARAMS = pltpu.CompilerParams(vmem_limit_bytes=48 * 1024 * 1024)


def vmem(count):
    return [pl.BlockSpec(memory_space=VMEM)] * count


def smem(count):
    return [pl.BlockSpec(memory_space=SMEM)] * count


def split(x):
    high = x.astype(BF16)
    return high, (x - high.astype(F32)).astype(BF16)


def product(left, right, contract=1):
    def one(a, b):
        return lax.dot_general(a, b, (((contract,), (0,)), ((), ())), preferred_element_type=F32)

    return one(left[0], right[1]) + one(left[1], right[0]) + one(left[0], right[0])


def unit_inverse(ref, member):
    lower = ref[member]
    row = lax.broadcasted_iota(jnp.int32, lower.shape, 0)
    col = lax.broadcasted_iota(jnp.int32, lower.shape, 1)
    return jnp.where(row > col, lower, jnp.where(row == col, 1.0, 0.0).astype(F32))


class Plan:
    def __init__(self, front, factor, unit_lower, tile_list):
        self.rows, self.cols = lax.axis_size("row"), lax.axis_size("col")
        self.lanes = self.rows // self.cols
        self.members, self.width, _ = unit_lower.shape
        self.na = tile_list.shape[1] // self.rows
        self.tile = factor.shape[0] // self.na
        self.nb = self.na * self.lanes
        self.row_tiles = front.shape[0] // self.tile
        self.col_tiles = front.shape[1] // self.tile
        self.depth = factor.shape[0]
        bits = [1 << i for i in range((self.cols - 1).bit_length())]
        self.orders = [
            bits[lane % len(bits):] + bits[:lane % len(bits)] for lane in range(self.lanes)
        ]
        self.steps = len(bits)
        self.splits = [2] * self.members

    def device(self, chip, lane, col):
        return (chip * self.lanes + lane) * self.cols + col

    def tree(self, step):
        pairs = []
        for col in range(self.cols):
            for lane, order in enumerate(self.orders):
                held, later = [0], [0]
                for bit in order[:step]:
                    held = held + [x ^ bit for x in held]
                for bit in order[step + 1:]:
                    later = later + [x ^ bit for x in later]
                for offset in held:
                    child = col ^ offset ^ order[step]
                    if any(child ^ x > col for x in later):
                        pairs.append(
                            (self.device(col ^ offset, lane, col), self.device(child, lane, col))
                        )
        return pairs

    def swap(self, x, shift):
        pairs = []
        for row in range(self.rows):
            chip, lane = divmod(row, self.lanes)
            pairs.append((chip * self.lanes + (lane + shift) % self.lanes, row))
        return lax.ppermute(x, "row", pairs)

    def line_hops(self):
        count, half = self.cols, self.cols // 2
        inward = [[(i, i + 1), (count - 1 - i, count - 2 - i)] for i in range(half - 1)]
        outward = [
            [(half - 1 - i, half - 2 - i), (half + i, half + i + 1)] for i in range(half - 1)
        ]
        return inward + [[(half - 1, half), (half, half - 1)]] + outward

    def line_step(self, hop, x, got):
        half = self.cols // 2
        if hop < half:
            return x + got
        place, i = lax.axis_index("col"), hop - half
        return jnp.where((place == half - 2 - i) | (place == half + i + 1), got, x)

    def on_diagonal(self):
        return lax.axis_index("row") // self.lanes == lax.axis_index("col")

    def at_end(self):
        place = lax.axis_index("col")
        return (place == 0) | (place == self.cols - 1)

    def bit_pairs(self, step):
        return [
            (self.device(chip, lane, col), self.device(chip ^ order[step], lane, col))
            for chip in range(self.cols)
            for lane, order in enumerate(self.orders)
            for col in range(self.cols)
        ]

    def offset_pairs(self, offset):
        pairs = []
        for lane, order in enumerate(self.orders):
            flip = sum(
                bit for step, bit in enumerate(order) if offset >> (self.steps - 1 - step) & 1
            )
            for chip in range(self.cols):
                for col in range(self.cols):
                    pairs.append(
                        (self.device(chip, lane, col), self.device(chip ^ flip, lane, col))
                    )
        return pairs

    def place_of(self, lane):
        chip, place = lax.axis_index("row") // self.lanes, jnp.int32(0)
        for step, bit in enumerate(self.orders[lane]):
            place = jnp.where((chip & bit) != 0, place + (1 << (self.steps - 1 - step)), place)
        return place

    def bit(self, step):
        row = lax.axis_index("row")
        chip, value = row // self.lanes, jnp.int32(0)
        for lane, order in enumerate(self.orders):
            value = jnp.where((row % self.lanes == lane) & ((chip & order[step]) != 0), 1, value)
        return value


class Chain:
    def __init__(self):
        self.last = ()

    def issue(self, *requests, after=()):
        out = []
        for x, axis, pairs in requests:
            if self.last or after:
                x, _ = lax.optimization_barrier((x, self.last + tuple(after)))
            out.append(lax.ppermute(x, axis, pairs))
        self.last = tuple(out)
        return out


def gather_kernel(plan, member, tiles_ref, valid_ref, front, factor, high, low, *rest):
    mirror, (buffer, sems) = rest[:plan.lanes], rest[plan.lanes:]
    size, na, nb = plan.tile, plan.na, plan.nb
    row, col = lax.axis_index("row"), lax.axis_index("col")
    lane = lax.rem(row, plan.lanes)
    row_slots = [row * na + a for a in range(na)]
    col_slots = [
        col * nb + lax.rem(lane + b // na, plan.lanes) * na + b % na for b in range(nb)
    ]
    copies = []
    for a in range(na):
        for b in range(nb):
            i = jnp.clip(tiles_ref[member, row_slots[a]] - row * plan.row_tiles, 0, plan.row_tiles - 1)
            j = jnp.clip(tiles_ref[member, col_slots[b]] - col * plan.col_tiles, 0, plan.col_tiles - 1)
            copy = pltpu.make_async_copy(
                front.at[
                    pl.ds(pl.multiple_of(i * size, size), size),
                    pl.ds(pl.multiple_of(j * size, size), size),
                ],
                buffer.at[a, b],
                sems.at[a, b],
            )
            copy.start()
            copies.append(copy)
    right = split(factor[...])
    local_row = lax.broadcasted_iota(jnp.int32, (size, size), 0)
    local_col = lax.broadcasted_iota(jnp.int32, (size, size), 1)
    for a in range(na):
        for b in range(nb):
            copies[a * nb + b].wait()
            live = (valid_ref[member, row_slots[a]] > 0) & (valid_ref[member, col_slots[b]] > 0)
            ahead = (tiles_ref[member, row_slots[a]] - tiles_ref[member, col_slots[b]]) * size
            gap = local_row - local_col + ahead
            x = buffer[a, b]
            x = jnp.where(gap > 0, x, jnp.where(gap == 0, 0.5 * x, 0.0))
            x = jnp.where(live, x, 0.0)
            x_high, x_low = split(x)
            high[a * size:(a + 1) * size, b * size:(b + 1) * size] = x_high
            low[a * size:(a + 1) * size, b * size:(b + 1) * size] = x_low
    for b in range(nb):
        left = (high[:, b * size:(b + 1) * size], low[:, b * size:(b + 1) * size])
        first = b % na * size
        mirror[b // na][first:first + size, :] = product(left, right, contract=0)


def forward_kernel(plan, member, high, low, factor, mirror, *rest):
    lanes, size, depth = plan.lanes, plan.tile, plan.depth
    parts, rest = rest[:lanes], rest[lanes:]
    earlier, rest = rest[:lanes * bool(member)], rest[lanes * bool(member):]
    splits = plan.splits[member]
    totals, rest = rest[:splits], rest[splits:]
    cross, (total, whole) = rest[:lanes], rest[lanes:]
    right = [split(part[...]) for part in parts]
    for a in range(plan.na):
        rows = slice(a * size, (a + 1) * size)
        total[rows, :] = sum(
            product(
                (high[rows, i * depth:(i + 1) * depth], low[rows, i * depth:(i + 1) * depth]),
                right[i],
            )
            for i in range(lanes)
        )
    share = depth // splits
    on_diagonal = plan.on_diagonal()
    for i in range(splits):
        rows = slice(i * share, (i + 1) * share)
        totals[i][...] = total[rows, :] + jnp.where(on_diagonal, mirror[rows, :], 0.0)
    whole[...] = product(split(factor[...]), split(total[...]), contract=0)
    share = plan.width // lanes
    lane = lax.rem(lax.axis_index("row"), lanes)
    for i in range(lanes):
        first = pl.multiple_of(lax.rem(lane + i, lanes) * share, share)
        cross[i][member * share:, :] = whole[pl.ds(first, share), :]
        if member:
            cross[i][:member * share, :] = earlier[i][...]


def place_kernel(plan, member, tiles_ref, unit_ref, *rest):
    splits = plan.splits[member]
    sums, rest = rest[:2 * splits], rest[2 * splits:]
    out, stack, zeros, sems, zero_sems = rest[member > 0:]
    size, width = plan.tile, plan.width
    row, at_end = lax.axis_index("row"), plan.at_end()

    def zero_copies(act):
        for other in range(plan.members):
            for t in range(plan.row_tiles):
                taken = False
                for a in range(plan.na):
                    taken = taken | (
                        tiles_ref[other, row * plan.na + a] == row * plan.row_tiles + t
                    )
                copy = pltpu.make_async_copy(
                    zeros,
                    out.at[t * size:(t + 1) * size, other * width:(other + 1) * width],
                    zero_sems.at[other, t],
                )
                pl.when(jnp.logical_not(taken))(functools.partial(act, copy))

    if member == 0:
        zeros[...] = jnp.zeros_like(zeros)
        zero_copies(lambda copy: copy.start())
    right = split(unit_inverse(unit_ref, member))
    share = plan.depth // splits
    for i in range(splits):
        x = jnp.where(at_end, sums[2 * i + 1][...], sums[2 * i][...])
        stack[i * share:(i + 1) * share, :] = -product(split(x), right)
    copies = []
    for a in range(plan.na):
        t = jnp.clip(
            tiles_ref[member, row * plan.na + a] - row * plan.row_tiles, 0, plan.row_tiles - 1
        )
        copy = pltpu.make_async_copy(
            stack.at[a * size:(a + 1) * size, :],
            out.at[
                pl.ds(pl.multiple_of(t * size, size), size), member * width:(member + 1) * width
            ],
            sems.at[a],
        )
        copy.start()
        copies.append(copy)
    for copy in copies:
        copy.wait()
    if member == 0:
        zero_copies(lambda copy: copy.wait())


def diagonal_kernel(plan, pivot, unit_ref, *rest):
    parts, (out, cross) = rest[:plan.lanes], rest[plan.lanes:]
    width, lanes, members = plan.width, plan.lanes, plan.members
    lane = lax.rem(lax.axis_index("row"), lanes)
    count = 1 << plan.steps
    size = members * width // (lanes * count)
    for other in range(lanes):
        mine = plan.place_of(other)
        for place in range(count):
            first = pl.multiple_of((mine ^ place) * size, size)
            piece = parts[0][pl.ds(first, size), :]
            for i in range(1, lanes):
                piece = jnp.where(
                    lax.rem(lane + i, lanes) == other, parts[i][pl.ds(first, size), :], piece
                )
            cross[other, place * size:(place + 1) * size, :] = piece
    share = width // lanes
    row = lax.broadcasted_iota(jnp.int32, (width, width), 0)
    col = lax.broadcasted_iota(jnp.int32, (width, width), 1)
    for member in range(members):
        rows = slice(member * share, (member + 1) * share)
        x = jnp.concatenate([cross[other, rows, :] for other in range(lanes)])
        x = jnp.where(row == col, pivot[member:member + 1, :], 0.0) + x + x.T
        inverse = split(unit_inverse(unit_ref, member))
        half = product(split(x), inverse)
        out[member] = product(inverse, split(half), contract=0)


def reverse(pairs):
    return [(receiver, sender) for sender, receiver in pairs]


def shards(inverse_front, factor, unit_lower, pivot_inverse, tile_list, tile_valid):
    plan = Plan(inverse_front, factor, unit_lower, tile_list)
    width, depth, lanes, members, steps = plan.width, plan.depth, plan.lanes, plan.members, plan.steps
    both = ("row", "col")
    factors = [factor[:, member * width:(member + 1) * width] for member in range(members)]

    def lane_sum(parts):
        out = parts[0]
        for shift in range(1, lanes):
            out = out + plan.swap(parts[lanes - shift], shift)
        return out

    def gather(member):
        return pl.pallas_call(
            functools.partial(gather_kernel, plan, member),
            in_specs=smem(2) + [pl.BlockSpec(memory_space=pl.ANY)] + vmem(1),
            out_specs=vmem(2 + lanes),
            out_shape=[jax.ShapeDtypeStruct((depth, depth * lanes), BF16)] * 2
            + [jax.ShapeDtypeStruct((depth, width), F32)] * lanes,
            scratch_shapes=[
                pltpu.VMEM((plan.na, plan.nb, plan.tile, plan.tile), F32),
                pltpu.SemaphoreType.DMA((plan.na, plan.nb)),
            ],
            compiler_params=PARAMS,
            cost_estimate=COST,
            name="gather_mirror",
        )(tile_list, tile_valid, inverse_front, factors[member])

    def forward(member, high, low, mirror, held, earlier):
        parts = [held] + [plan.swap(held, shift) for shift in range(1, lanes)]
        splits = plan.splits[member]
        outs = pl.pallas_call(
            functools.partial(forward_kernel, plan, member),
            in_specs=vmem(4 + lanes + len(earlier)),
            out_specs=vmem(splits + lanes),
            out_shape=[jax.ShapeDtypeStruct((depth // splits, width), F32)] * splits
            + [jax.ShapeDtypeStruct(((member + 1) * width // lanes, width), F32)] * lanes,
            scratch_shapes=[
                pltpu.VMEM((depth, width), F32),
                pltpu.VMEM((width, width), F32),
            ],
            compiler_params=PARAMS,
            cost_estimate=COST,
            name="forward",
        )(high, low, factors[member], mirror, *parts, *earlier)
        return outs[:splits], outs[splits:], parts[-1]

    hops = plan.line_hops()

    def enter(x, after=()):
        if after:
            x, _ = lax.optimization_barrier((x, tuple(after)))
        return lax.ppermute(x, "col", hops[0])

    def run(x, got, ties=()):
        sent = []
        for hop in range(1, len(hops)):
            x = plan.line_step(hop - 1, x, got)
            sent.append(x)
            tie = ties[hop - 1] if hop <= len(ties) else ()
            y = lax.optimization_barrier((x, tuple(tie)))[0] if tie else x
            got = lax.ppermute(y, "col", hops[hop])
        if len(hops) == 1:
            got = x = x + got
        return x, got, sent

    spread, collect = Chain(), Chain()
    count = members * steps
    tiles, held, mirror, chunks, entered = {}, {}, {}, [], {}
    after, cross, last_swap = (), [], ()
    for phase in range(count + 1):
        if phase < count:
            out, step = divmod(phase, steps)
            x = factors[out] if step == 0 else held[out]
            got_out, = spread.issue((x, both, plan.tree(step)), after=after)
        if phase:
            back, turn = divmod(phase - 1, steps)
            got_back, = collect.issue(
                (mirror[back], both, reverse(plan.tree(steps - 1 - turn))), after=after
            )
        if chunks and 0 not in entered:
            entered[0] = enter(chunks[0])
            entered[0], got_out, got_back = lax.optimization_barrier(
                (entered[0], got_out, got_back)
            )
        after = ()
        if phase % steps == 0 and phase < count:
            high, low, *parts = gather(out) if out == 0 else tiles[out]
            tiles[out] = (high, low)
            mirror[out] = lane_sum(parts)
        if phase % steps == 1 % steps and phase < count and out + 1 < members:
            tiles[out + 1] = gather(out + 1)
            after = (tiles[out + 1][0],)
        if phase < count:
            held[out] = jnp.where(plan.on_diagonal(), x, got_out) if step == 0 else x + got_out
        if phase:
            if turn < steps - 1:
                mirror[back] = mirror[back] + got_back
            else:
                sums, cross, last_swap = forward(back, *tiles[back], mirror[back], held[back], cross)
                share = sums[0].shape[0]
                after = tuple(
                    part + got_back[i * share:(i + 1) * share] for i, part in enumerate(sums)
                )
                chunks += after

    x, _ = lax.optimization_barrier((lane_sum(cross), after))
    for step in range(steps):
        x = x.reshape(2, x.shape[0] // 2, x.shape[1])
        bit = plan.bit(step)
        send = lax.dynamic_index_in_dim(x, 1 - bit, 0, keepdims=False)
        keep = lax.dynamic_index_in_dim(x, bit, 0, keepdims=False)
        x = keep + lax.ppermute(send, both, plan.bit_pairs(step))
    update = x

    def place(member, column):
        sums, splits = [], plan.splits[member]
        first = sum(plan.splits[:member])
        for i in range(first, first + splits):
            sums += [chunks[i], ends[i]]
        return pl.pallas_call(
            functools.partial(place_kernel, plan, member),
            in_specs=smem(1) + vmem(1 + 2 * splits)
            + [pl.BlockSpec(memory_space=pl.ANY)] * (member > 0),
            out_specs=pl.BlockSpec(memory_space=pl.ANY),
            out_shape=jax.ShapeDtypeStruct((inverse_front.shape[0], factor.shape[1]), F32),
            scratch_shapes=[
                pltpu.VMEM((depth, width), F32),
                pltpu.VMEM((plan.tile, width), F32),
                pltpu.SemaphoreType.DMA((plan.na,)),
                pltpu.SemaphoreType.DMA((members, plan.row_tiles)),
            ],
            input_output_aliases={2 + 2 * splits: 0} if member else {},
            compiler_params=PARAMS,
            cost_estimate=COST,
            name="place",
        )(tile_list, unit_lower, *sums, *([column] if member else []))

    ends, sent, column, last = {}, {}, None, len(chunks) - 1
    middle = len(hops) - 1
    for i in range(last + 1):
        if i < last:
            if i + 1 == last and last > 2:
                wait = (ends[i - 2],)
            else:
                wait = (entered[i], last_swap) if i == 0 else ()
            entered[i + 1] = enter(chunks[i + 1], wait)
        ties = [()] * (middle - 1) + [(entered[i + 1],)] if i < last and middle else ()
        chunks[i], ends[i], sent[i] = run(chunks[i], entered[i], ties)
    ahead = sent[max(last - 1, 0)]
    update, got, _ = run(update, enter(update), [(x,) for x in ahead])
    for member in range(members):
        column = place(member, column)
        if member == 0:
            got, _ = lax.optimization_barrier((got, column))

    x = update
    x = jnp.where(plan.at_end(), got, x)
    pieces = [x] + [lax.ppermute(x, both, plan.offset_pairs(r)) for r in range(1, 1 << steps)]
    x, _ = lax.optimization_barrier((jnp.concatenate(pieces), column))
    parts = [x] + [plan.swap(x, shift) for shift in range(1, lanes)]
    diagonal = pl.pallas_call(
        functools.partial(diagonal_kernel, plan),
        in_specs=vmem(2 + lanes),
        out_specs=vmem(1)[0],
        out_shape=jax.ShapeDtypeStruct(unit_lower.shape, F32),
        scratch_shapes=[pltpu.VMEM((lanes, members * width // lanes, width), F32)],
        compiler_params=PARAMS,
        cost_estimate=COST,
        name="diagonal",
    )(pivot_inverse, unit_lower, *parts)
    return (column, diagonal)


def solution(mesh):
    in_specs = (P("row", "col"), P("row", None), P(), P(), P(), P())
    out_specs = (P("row", None), P())
    return jax.shard_map(shards, mesh=mesh, in_specs=in_specs, out_specs=out_specs, check_vma=False)
```

```python
import functools

import jax
import jax.numpy as jnp
from jax import lax
from jax.experimental import pallas as pl
from jax.experimental.pallas import tpu as pltpu
from jax.sharding import PartitionSpec as P

F32 = jnp.float32
BF16 = jnp.bfloat16
VMEM = pltpu.MemorySpace.VMEM
SMEM = pltpu.MemorySpace.SMEM
COST = pl.CostEstimate(flops=1600 << 20, bytes_accessed=8 << 20, transcendentals=0)
PARAMS = pltpu.CompilerParams(vmem_limit_bytes=48 * 1024 * 1024)


def vmem(count):
    return [pl.BlockSpec(memory_space=VMEM)] * count


def smem(count):
    return [pl.BlockSpec(memory_space=SMEM)] * count


def split(x):
    high = x.astype(BF16)
    return high, (x - high.astype(F32)).astype(BF16)


def product(left, right, contract=1):
    def one(a, b):
        return lax.dot_general(a, b, (((contract,), (0,)), ((), ())), preferred_element_type=F32)

    return one(left[0], right[1]) + one(left[1], right[0]) + one(left[0], right[0])


def unit_inverse(ref, member):
    lower = ref[member]
    row = lax.broadcasted_iota(jnp.int32, lower.shape, 0)
    col = lax.broadcasted_iota(jnp.int32, lower.shape, 1)
    return jnp.where(row > col, lower, jnp.where(row == col, 1.0, 0.0).astype(F32))


class Plan:
    def __init__(self, front, factor, unit_lower, tile_list):
        self.rows, self.cols = lax.axis_size("row"), lax.axis_size("col")
        self.lanes = self.rows // self.cols
        self.members, self.width, _ = unit_lower.shape
        self.na = tile_list.shape[1] // self.rows
        self.tile = factor.shape[0] // self.na
        self.nb = self.na * self.lanes
        self.row_tiles = front.shape[0] // self.tile
        self.col_tiles = front.shape[1] // self.tile
        self.depth = factor.shape[0]
        bits = [1 << i for i in range((self.cols - 1).bit_length())]
        self.orders = [
            bits[lane % len(bits):] + bits[:lane % len(bits)] for lane in range(self.lanes)
        ]
        self.steps = len(bits)
        self.splits = [2] * self.members

    def device(self, chip, lane, col):
        return (chip * self.lanes + lane) * self.cols + col

    def tree(self, step):
        pairs = []
        for col in range(self.cols):
            for lane, order in enumerate(self.orders):
                held, later = [0], [0]
                for bit in order[:step]:
                    held = held + [x ^ bit for x in held]
                for bit in order[step + 1:]:
                    later = later + [x ^ bit for x in later]
                for offset in held:
                    child = col ^ offset ^ order[step]
                    if any(child ^ x > col for x in later):
                        pairs.append(
                            (self.device(col ^ offset, lane, col), self.device(child, lane, col))
                        )
        return pairs

    def swap(self, x, shift):
        pairs = []
        for row in range(self.rows):
            chip, lane = divmod(row, self.lanes)
            pairs.append((chip * self.lanes + (lane + shift) % self.lanes, row))
        return lax.ppermute(x, "row", pairs)

    def line_hops(self):
        count, half = self.cols, self.cols // 2
        inward = [[(i, i + 1), (count - 1 - i, count - 2 - i)] for i in range(half - 1)]
        outward = [
            [(half - 1 - i, half - 2 - i), (half + i, half + i + 1)] for i in range(half - 1)
        ]
        return inward + [[(half - 1, half), (half, half - 1)]] + outward

    def line_step(self, hop, x, got):
        half = self.cols // 2
        if hop < half:
            return x + got
        place, i = lax.axis_index("col"), hop - half
        return jnp.where((place == half - 2 - i) | (place == half + i + 1), got, x)

    def on_diagonal(self):
        return lax.axis_index("row") // self.lanes == lax.axis_index("col")

    def at_end(self):
        place = lax.axis_index("col")
        return (place == 0) | (place == self.cols - 1)

    def bit_pairs(self, step):
        return [
            (self.device(chip, lane, col), self.device(chip ^ order[step], lane, col))
            for chip in range(self.cols)
            for lane, order in enumerate(self.orders)
            for col in range(self.cols)
        ]

    def offset_pairs(self, offset):
        pairs = []
        for lane, order in enumerate(self.orders):
            flip = sum(
                bit for step, bit in enumerate(order) if offset >> (self.steps - 1 - step) & 1
            )
            for chip in range(self.cols):
                for col in range(self.cols):
                    pairs.append(
                        (self.device(chip, lane, col), self.device(chip ^ flip, lane, col))
                    )
        return pairs

    def place_of(self, lane):
        chip, place = lax.axis_index("row") // self.lanes, jnp.int32(0)
        for step, bit in enumerate(self.orders[lane]):
            place = jnp.where((chip & bit) != 0, place + (1 << (self.steps - 1 - step)), place)
        return place

    def bit(self, step):
        row = lax.axis_index("row")
        chip, value = row // self.lanes, jnp.int32(0)
        for lane, order in enumerate(self.orders):
            value = jnp.where((row % self.lanes == lane) & ((chip & order[step]) != 0), 1, value)
        return value


class Chain:
    def __init__(self):
        self.last = ()

    def issue(self, *requests, after=()):
        out = []
        for x, axis, pairs in requests:
            if self.last or after:
                x, _ = lax.optimization_barrier((x, self.last + tuple(after)))
            out.append(lax.ppermute(x, axis, pairs))
        self.last = tuple(out)
        return out


def gather_kernel(plan, member, tiles_ref, valid_ref, front, factor, high, low, *rest):
    mirror, (buffer, sems) = rest[:plan.lanes], rest[plan.lanes:]
    size, na, nb = plan.tile, plan.na, plan.nb
    row, col = lax.axis_index("row"), lax.axis_index("col")
    lane = lax.rem(row, plan.lanes)
    row_slots = [row * na + a for a in range(na)]
    col_slots = [
        col * nb + lax.rem(lane + b // na, plan.lanes) * na + b % na for b in range(nb)
    ]
    copies = []
    for a in range(na):
        for b in range(nb):
            i = jnp.clip(tiles_ref[member, row_slots[a]] - row * plan.row_tiles, 0, plan.row_tiles - 1)
            j = jnp.clip(tiles_ref[member, col_slots[b]] - col * plan.col_tiles, 0, plan.col_tiles - 1)
            copy = pltpu.make_async_copy(
                front.at[
                    pl.ds(pl.multiple_of(i * size, size), size),
                    pl.ds(pl.multiple_of(j * size, size), size),
                ],
                buffer.at[a, b],
                sems.at[a, b],
            )
            copy.start()
            copies.append(copy)
    right = split(factor[...])
    local_row = lax.broadcasted_iota(jnp.int32, (size, size), 0)
    local_col = lax.broadcasted_iota(jnp.int32, (size, size), 1)
    for a in range(na):
        for b in range(nb):
            copies[a * nb + b].wait()
            live = (valid_ref[member, row_slots[a]] > 0) & (valid_ref[member, col_slots[b]] > 0)
            ahead = (tiles_ref[member, row_slots[a]] - tiles_ref[member, col_slots[b]]) * size
            gap = local_row - local_col + ahead
            x = buffer[a, b]
            x = jnp.where(gap > 0, x, jnp.where(gap == 0, 0.5 * x, 0.0))
            x = jnp.where(live, x, 0.0)
            x_high, x_low = split(x)
            high[a * size:(a + 1) * size, b * size:(b + 1) * size] = x_high
            low[a * size:(a + 1) * size, b * size:(b + 1) * size] = x_low
    for b in range(nb):
        left = (high[:, b * size:(b + 1) * size], low[:, b * size:(b + 1) * size])
        first = b % na * size
        mirror[b // na][first:first + size, :] = product(left, right, contract=0)


def forward_kernel(plan, member, high, low, factor, mirror, *rest):
    lanes, size, depth = plan.lanes, plan.tile, plan.depth
    parts, rest = rest[:lanes], rest[lanes:]
    earlier, rest = rest[:lanes * bool(member)], rest[lanes * bool(member):]
    splits = plan.splits[member]
    totals, rest = rest[:splits], rest[splits:]
    cross, (total, whole) = rest[:lanes], rest[lanes:]
    right = [split(part[...]) for part in parts]
    for a in range(plan.na):
        rows = slice(a * size, (a + 1) * size)
        total[rows, :] = sum(
            product(
                (high[rows, i * depth:(i + 1) * depth], low[rows, i * depth:(i + 1) * depth]),
                right[i],
            )
            for i in range(lanes)
        )
    share = depth // splits
    on_diagonal = plan.on_diagonal()
    for i in range(splits):
        rows = slice(i * share, (i + 1) * share)
        totals[i][...] = total[rows, :] + jnp.where(on_diagonal, mirror[rows, :], 0.0)
    whole[...] = product(split(factor[...]), split(total[...]), contract=0)
    share = plan.width // lanes
    lane = lax.rem(lax.axis_index("row"), lanes)
    for i in range(lanes):
        first = pl.multiple_of(lax.rem(lane + i, lanes) * share, share)
        cross[i][member * share:, :] = whole[pl.ds(first, share), :]
        if member:
            cross[i][:member * share, :] = earlier[i][...]


def place_kernel(plan, member, tiles_ref, unit_ref, *rest):
    splits = plan.splits[member]
    sums, rest = rest[:2 * splits], rest[2 * splits:]
    out, stack, zeros, sems, zero_sems = rest[member > 0:]
    size, width = plan.tile, plan.width
    row, at_end = lax.axis_index("row"), plan.at_end()

    def zero_copies(act):
        for other in range(plan.members):
            for t in range(plan.row_tiles):
                taken = False
                for a in range(plan.na):
                    taken = taken | (
                        tiles_ref[other, row * plan.na + a] == row * plan.row_tiles + t
                    )
                copy = pltpu.make_async_copy(
                    zeros,
                    out.at[t * size:(t + 1) * size, other * width:(other + 1) * width],
                    zero_sems.at[other, t],
                )
                pl.when(jnp.logical_not(taken))(functools.partial(act, copy))

    if member == 0:
        zeros[...] = jnp.zeros_like(zeros)
        zero_copies(lambda copy: copy.start())
    right = split(unit_inverse(unit_ref, member))
    share = plan.depth // splits
    for i in range(splits):
        x = jnp.where(at_end, sums[2 * i + 1][...], sums[2 * i][...])
        stack[i * share:(i + 1) * share, :] = -product(split(x), right)
    copies = []
    for a in range(plan.na):
        t = jnp.clip(
            tiles_ref[member, row * plan.na + a] - row * plan.row_tiles, 0, plan.row_tiles - 1
        )
        copy = pltpu.make_async_copy(
            stack.at[a * size:(a + 1) * size, :],
            out.at[
                pl.ds(pl.multiple_of(t * size, size), size), member * width:(member + 1) * width
            ],
            sems.at[a],
        )
        copy.start()
        copies.append(copy)
    for copy in copies:
        copy.wait()
    if member == 0:
        zero_copies(lambda copy: copy.wait())


def diagonal_kernel(plan, pivot, unit_ref, *rest):
    parts, (out, cross) = rest[:plan.lanes], rest[plan.lanes:]
    width, lanes, members = plan.width, plan.lanes, plan.members
    lane = lax.rem(lax.axis_index("row"), lanes)
    count = 1 << plan.steps
    size = members * width // (lanes * count)
    for other in range(lanes):
        mine = plan.place_of(other)
        for place in range(count):
            first = pl.multiple_of((mine ^ place) * size, size)
            piece = parts[0][pl.ds(first, size), :]
            for i in range(1, lanes):
                piece = jnp.where(
                    lax.rem(lane + i, lanes) == other, parts[i][pl.ds(first, size), :], piece
                )
            cross[other, place * size:(place + 1) * size, :] = piece
    share = width // lanes
    row = lax.broadcasted_iota(jnp.int32, (width, width), 0)
    col = lax.broadcasted_iota(jnp.int32, (width, width), 1)
    for member in range(members):
        rows = slice(member * share, (member + 1) * share)
        x = jnp.concatenate([cross[other, rows, :] for other in range(lanes)])
        x = jnp.where(row == col, pivot[member:member + 1, :], 0.0) + x + x.T
        inverse = split(unit_inverse(unit_ref, member))
        half = product(split(x), inverse)
        out[member] = product(inverse, split(half), contract=0)


def reverse(pairs):
    return [(receiver, sender) for sender, receiver in pairs]


def shards(inverse_front, factor, unit_lower, pivot_inverse, tile_list, tile_valid):
    plan = Plan(inverse_front, factor, unit_lower, tile_list)
    width, depth, lanes, members, steps = plan.width, plan.depth, plan.lanes, plan.members, plan.steps
    both = ("row", "col")
    factors = [factor[:, member * width:(member + 1) * width] for member in range(members)]

    def lane_sum(parts):
        out = parts[0]
        for shift in range(1, lanes):
            out = out + plan.swap(parts[lanes - shift], shift)
        return out

    def gather(member):
        return pl.pallas_call(
            functools.partial(gather_kernel, plan, member),
            in_specs=smem(2) + [pl.BlockSpec(memory_space=pl.ANY)] + vmem(1),
            out_specs=vmem(2 + lanes),
            out_shape=[jax.ShapeDtypeStruct((depth, depth * lanes), BF16)] * 2
            + [jax.ShapeDtypeStruct((depth, width), F32)] * lanes,
            scratch_shapes=[
                pltpu.VMEM((plan.na, plan.nb, plan.tile, plan.tile), F32),
                pltpu.SemaphoreType.DMA((plan.na, plan.nb)),
            ],
            compiler_params=PARAMS,
            cost_estimate=COST,
            name="gather_mirror",
        )(tile_list, tile_valid, inverse_front, factors[member])

    def forward(member, high, low, mirror, held, earlier):
        parts = [held] + [plan.swap(held, shift) for shift in range(1, lanes)]
        splits = plan.splits[member]
        outs = pl.pallas_call(
            functools.partial(forward_kernel, plan, member),
            in_specs=vmem(4 + lanes + len(earlier)),
            out_specs=vmem(splits + lanes),
            out_shape=[jax.ShapeDtypeStruct((depth // splits, width), F32)] * splits
            + [jax.ShapeDtypeStruct(((member + 1) * width // lanes, width), F32)] * lanes,
            scratch_shapes=[
                pltpu.VMEM((depth, width), F32),
                pltpu.VMEM((width, width), F32),
            ],
            compiler_params=PARAMS,
            cost_estimate=COST,
            name="forward",
        )(high, low, factors[member], mirror, *parts, *earlier)
        return outs[:splits], outs[splits:], parts[-1]

    hops = plan.line_hops()

    def enter(x, after=()):
        if after:
            x, _ = lax.optimization_barrier((x, tuple(after)))
        return lax.ppermute(x, "col", hops[0])

    def run(x, got, ties=()):
        sent, brought = [], [got]
        for hop in range(1, len(hops)):
            x = plan.line_step(hop - 1, x, got)
            sent.append(x)
            tie = ties[hop - 1] if hop <= len(ties) else ()
            y = lax.optimization_barrier((x, tuple(tie)))[0] if tie else x
            got = lax.ppermute(y, "col", hops[hop])
            brought.append(got)
        if len(hops) == 1:
            got = x = x + got
        return x, got, sent, brought

    spread, collect = Chain(), Chain()
    count = members * steps
    tiles, held, mirror, chunks, entered = {}, {}, {}, [], {}
    after, cross, last_swap = (), [], ()
    for phase in range(count + 1):
        if phase < count:
            out, step = divmod(phase, steps)
            x = factors[out] if step == 0 else held[out]
            got_out, = spread.issue((x, both, plan.tree(step)), after=after)
        if phase:
            back, turn = divmod(phase - 1, steps)
            got_back, = collect.issue(
                (mirror[back], both, reverse(plan.tree(steps - 1 - turn))), after=after
            )
        if chunks and 0 not in entered:
            entered[0] = enter(chunks[0])
            entered[0], got_out, got_back = lax.optimization_barrier(
                (entered[0], got_out, got_back)
            )
        after = ()
        if phase % steps == 0 and phase < count:
            high, low, *parts = gather(out) if out == 0 else tiles[out]
            tiles[out] = (high, low)
            mirror[out] = lane_sum(parts)
        if phase % steps == 1 % steps and phase < count and out + 1 < members:
            tiles[out + 1] = gather(out + 1)
            after = (tiles[out + 1][0],)
        if phase < count:
            held[out] = jnp.where(plan.on_diagonal(), x, got_out) if step == 0 else x + got_out
        if phase:
            if turn < steps - 1:
                mirror[back] = mirror[back] + got_back
            else:
                sums, cross, last_swap = forward(back, *tiles[back], mirror[back], held[back], cross)
                share = sums[0].shape[0]
                after = tuple(
                    part + got_back[i * share:(i + 1) * share] for i, part in enumerate(sums)
                )
                chunks += after

    x, _ = lax.optimization_barrier((lane_sum(cross), after))
    for step in range(steps):
        x = x.reshape(2, x.shape[0] // 2, x.shape[1])
        bit = plan.bit(step)
        send = lax.dynamic_index_in_dim(x, 1 - bit, 0, keepdims=False)
        keep = lax.dynamic_index_in_dim(x, bit, 0, keepdims=False)
        x = keep + lax.ppermute(send, both, plan.bit_pairs(step))
    update = x

    def place(member, column):
        sums, splits = [], plan.splits[member]
        first = sum(plan.splits[:member])
        for i in range(first, first + splits):
            sums += [chunks[i], ends[i]]
        return pl.pallas_call(
            functools.partial(place_kernel, plan, member),
            in_specs=smem(1) + vmem(1 + 2 * splits)
            + [pl.BlockSpec(memory_space=pl.ANY)] * (member > 0),
            out_specs=pl.BlockSpec(memory_space=pl.ANY),
            out_shape=jax.ShapeDtypeStruct((inverse_front.shape[0], factor.shape[1]), F32),
            scratch_shapes=[
                pltpu.VMEM((depth, width), F32),
                pltpu.VMEM((plan.tile, width), F32),
                pltpu.SemaphoreType.DMA((plan.na,)),
                pltpu.SemaphoreType.DMA((members, plan.row_tiles)),
            ],
            input_output_aliases={2 + 2 * splits: 0} if member else {},
            compiler_params=PARAMS,
            cost_estimate=COST,
            name="place",
        )(tile_list, unit_lower, *sums, *([column] if member else []))

    ends, sent, brought, column = {}, {}, {}, None
    last, middle = len(chunks) - 1, len(hops) - 1
    for i in range(last + 1):
        if i > 2:
            entered[i] = enter(chunks[i], (brought[i - 2][min(1, middle)],))
        if i == 1 and last > 1:
            entered[2] = enter(chunks[2])
        ties = [()] * middle
        if i < 2 and i < last and middle:
            if i == 0:
                entered[1] = enter(chunks[1], (entered[0], last_swap))
            ties[-1] = (entered[i + 1],)
        elif i > 1 and middle:
            ties = [(brought[i - 2][hop + 1],) for hop in range(1, middle)]
            ties.append((brought[i - 1][-1],))
        chunks[i], ends[i], sent[i], brought[i] = run(chunks[i], entered[i], ties)
    update, got, _, _ = run(update, enter(update), [(x,) for x in sent[last]])
    for member in range(members):
        column = place(member, column)
        if member == 0:
            got, _ = lax.optimization_barrier((got, column))

    x = update
    x = jnp.where(plan.at_end(), got, x)
    pieces = [x] + [lax.ppermute(x, both, plan.offset_pairs(r)) for r in range(1, 1 << steps)]
    x, _ = lax.optimization_barrier((jnp.concatenate(pieces), column))
    parts = [x] + [plan.swap(x, shift) for shift in range(1, lanes)]
    diagonal = pl.pallas_call(
        functools.partial(diagonal_kernel, plan),
        in_specs=vmem(2 + lanes),
        out_specs=vmem(1)[0],
        out_shape=jax.ShapeDtypeStruct(unit_lower.shape, F32),
        scratch_shapes=[pltpu.VMEM((lanes, members * width // lanes, width), F32)],
        compiler_params=PARAMS,
        cost_estimate=COST,
        name="diagonal",
    )(pivot_inverse, unit_lower, *parts)
    return (column, diagonal)


def solution(mesh):
    in_specs = (P("row", "col"), P("row", None), P(), P(), P(), P())
    out_specs = (P("row", None), P())
    return jax.shard_map(shards, mesh=mesh, in_specs=in_specs, out_specs=out_specs, check_vma=False)
```

```python
import functools

import jax
import jax.numpy as jnp
from jax import lax
from jax.experimental import pallas as pl
from jax.experimental.pallas import tpu as pltpu
from jax.sharding import PartitionSpec as P

F32 = jnp.float32
BF16 = jnp.bfloat16
VMEM = pltpu.MemorySpace.VMEM
SMEM = pltpu.MemorySpace.SMEM
COST = pl.CostEstimate(flops=1600 << 20, bytes_accessed=8 << 20, transcendentals=0)
PARAMS = pltpu.CompilerParams(vmem_limit_bytes=48 * 1024 * 1024)


def vmem(count):
    return [pl.BlockSpec(memory_space=VMEM)] * count


def smem(count):
    return [pl.BlockSpec(memory_space=SMEM)] * count


def split(x):
    high = x.astype(BF16)
    return high, (x - high.astype(F32)).astype(BF16)


def product(left, right, contract=1):
    def one(a, b):
        return lax.dot_general(a, b, (((contract,), (0,)), ((), ())), preferred_element_type=F32)

    return one(left[0], right[1]) + one(left[1], right[0]) + one(left[0], right[0])


def unit_inverse(ref, member):
    lower = ref[member]
    row = lax.broadcasted_iota(jnp.int32, lower.shape, 0)
    col = lax.broadcasted_iota(jnp.int32, lower.shape, 1)
    return jnp.where(row > col, lower, jnp.where(row == col, 1.0, 0.0).astype(F32))


class Plan:
    def __init__(self, front, factor, unit_lower, tile_list):
        self.rows, self.cols = lax.axis_size("row"), lax.axis_size("col")
        self.lanes = self.rows // self.cols
        self.members, self.width, _ = unit_lower.shape
        self.na = tile_list.shape[1] // self.rows
        self.tile = factor.shape[0] // self.na
        self.nb = self.na * self.lanes
        self.row_tiles = front.shape[0] // self.tile
        self.col_tiles = front.shape[1] // self.tile
        self.depth = factor.shape[0]
        bits = [1 << i for i in range((self.cols - 1).bit_length())]
        self.orders = [
            bits[lane % len(bits):] + bits[:lane % len(bits)] for lane in range(self.lanes)
        ]
        self.steps = len(bits)
        self.splits = [2] * self.members

    def device(self, chip, lane, col):
        return (chip * self.lanes + lane) * self.cols + col

    def tree(self, step):
        pairs = []
        for col in range(self.cols):
            for lane, order in enumerate(self.orders):
                held, later = [0], [0]
                for bit in order[:step]:
                    held = held + [x ^ bit for x in held]
                for bit in order[step + 1:]:
                    later = later + [x ^ bit for x in later]
                for offset in held:
                    child = col ^ offset ^ order[step]
                    if any(child ^ x > col for x in later):
                        pairs.append(
                            (self.device(col ^ offset, lane, col), self.device(child, lane, col))
                        )
        return pairs

    def swap(self, x, shift):
        pairs = []
        for row in range(self.rows):
            chip, lane = divmod(row, self.lanes)
            pairs.append((chip * self.lanes + (lane + shift) % self.lanes, row))
        return lax.ppermute(x, "row", pairs)

    def line_hops(self):
        count, half = self.cols, self.cols // 2
        inward = [[(i, i + 1), (count - 1 - i, count - 2 - i)] for i in range(half - 1)]
        outward = [
            [(half - 1 - i, half - 2 - i), (half + i, half + i + 1)] for i in range(half - 1)
        ]
        return inward + [[(half - 1, half), (half, half - 1)]] + outward

    def line_step(self, hop, x, got):
        half = self.cols // 2
        if hop < half:
            return x + got
        place, i = lax.axis_index("col"), hop - half
        return jnp.where((place == half - 2 - i) | (place == half + i + 1), got, x)

    def on_diagonal(self):
        return lax.axis_index("row") // self.lanes == lax.axis_index("col")

    def at_end(self):
        place = lax.axis_index("col")
        return (place == 0) | (place == self.cols - 1)

    def bit_pairs(self, step):
        return [
            (self.device(chip, lane, col), self.device(chip ^ order[step], lane, col))
            for chip in range(self.cols)
            for lane, order in enumerate(self.orders)
            for col in range(self.cols)
        ]

    def offset_pairs(self, offset):
        pairs = []
        for lane, order in enumerate(self.orders):
            flip = sum(
                bit for step, bit in enumerate(order) if offset >> (self.steps - 1 - step) & 1
            )
            for chip in range(self.cols):
                for col in range(self.cols):
                    pairs.append(
                        (self.device(chip, lane, col), self.device(chip ^ flip, lane, col))
                    )
        return pairs

    def place_of(self, lane):
        chip, place = lax.axis_index("row") // self.lanes, jnp.int32(0)
        for step, bit in enumerate(self.orders[lane]):
            place = jnp.where((chip & bit) != 0, place + (1 << (self.steps - 1 - step)), place)
        return place

    def bit(self, step):
        row = lax.axis_index("row")
        chip, value = row // self.lanes, jnp.int32(0)
        for lane, order in enumerate(self.orders):
            value = jnp.where((row % self.lanes == lane) & ((chip & order[step]) != 0), 1, value)
        return value


class Chain:
    def __init__(self):
        self.last = ()

    def issue(self, *requests, after=()):
        out = []
        for x, axis, pairs in requests:
            if self.last or after:
                x, _ = lax.optimization_barrier((x, self.last + tuple(after)))
            out.append(lax.ppermute(x, axis, pairs))
        self.last = tuple(out)
        return out


def gather_kernel(plan, member, tiles_ref, valid_ref, front, factor, high, low, *rest):
    mirror, (buffer, sems) = rest[:plan.lanes], rest[plan.lanes:]
    size, na, nb = plan.tile, plan.na, plan.nb
    row, col = lax.axis_index("row"), lax.axis_index("col")
    lane = lax.rem(row, plan.lanes)
    row_slots = [row * na + a for a in range(na)]
    col_slots = [
        col * nb + lax.rem(lane + b // na, plan.lanes) * na + b % na for b in range(nb)
    ]
    copies = []
    for a in range(na):
        for b in range(nb):
            i = jnp.clip(tiles_ref[member, row_slots[a]] - row * plan.row_tiles, 0, plan.row_tiles - 1)
            j = jnp.clip(tiles_ref[member, col_slots[b]] - col * plan.col_tiles, 0, plan.col_tiles - 1)
            copy = pltpu.make_async_copy(
                front.at[
                    pl.ds(pl.multiple_of(i * size, size), size),
                    pl.ds(pl.multiple_of(j * size, size), size),
                ],
                buffer.at[a, b],
                sems.at[a, b],
            )
            copy.start()
            copies.append(copy)
    right = split(factor[...])
    local_row = lax.broadcasted_iota(jnp.int32, (size, size), 0)
    local_col = lax.broadcasted_iota(jnp.int32, (size, size), 1)
    for a in range(na):
        for b in range(nb):
            copies[a * nb + b].wait()
            live = (valid_ref[member, row_slots[a]] > 0) & (valid_ref[member, col_slots[b]] > 0)
            ahead = (tiles_ref[member, row_slots[a]] - tiles_ref[member, col_slots[b]]) * size
            gap = local_row - local_col + ahead
            x = buffer[a, b]
            x = jnp.where(gap > 0, x, jnp.where(gap == 0, 0.5 * x, 0.0))
            x = jnp.where(live, x, 0.0)
            x_high, x_low = split(x)
            high[a * size:(a + 1) * size, b * size:(b + 1) * size] = x_high
            low[a * size:(a + 1) * size, b * size:(b + 1) * size] = x_low
    for b in range(nb):
        left = (high[:, b * size:(b + 1) * size], low[:, b * size:(b + 1) * size])
        first = b % na * size
        mirror[b // na][first:first + size, :] = product(left, right, contract=0)


def forward_kernel(plan, member, high, low, factor, mirror, *rest):
    lanes, size, depth = plan.lanes, plan.tile, plan.depth
    parts, rest = rest[:lanes], rest[lanes:]
    earlier, rest = rest[:lanes * bool(member)], rest[lanes * bool(member):]
    splits = plan.splits[member]
    totals, rest = rest[:splits], rest[splits:]
    cross, (total, whole) = rest[:lanes], rest[lanes:]
    right = [split(part[...]) for part in parts]
    for a in range(plan.na):
        rows = slice(a * size, (a + 1) * size)
        total[rows, :] = sum(
            product(
                (high[rows, i * depth:(i + 1) * depth], low[rows, i * depth:(i + 1) * depth]),
                right[i],
            )
            for i in range(lanes)
        )
    share = depth // splits
    on_diagonal = plan.on_diagonal()
    for i in range(splits):
        rows = slice(i * share, (i + 1) * share)
        totals[i][...] = total[rows, :] + jnp.where(on_diagonal, mirror[rows, :], 0.0)
    whole[...] = product(split(factor[...]), split(total[...]), contract=0)
    share = plan.width // lanes
    lane = lax.rem(lax.axis_index("row"), lanes)
    for i in range(lanes):
        first = pl.multiple_of(lax.rem(lane + i, lanes) * share, share)
        cross[i][member * share:, :] = whole[pl.ds(first, share), :]
        if member:
            cross[i][:member * share, :] = earlier[i][...]


def place_kernel(plan, member, tiles_ref, unit_ref, *rest):
    splits = plan.splits[member]
    sums, rest = rest[:2 * splits], rest[2 * splits:]
    out, stack, zeros, sems, zero_sems = rest[member > 0:]
    size, width = plan.tile, plan.width
    row, at_end = lax.axis_index("row"), plan.at_end()

    def zero_copies(act):
        for other in range(plan.members):
            for t in range(plan.row_tiles):
                taken = False
                for a in range(plan.na):
                    taken = taken | (
                        tiles_ref[other, row * plan.na + a] == row * plan.row_tiles + t
                    )
                copy = pltpu.make_async_copy(
                    zeros,
                    out.at[t * size:(t + 1) * size, other * width:(other + 1) * width],
                    zero_sems.at[other, t],
                )
                pl.when(jnp.logical_not(taken))(functools.partial(act, copy))

    if member == 0:
        zeros[...] = jnp.zeros_like(zeros)
        zero_copies(lambda copy: copy.start())
    right = split(unit_inverse(unit_ref, member))
    share = plan.depth // splits
    for i in range(splits):
        x = jnp.where(at_end, sums[2 * i + 1][...], sums[2 * i][...])
        stack[i * share:(i + 1) * share, :] = -product(split(x), right)
    copies = []
    for a in range(plan.na):
        t = jnp.clip(
            tiles_ref[member, row * plan.na + a] - row * plan.row_tiles, 0, plan.row_tiles - 1
        )
        copy = pltpu.make_async_copy(
            stack.at[a * size:(a + 1) * size, :],
            out.at[
                pl.ds(pl.multiple_of(t * size, size), size), member * width:(member + 1) * width
            ],
            sems.at[a],
        )
        copy.start()
        copies.append(copy)
    for copy in copies:
        copy.wait()
    if member == 0:
        zero_copies(lambda copy: copy.wait())


def diagonal_kernel(plan, pivot, unit_ref, *rest):
    parts, (out, cross) = rest[:plan.lanes], rest[plan.lanes:]
    width, lanes, members = plan.width, plan.lanes, plan.members
    lane = lax.rem(lax.axis_index("row"), lanes)
    count = 1 << plan.steps
    size = members * width // (lanes * count)
    for other in range(lanes):
        mine = plan.place_of(other)
        for place in range(count):
            first = pl.multiple_of((mine ^ place) * size, size)
            piece = parts[0][pl.ds(first, size), :]
            for i in range(1, lanes):
                piece = jnp.where(
                    lax.rem(lane + i, lanes) == other, parts[i][pl.ds(first, size), :], piece
                )
            cross[other, place * size:(place + 1) * size, :] = piece
    share = width // lanes
    row = lax.broadcasted_iota(jnp.int32, (width, width), 0)
    col = lax.broadcasted_iota(jnp.int32, (width, width), 1)
    for member in range(members):
        rows = slice(member * share, (member + 1) * share)
        x = jnp.concatenate([cross[other, rows, :] for other in range(lanes)])
        x = jnp.where(row == col, pivot[member:member + 1, :], 0.0) + x + x.T
        inverse = split(unit_inverse(unit_ref, member))
        half = product(split(x), inverse)
        out[member] = product(inverse, split(half), contract=0)


def reverse(pairs):
    return [(receiver, sender) for sender, receiver in pairs]


def shards(inverse_front, factor, unit_lower, pivot_inverse, tile_list, tile_valid):
    plan = Plan(inverse_front, factor, unit_lower, tile_list)
    width, depth, lanes, members, steps = plan.width, plan.depth, plan.lanes, plan.members, plan.steps
    both = ("row", "col")
    factors = [factor[:, member * width:(member + 1) * width] for member in range(members)]

    def lane_sum(parts):
        out = parts[0]
        for shift in range(1, lanes):
            out = out + plan.swap(parts[lanes - shift], shift)
        return out

    def gather(member):
        return pl.pallas_call(
            functools.partial(gather_kernel, plan, member),
            in_specs=smem(2) + [pl.BlockSpec(memory_space=pl.ANY)] + vmem(1),
            out_specs=vmem(2 + lanes),
            out_shape=[jax.ShapeDtypeStruct((depth, depth * lanes), BF16)] * 2
            + [jax.ShapeDtypeStruct((depth, width), F32)] * lanes,
            scratch_shapes=[
                pltpu.VMEM((plan.na, plan.nb, plan.tile, plan.tile), F32),
                pltpu.SemaphoreType.DMA((plan.na, plan.nb)),
            ],
            compiler_params=PARAMS,
            cost_estimate=COST,
            name="gather_mirror",
        )(tile_list, tile_valid, inverse_front, factors[member])

    def forward(member, high, low, mirror, held, earlier):
        parts = [held] + [plan.swap(held, shift) for shift in range(1, lanes)]
        splits = plan.splits[member]
        outs = pl.pallas_call(
            functools.partial(forward_kernel, plan, member),
            in_specs=vmem(4 + lanes + len(earlier)),
            out_specs=vmem(splits + lanes),
            out_shape=[jax.ShapeDtypeStruct((depth // splits, width), F32)] * splits
            + [jax.ShapeDtypeStruct(((member + 1) * width // lanes, width), F32)] * lanes,
            scratch_shapes=[
                pltpu.VMEM((depth, width), F32),
                pltpu.VMEM((width, width), F32),
            ],
            compiler_params=PARAMS,
            cost_estimate=COST,
            name="forward",
        )(high, low, factors[member], mirror, *parts, *earlier)
        return outs[:splits], outs[splits:]

    hops = plan.line_hops()

    def enter(x, after=()):
        if after:
            x, _ = lax.optimization_barrier((x, tuple(after)))
        return lax.ppermute(x, "col", hops[0])

    def run(x, got, ties=(), second=None):
        sent, brought = [], [got]
        for hop in range(1, len(hops)):
            x = plan.line_step(hop - 1, x, got)
            sent.append(x)
            tie = ties[hop - 1] if hop <= len(ties) else ()
            y = lax.optimization_barrier((x, tuple(tie)))[0] if tie else x
            if hop == 1 and second is not None:
                got = second
            else:
                got = lax.ppermute(y, "col", hops[hop])
            brought.append(got)
        if len(hops) == 1:
            got = x = x + got
        return x, got, sent, brought

    spread, collect = Chain(), Chain()
    count = members * steps
    tiles, held, mirror, chunks, entered = {}, {}, {}, [], {}
    after, cross, second = (), [], None
    for phase in range(count + 1):
        if phase < count:
            out, step = divmod(phase, steps)
            x = factors[out] if step == 0 else held[out]
            got_out, = spread.issue((x, both, plan.tree(step)), after=after)
        if phase:
            back, turn = divmod(phase - 1, steps)
            got_back, = collect.issue(
                (mirror[back], both, reverse(plan.tree(steps - 1 - turn))), after=after
            )
        if chunks and 0 not in entered:
            entered[0] = enter(chunks[0])
            entered[0], got_out = lax.optimization_barrier((entered[0], got_out))
            if len(hops) > 1 and len(chunks) > 1:
                second = lax.ppermute(plan.line_step(0, chunks[0], entered[0]), "col", hops[1])
                entered[1] = enter(chunks[1], (entered[0],))
                second, entered[1], got_back = lax.optimization_barrier(
                    (second, entered[1], got_back)
                )
        after = ()
        if phase % steps == 0 and phase < count:
            high, low, *parts = gather(out) if out == 0 else tiles[out]
            tiles[out] = (high, low)
            mirror[out] = lane_sum(parts)
        if phase % steps == 1 % steps and phase < count and out + 1 < members:
            tiles[out + 1] = gather(out + 1)
            after = (tiles[out + 1][0],)
        if phase < count:
            held[out] = jnp.where(plan.on_diagonal(), x, got_out) if step == 0 else x + got_out
        if phase:
            if turn < steps - 1:
                mirror[back] = mirror[back] + got_back
            else:
                sums, cross = forward(back, *tiles[back], mirror[back], held[back], cross)
                share = sums[0].shape[0]
                after = tuple(
                    part + got_back[i * share:(i + 1) * share] for i, part in enumerate(sums)
                )
                chunks += after

    x, _ = lax.optimization_barrier((lane_sum(cross), after))
    for step in range(steps):
        x = x.reshape(2, x.shape[0] // 2, x.shape[1])
        bit = plan.bit(step)
        send = lax.dynamic_index_in_dim(x, 1 - bit, 0, keepdims=False)
        keep = lax.dynamic_index_in_dim(x, bit, 0, keepdims=False)
        x = keep + lax.ppermute(send, both, plan.bit_pairs(step))
    update = x

    def place(member, column):
        sums, splits = [], plan.splits[member]
        first = sum(plan.splits[:member])
        for i in range(first, first + splits):
            sums += [chunks[i], ends[i]]
        return pl.pallas_call(
            functools.partial(place_kernel, plan, member),
            in_specs=smem(1) + vmem(1 + 2 * splits)
            + [pl.BlockSpec(memory_space=pl.ANY)] * (member > 0),
            out_specs=pl.BlockSpec(memory_space=pl.ANY),
            out_shape=jax.ShapeDtypeStruct((inverse_front.shape[0], factor.shape[1]), F32),
            scratch_shapes=[
                pltpu.VMEM((depth, width), F32),
                pltpu.VMEM((plan.tile, width), F32),
                pltpu.SemaphoreType.DMA((plan.na,)),
                pltpu.SemaphoreType.DMA((members, plan.row_tiles)),
            ],
            input_output_aliases={2 + 2 * splits: 0} if member else {},
            compiler_params=PARAMS,
            cost_estimate=COST,
            name="place",
        )(tile_list, unit_lower, *sums, *([column] if member else []))

    ends, sent, brought, column = {}, {}, {}, None
    last, middle = len(chunks) - 1, len(hops) - 1
    for i in range(last + 1):
        if i > 2:
            entered[i] = enter(chunks[i], (brought[i - 2][min(1, middle)],))
        if i == 1 and last > 1:
            entered[2] = enter(chunks[2])
        ties = [()] * middle
        if i < 2 and i < last and middle:
            if 1 not in entered:
                entered[1] = enter(chunks[1], (entered[0],))
            ties[-1] = (entered[i + 1],)
        elif i > 1 and middle:
            ties = [(brought[i - 2][hop + 1],) for hop in range(1, middle)]
            ties.append((brought[i - 1][-1],))
        chunks[i], ends[i], sent[i], brought[i] = run(
            chunks[i], entered[i], ties, second if i == 0 else None
        )
    update, got, _, _ = run(update, enter(update), [(x,) for x in sent[last]])
    for member in range(members):
        column = place(member, column)
        if member == 0:
            got, _ = lax.optimization_barrier((got, column))

    x = update
    x = jnp.where(plan.at_end(), got, x)
    pieces = [x] + [lax.ppermute(x, both, plan.offset_pairs(r)) for r in range(1, 1 << steps)]
    x, _ = lax.optimization_barrier((jnp.concatenate(pieces), column))
    parts = [x] + [plan.swap(x, shift) for shift in range(1, lanes)]
    diagonal = pl.pallas_call(
        functools.partial(diagonal_kernel, plan),
        in_specs=vmem(2 + lanes),
        out_specs=vmem(1)[0],
        out_shape=jax.ShapeDtypeStruct(unit_lower.shape, F32),
        scratch_shapes=[pltpu.VMEM((lanes, members * width // lanes, width), F32)],
        compiler_params=PARAMS,
        cost_estimate=COST,
        name="diagonal",
    )(pivot_inverse, unit_lower, *parts)
    return (column, diagonal)


def solution(mesh):
    in_specs = (P("row", "col"), P("row", None), P(), P(), P(), P())
    out_specs = (P("row", None), P())
    return jax.shard_map(shards, mesh=mesh, in_specs=in_specs, out_specs=out_specs, check_vma=False)
```

```python
import functools

import jax
import jax.numpy as jnp
from jax import lax
from jax.experimental import pallas as pl
from jax.experimental.pallas import tpu as pltpu
from jax.sharding import PartitionSpec as P

F32 = jnp.float32
BF16 = jnp.bfloat16
VMEM = pltpu.MemorySpace.VMEM
SMEM = pltpu.MemorySpace.SMEM
COST = pl.CostEstimate(flops=1600 << 20, bytes_accessed=8 << 20, transcendentals=0)
PARAMS = pltpu.CompilerParams(vmem_limit_bytes=48 * 1024 * 1024)


def vmem(count):
    return [pl.BlockSpec(memory_space=VMEM)] * count


def smem(count):
    return [pl.BlockSpec(memory_space=SMEM)] * count


def split(x):
    high = x.astype(BF16)
    return high, (x - high.astype(F32)).astype(BF16)


def product(left, right, contract=1):
    def one(a, b):
        return lax.dot_general(a, b, (((contract,), (0,)), ((), ())), preferred_element_type=F32)

    return one(left[0], right[1]) + one(left[1], right[0]) + one(left[0], right[0])


def unit_inverse(ref, member):
    lower = ref[member]
    row = lax.broadcasted_iota(jnp.int32, lower.shape, 0)
    col = lax.broadcasted_iota(jnp.int32, lower.shape, 1)
    return jnp.where(row > col, lower, jnp.where(row == col, 1.0, 0.0).astype(F32))


class Plan:
    def __init__(self, front, factor, unit_lower, tile_list):
        self.rows, self.cols = lax.axis_size("row"), lax.axis_size("col")
        self.lanes = self.rows // self.cols
        self.members, self.width, _ = unit_lower.shape
        self.na = tile_list.shape[1] // self.rows
        self.tile = factor.shape[0] // self.na
        self.nb = self.na * self.lanes
        self.row_tiles = front.shape[0] // self.tile
        self.col_tiles = front.shape[1] // self.tile
        self.depth = factor.shape[0]
        bits = [1 << i for i in range((self.cols - 1).bit_length())]
        self.orders = [
            bits[lane % len(bits):] + bits[:lane % len(bits)] for lane in range(self.lanes)
        ]
        self.steps = len(bits)
        self.splits = [2] * self.members

    def device(self, chip, lane, col):
        return (chip * self.lanes + lane) * self.cols + col

    def tree(self, step):
        pairs = []
        for col in range(self.cols):
            for lane, order in enumerate(self.orders):
                held, later = [0], [0]
                for bit in order[:step]:
                    held = held + [x ^ bit for x in held]
                for bit in order[step + 1:]:
                    later = later + [x ^ bit for x in later]
                for offset in held:
                    child = col ^ offset ^ order[step]
                    if any(child ^ x > col for x in later):
                        pairs.append(
                            (self.device(col ^ offset, lane, col), self.device(child, lane, col))
                        )
        return pairs

    def swap(self, x, shift):
        pairs = []
        for row in range(self.rows):
            chip, lane = divmod(row, self.lanes)
            pairs.append((chip * self.lanes + (lane + shift) % self.lanes, row))
        return lax.ppermute(x, "row", pairs)

    def line_hops(self):
        count, half = self.cols, self.cols // 2
        inward = [[(i, i + 1), (count - 1 - i, count - 2 - i)] for i in range(half - 1)]
        outward = [
            [(half - 1 - i, half - 2 - i), (half + i, half + i + 1)] for i in range(half - 1)
        ]
        return inward + [[(half - 1, half), (half, half - 1)]] + outward

    def line_step(self, hop, x, got):
        half = self.cols // 2
        if hop < half:
            return x + got
        place, i = lax.axis_index("col"), hop - half
        return jnp.where((place == half - 2 - i) | (place == half + i + 1), got, x)

    def on_diagonal(self):
        return lax.axis_index("row") // self.lanes == lax.axis_index("col")

    def at_end(self):
        place = lax.axis_index("col")
        return (place == 0) | (place == self.cols - 1)

    def bit_pairs(self, step):
        return [
            (self.device(chip, lane, col), self.device(chip ^ order[step], lane, col))
            for chip in range(self.cols)
            for lane, order in enumerate(self.orders)
            for col in range(self.cols)
        ]

    def offset_pairs(self, offset):
        pairs = []
        for lane, order in enumerate(self.orders):
            flip = sum(
                bit for step, bit in enumerate(order) if offset >> (self.steps - 1 - step) & 1
            )
            for chip in range(self.cols):
                for col in range(self.cols):
                    pairs.append(
                        (self.device(chip, lane, col), self.device(chip ^ flip, lane, col))
                    )
        return pairs

    def place_of(self, lane):
        chip, place = lax.axis_index("row") // self.lanes, jnp.int32(0)
        for step, bit in enumerate(self.orders[lane]):
            place = jnp.where((chip & bit) != 0, place + (1 << (self.steps - 1 - step)), place)
        return place

    def bit(self, step):
        row = lax.axis_index("row")
        chip, value = row // self.lanes, jnp.int32(0)
        for lane, order in enumerate(self.orders):
            value = jnp.where((row % self.lanes == lane) & ((chip & order[step]) != 0), 1, value)
        return value


class Chain:
    def __init__(self):
        self.last = ()

    def issue(self, *requests, after=()):
        out = []
        for x, axis, pairs in requests:
            if self.last or after:
                x, _ = lax.optimization_barrier((x, self.last + tuple(after)))
            out.append(lax.ppermute(x, axis, pairs))
        self.last = tuple(out)
        return out


def gather_kernel(plan, member, tiles_ref, valid_ref, front, factor, high, low, *rest):
    mirror, (buffer, sems) = rest[:plan.lanes], rest[plan.lanes:]
    size, na, nb = plan.tile, plan.na, plan.nb
    row, col = lax.axis_index("row"), lax.axis_index("col")
    lane = lax.rem(row, plan.lanes)
    row_slots = [row * na + a for a in range(na)]
    col_slots = [
        col * nb + lax.rem(lane + b // na, plan.lanes) * na + b % na for b in range(nb)
    ]
    copies = []
    for a in range(na):
        for b in range(nb):
            i = jnp.clip(tiles_ref[member, row_slots[a]] - row * plan.row_tiles, 0, plan.row_tiles - 1)
            j = jnp.clip(tiles_ref[member, col_slots[b]] - col * plan.col_tiles, 0, plan.col_tiles - 1)
            copy = pltpu.make_async_copy(
                front.at[
                    pl.ds(pl.multiple_of(i * size, size), size),
                    pl.ds(pl.multiple_of(j * size, size), size),
                ],
                buffer.at[a, b],
                sems.at[a, b],
            )
            copy.start()
            copies.append(copy)
    right = split(factor[...])
    local_row = lax.broadcasted_iota(jnp.int32, (size, size), 0)
    local_col = lax.broadcasted_iota(jnp.int32, (size, size), 1)
    for a in range(na):
        for b in range(nb):
            copies[a * nb + b].wait()
            live = (valid_ref[member, row_slots[a]] > 0) & (valid_ref[member, col_slots[b]] > 0)
            ahead = (tiles_ref[member, row_slots[a]] - tiles_ref[member, col_slots[b]]) * size
            gap = local_row - local_col + ahead
            x = buffer[a, b]
            x = jnp.where(gap > 0, x, jnp.where(gap == 0, 0.5 * x, 0.0))
            x = jnp.where(live, x, 0.0)
            x_high, x_low = split(x)
            high[a * size:(a + 1) * size, b * size:(b + 1) * size] = x_high
            low[a * size:(a + 1) * size, b * size:(b + 1) * size] = x_low
    for b in range(nb):
        left = (high[:, b * size:(b + 1) * size], low[:, b * size:(b + 1) * size])
        first = b % na * size
        mirror[b // na][first:first + size, :] = product(left, right, contract=0)


def forward_kernel(plan, member, high, low, factor, mirror, *rest):
    lanes, size, depth = plan.lanes, plan.tile, plan.depth
    parts, rest = rest[:lanes], rest[lanes:]
    earlier, rest = rest[:lanes * bool(member)], rest[lanes * bool(member):]
    splits = plan.splits[member]
    totals, rest = rest[:splits], rest[splits:]
    cross, (total, whole) = rest[:lanes], rest[lanes:]
    right = [split(part[...]) for part in parts]
    for a in range(plan.na):
        rows = slice(a * size, (a + 1) * size)
        total[rows, :] = sum(
            product(
                (high[rows, i * depth:(i + 1) * depth], low[rows, i * depth:(i + 1) * depth]),
                right[i],
            )
            for i in range(lanes)
        )
    share = depth // splits
    on_diagonal = plan.on_diagonal()
    for i in range(splits):
        rows = slice(i * share, (i + 1) * share)
        totals[i][...] = total[rows, :] + jnp.where(on_diagonal, mirror[rows, :], 0.0)
    whole[...] = product(split(factor[...]), split(total[...]), contract=0)
    share = plan.width // lanes
    lane = lax.rem(lax.axis_index("row"), lanes)
    for i in range(lanes):
        first = pl.multiple_of(lax.rem(lane + i, lanes) * share, share)
        cross[i][member * share:, :] = whole[pl.ds(first, share), :]
        if member:
            cross[i][:member * share, :] = earlier[i][...]


def place_kernel(plan, member, tiles_ref, unit_ref, *rest):
    splits = plan.splits[member]
    sums, rest = rest[:2 * splits], rest[2 * splits:]
    out, stack, zeros, sems, zero_sems = rest[member > 0:]
    size, width = plan.tile, plan.width
    row, at_end = lax.axis_index("row"), plan.at_end()

    def zero_copies(act):
        for other in range(plan.members):
            for t in range(plan.row_tiles):
                taken = False
                for a in range(plan.na):
                    taken = taken | (
                        tiles_ref[other, row * plan.na + a] == row * plan.row_tiles + t
                    )
                copy = pltpu.make_async_copy(
                    zeros,
                    out.at[t * size:(t + 1) * size, other * width:(other + 1) * width],
                    zero_sems.at[other, t],
                )
                pl.when(jnp.logical_not(taken))(functools.partial(act, copy))

    if member == 0:
        zeros[...] = jnp.zeros_like(zeros)
        zero_copies(lambda copy: copy.start())
    right = split(unit_inverse(unit_ref, member))
    share = plan.depth // splits
    for i in range(splits):
        x = jnp.where(at_end, sums[2 * i + 1][...], sums[2 * i][...])
        stack[i * share:(i + 1) * share, :] = -product(split(x), right)
    copies = []
    for a in range(plan.na):
        t = jnp.clip(
            tiles_ref[member, row * plan.na + a] - row * plan.row_tiles, 0, plan.row_tiles - 1
        )
        copy = pltpu.make_async_copy(
            stack.at[a * size:(a + 1) * size, :],
            out.at[
                pl.ds(pl.multiple_of(t * size, size), size), member * width:(member + 1) * width
            ],
            sems.at[a],
        )
        copy.start()
        copies.append(copy)
    for copy in copies:
        copy.wait()
    if member == 0:
        zero_copies(lambda copy: copy.wait())


def diagonal_kernel(plan, pivot, unit_ref, *rest):
    parts, (out, cross) = rest[:plan.lanes], rest[plan.lanes:]
    width, lanes, members = plan.width, plan.lanes, plan.members
    lane = lax.rem(lax.axis_index("row"), lanes)
    count = 1 << plan.steps
    size = members * width // (lanes * count)
    for other in range(lanes):
        mine = plan.place_of(other)
        for place in range(count):
            first = pl.multiple_of((mine ^ place) * size, size)
            piece = parts[0][pl.ds(first, size), :]
            for i in range(1, lanes):
                piece = jnp.where(
                    lax.rem(lane + i, lanes) == other, parts[i][pl.ds(first, size), :], piece
                )
            cross[other, place * size:(place + 1) * size, :] = piece
    share = width // lanes
    row = lax.broadcasted_iota(jnp.int32, (width, width), 0)
    col = lax.broadcasted_iota(jnp.int32, (width, width), 1)
    for member in range(members):
        rows = slice(member * share, (member + 1) * share)
        x = jnp.concatenate([cross[other, rows, :] for other in range(lanes)])
        x = jnp.where(row == col, pivot[member:member + 1, :], 0.0) + x + x.T
        inverse = split(unit_inverse(unit_ref, member))
        half = product(split(x), inverse)
        out[member] = product(inverse, split(half), contract=0)


def reverse(pairs):
    return [(receiver, sender) for sender, receiver in pairs]


def shards(inverse_front, factor, unit_lower, pivot_inverse, tile_list, tile_valid):
    plan = Plan(inverse_front, factor, unit_lower, tile_list)
    width, depth, lanes, members, steps = plan.width, plan.depth, plan.lanes, plan.members, plan.steps
    both = ("row", "col")
    factors = [factor[:, member * width:(member + 1) * width] for member in range(members)]

    def lane_sum(parts):
        out = parts[0]
        for shift in range(1, lanes):
            out = out + plan.swap(parts[lanes - shift], shift)
        return out

    def gather(member):
        return pl.pallas_call(
            functools.partial(gather_kernel, plan, member),
            in_specs=smem(2) + [pl.BlockSpec(memory_space=pl.ANY)] + vmem(1),
            out_specs=vmem(2 + lanes),
            out_shape=[jax.ShapeDtypeStruct((depth, depth * lanes), BF16)] * 2
            + [jax.ShapeDtypeStruct((depth, width), F32)] * lanes,
            scratch_shapes=[
                pltpu.VMEM((plan.na, plan.nb, plan.tile, plan.tile), F32),
                pltpu.SemaphoreType.DMA((plan.na, plan.nb)),
            ],
            compiler_params=PARAMS,
            cost_estimate=COST,
            name="gather_mirror",
        )(tile_list, tile_valid, inverse_front, factors[member])

    def forward(member, high, low, mirror, held, earlier):
        parts = [held] + [plan.swap(held, shift) for shift in range(1, lanes)]
        splits = plan.splits[member]
        outs = pl.pallas_call(
            functools.partial(forward_kernel, plan, member),
            in_specs=vmem(4 + lanes + len(earlier)),
            out_specs=vmem(splits + lanes),
            out_shape=[jax.ShapeDtypeStruct((depth // splits, width), F32)] * splits
            + [jax.ShapeDtypeStruct(((member + 1) * width // lanes, width), F32)] * lanes,
            scratch_shapes=[
                pltpu.VMEM((depth, width), F32),
                pltpu.VMEM((width, width), F32),
            ],
            compiler_params=PARAMS,
            cost_estimate=COST,
            name="forward",
        )(high, low, factors[member], mirror, *parts, *earlier)
        return outs[:splits], outs[splits:]

    hops = plan.line_hops()

    def enter(x, after=()):
        if after:
            x, _ = lax.optimization_barrier((x, tuple(after)))
        return lax.ppermute(x, "col", hops[0])

    def run(x, got, ties=(), second=None):
        sent, brought = [], [got]
        for hop in range(1, len(hops)):
            x = plan.line_step(hop - 1, x, got)
            sent.append(x)
            tie = ties[hop - 1] if hop <= len(ties) else ()
            y = lax.optimization_barrier((x, tuple(tie)))[0] if tie else x
            if hop == 1 and second is not None:
                got = second
            else:
                got = lax.ppermute(y, "col", hops[hop])
            brought.append(got)
        if len(hops) == 1:
            got = x = x + got
        return x, got, sent, brought

    spread, collect = Chain(), Chain()
    count = members * steps
    tiles, held, mirror, chunks, entered = {}, {}, {}, [], {}
    after, cross, second = (), [], None
    for phase in range(count + 1):
        if phase < count:
            out, step = divmod(phase, steps)
            x = factors[out] if step == 0 else held[out]
            got_out, = spread.issue((x, both, plan.tree(step)), after=after)
        if phase:
            back, turn = divmod(phase - 1, steps)
            got_back, = collect.issue(
                (mirror[back], both, reverse(plan.tree(steps - 1 - turn))), after=after
            )
        if chunks and 0 not in entered:
            entered[0] = enter(chunks[0])
            entered[0], got_out, got_back = lax.optimization_barrier(
                (entered[0], got_out, got_back)
            )
            if len(hops) > 1 and len(chunks) > 1:
                second = lax.ppermute(plan.line_step(0, chunks[0], entered[0]), "col", hops[1])
                entered[1] = enter(chunks[1], (entered[0],))
        after = ()
        if phase % steps == 0 and phase < count:
            high, low, *parts = gather(out) if out == 0 else tiles[out]
            tiles[out] = (high, low)
            mirror[out] = lane_sum(parts)
        if phase % steps == 1 % steps and phase < count and out + 1 < members:
            tiles[out + 1] = gather(out + 1)
            after = (tiles[out + 1][0],)
        if phase < count:
            held[out] = jnp.where(plan.on_diagonal(), x, got_out) if step == 0 else x + got_out
        if phase:
            if turn < steps - 1:
                mirror[back] = mirror[back] + got_back
            else:
                x = mirror[back]
                if second is not None and len(chunks) == plan.splits[0]:
                    x, second, entered[1] = lax.optimization_barrier((x, second, entered[1]))
                sums, cross = forward(back, *tiles[back], x, held[back], cross)
                share = sums[0].shape[0]
                after = tuple(
                    part + got_back[i * share:(i + 1) * share] for i, part in enumerate(sums)
                )
                chunks += after

    x, _ = lax.optimization_barrier((lane_sum(cross), after))
    for step in range(steps):
        x = x.reshape(2, x.shape[0] // 2, x.shape[1])
        bit = plan.bit(step)
        send = lax.dynamic_index_in_dim(x, 1 - bit, 0, keepdims=False)
        keep = lax.dynamic_index_in_dim(x, bit, 0, keepdims=False)
        x = keep + lax.ppermute(send, both, plan.bit_pairs(step))
    update = x

    def place(member, column):
        sums, splits = [], plan.splits[member]
        first = sum(plan.splits[:member])
        for i in range(first, first + splits):
            sums += [chunks[i], ends[i]]
        return pl.pallas_call(
            functools.partial(place_kernel, plan, member),
            in_specs=smem(1) + vmem(1 + 2 * splits)
            + [pl.BlockSpec(memory_space=pl.ANY)] * (member > 0),
            out_specs=pl.BlockSpec(memory_space=pl.ANY),
            out_shape=jax.ShapeDtypeStruct((inverse_front.shape[0], factor.shape[1]), F32),
            scratch_shapes=[
                pltpu.VMEM((depth, width), F32),
                pltpu.VMEM((plan.tile, width), F32),
                pltpu.SemaphoreType.DMA((plan.na,)),
                pltpu.SemaphoreType.DMA((members, plan.row_tiles)),
            ],
            input_output_aliases={2 + 2 * splits: 0} if member else {},
            compiler_params=PARAMS,
            cost_estimate=COST,
            name="place",
        )(tile_list, unit_lower, *sums, *([column] if member else []))

    ends, sent, brought, column = {}, {}, {}, None
    last, middle = len(chunks) - 1, len(hops) - 1
    for i in range(last + 1):
        if i > 2:
            entered[i] = enter(chunks[i], (brought[i - 2][min(1, middle)],))
        if i == 1 and last > 1:
            entered[2] = enter(chunks[2])
        ties = [()] * middle
        if i < 2 and i < last and middle:
            if 1 not in entered:
                entered[1] = enter(chunks[1], (entered[0],))
            ties[-1] = (entered[i + 1],)
        elif i > 1 and middle:
            ties = [(brought[i - 2][hop + 1],) for hop in range(1, middle)]
            ties.append((brought[i - 1][-1],))
        chunks[i], ends[i], sent[i], brought[i] = run(
            chunks[i], entered[i], ties, second if i == 0 else None
        )
    update, got, _, _ = run(update, enter(update), [(x,) for x in sent[last]])
    for member in range(members):
        column = place(member, column)
        if member == 0:
            got, _ = lax.optimization_barrier((got, column))

    x = update
    x = jnp.where(plan.at_end(), got, x)
    pieces = [x] + [lax.ppermute(x, both, plan.offset_pairs(r)) for r in range(1, 1 << steps)]
    x, _ = lax.optimization_barrier((jnp.concatenate(pieces), column))
    parts = [x] + [plan.swap(x, shift) for shift in range(1, lanes)]
    diagonal = pl.pallas_call(
        functools.partial(diagonal_kernel, plan),
        in_specs=vmem(2 + lanes),
        out_specs=vmem(1)[0],
        out_shape=jax.ShapeDtypeStruct(unit_lower.shape, F32),
        scratch_shapes=[pltpu.VMEM((lanes, members * width // lanes, width), F32)],
        compiler_params=PARAMS,
        cost_estimate=COST,
        name="diagonal",
    )(pivot_inverse, unit_lower, *parts)
    return (column, diagonal)


def solution(mesh):
    in_specs = (P("row", "col"), P("row", None), P(), P(), P(), P())
    out_specs = (P("row", None), P())
    return jax.shard_map(shards, mesh=mesh, in_specs=in_specs, out_specs=out_specs, check_vma=False)
```

```python
import functools

import jax
import jax.numpy as jnp
from jax import lax
from jax.experimental import pallas as pl
from jax.experimental.pallas import tpu as pltpu
from jax.sharding import PartitionSpec as P

F32 = jnp.float32
BF16 = jnp.bfloat16
VMEM = pltpu.MemorySpace.VMEM
SMEM = pltpu.MemorySpace.SMEM
COST = pl.CostEstimate(flops=1600 << 20, bytes_accessed=8 << 20, transcendentals=0)
PARAMS = pltpu.CompilerParams(vmem_limit_bytes=48 * 1024 * 1024)


def vmem(count):
    return [pl.BlockSpec(memory_space=VMEM)] * count


def smem(count):
    return [pl.BlockSpec(memory_space=SMEM)] * count


def split(x):
    high = x.astype(BF16)
    return high, (x - high.astype(F32)).astype(BF16)


def product(left, right, contract=1):
    def one(a, b):
        return lax.dot_general(a, b, (((contract,), (0,)), ((), ())), preferred_element_type=F32)

    return one(left[0], right[1]) + one(left[1], right[0]) + one(left[0], right[0])


def unit_inverse(ref, member):
    lower = ref[member]
    row = lax.broadcasted_iota(jnp.int32, lower.shape, 0)
    col = lax.broadcasted_iota(jnp.int32, lower.shape, 1)
    return jnp.where(row > col, lower, jnp.where(row == col, 1.0, 0.0).astype(F32))


class Plan:
    def __init__(self, front, factor, unit_lower, tile_list):
        self.rows, self.cols = lax.axis_size("row"), lax.axis_size("col")
        self.lanes = self.rows // self.cols
        self.members, self.width, _ = unit_lower.shape
        self.na = tile_list.shape[1] // self.rows
        self.tile = factor.shape[0] // self.na
        self.nb = self.na * self.lanes
        self.row_tiles = front.shape[0] // self.tile
        self.col_tiles = front.shape[1] // self.tile
        self.depth = factor.shape[0]
        bits = [1 << i for i in range((self.cols - 1).bit_length())]
        self.orders = [
            bits[lane % len(bits):] + bits[:lane % len(bits)] for lane in range(self.lanes)
        ]
        self.steps = len(bits)
        self.splits = [2] * self.members

    def device(self, chip, lane, col):
        return (chip * self.lanes + lane) * self.cols + col

    def tree(self, step):
        pairs = []
        for col in range(self.cols):
            for lane, order in enumerate(self.orders):
                held, later = [0], [0]
                for bit in order[:step]:
                    held = held + [x ^ bit for x in held]
                for bit in order[step + 1:]:
                    later = later + [x ^ bit for x in later]
                for offset in held:
                    child = col ^ offset ^ order[step]
                    if any(child ^ x > col for x in later):
                        pairs.append(
                            (self.device(col ^ offset, lane, col), self.device(child, lane, col))
                        )
        return pairs

    def swap(self, x, shift):
        pairs = []
        for row in range(self.rows):
            chip, lane = divmod(row, self.lanes)
            pairs.append((chip * self.lanes + (lane + shift) % self.lanes, row))
        return lax.ppermute(x, "row", pairs)

    def line_hops(self):
        count, half = self.cols, self.cols // 2
        inward = [[(i, i + 1), (count - 1 - i, count - 2 - i)] for i in range(half - 1)]
        outward = [
            [(half - 1 - i, half - 2 - i), (half + i, half + i + 1)] for i in range(half - 1)
        ]
        return inward + [[(half - 1, half), (half, half - 1)]] + outward

    def line_step(self, hop, x, got):
        half = self.cols // 2
        if hop < half:
            return x + got
        place, i = lax.axis_index("col"), hop - half
        return jnp.where((place == half - 2 - i) | (place == half + i + 1), got, x)

    def on_diagonal(self):
        return lax.axis_index("row") // self.lanes == lax.axis_index("col")

    def at_end(self):
        place = lax.axis_index("col")
        return (place == 0) | (place == self.cols - 1)

    def bit_pairs(self, step):
        return [
            (self.device(chip, lane, col), self.device(chip ^ order[step], lane, col))
            for chip in range(self.cols)
            for lane, order in enumerate(self.orders)
            for col in range(self.cols)
        ]

    def offset_pairs(self, offset):
        pairs = []
        for lane, order in enumerate(self.orders):
            flip = sum(
                bit for step, bit in enumerate(order) if offset >> (self.steps - 1 - step) & 1
            )
            for chip in range(self.cols):
                for col in range(self.cols):
                    pairs.append(
                        (self.device(chip, lane, col), self.device(chip ^ flip, lane, col))
                    )
        return pairs

    def place_of(self, lane):
        chip, place = lax.axis_index("row") // self.lanes, jnp.int32(0)
        for step, bit in enumerate(self.orders[lane]):
            place = jnp.where((chip & bit) != 0, place + (1 << (self.steps - 1 - step)), place)
        return place

    def bit(self, step):
        row = lax.axis_index("row")
        chip, value = row // self.lanes, jnp.int32(0)
        for lane, order in enumerate(self.orders):
            value = jnp.where((row % self.lanes == lane) & ((chip & order[step]) != 0), 1, value)
        return value


class Chain:
    def __init__(self):
        self.last = ()

    def issue(self, *requests, after=()):
        out = []
        for x, axis, pairs in requests:
            if self.last or after:
                x, _ = lax.optimization_barrier((x, self.last + tuple(after)))
            out.append(lax.ppermute(x, axis, pairs))
        self.last = tuple(out)
        return out


def gather_kernel(plan, member, tiles_ref, valid_ref, front, factor, high, low, *rest):
    mirror, (buffer, sems) = rest[:plan.lanes], rest[plan.lanes:]
    size, na, nb = plan.tile, plan.na, plan.nb
    row, col = lax.axis_index("row"), lax.axis_index("col")
    lane = lax.rem(row, plan.lanes)
    row_slots = [row * na + a for a in range(na)]
    col_slots = [
        col * nb + lax.rem(lane + b // na, plan.lanes) * na + b % na for b in range(nb)
    ]
    copies = []
    for a in range(na):
        for b in range(nb):
            i = jnp.clip(tiles_ref[member, row_slots[a]] - row * plan.row_tiles, 0, plan.row_tiles - 1)
            j = jnp.clip(tiles_ref[member, col_slots[b]] - col * plan.col_tiles, 0, plan.col_tiles - 1)
            copy = pltpu.make_async_copy(
                front.at[
                    pl.ds(pl.multiple_of(i * size, size), size),
                    pl.ds(pl.multiple_of(j * size, size), size),
                ],
                buffer.at[a, b],
                sems.at[a, b],
            )
            copy.start()
            copies.append(copy)
    right = split(factor[...])
    local_row = lax.broadcasted_iota(jnp.int32, (size, size), 0)
    local_col = lax.broadcasted_iota(jnp.int32, (size, size), 1)
    for a in range(na):
        for b in range(nb):
            copies[a * nb + b].wait()
            live = (valid_ref[member, row_slots[a]] > 0) & (valid_ref[member, col_slots[b]] > 0)
            ahead = (tiles_ref[member, row_slots[a]] - tiles_ref[member, col_slots[b]]) * size
            gap = local_row - local_col + ahead
            x = buffer[a, b]
            x = jnp.where(gap > 0, x, jnp.where(gap == 0, 0.5 * x, 0.0))
            x = jnp.where(live, x, 0.0)
            x_high, x_low = split(x)
            high[a * size:(a + 1) * size, b * size:(b + 1) * size] = x_high
            low[a * size:(a + 1) * size, b * size:(b + 1) * size] = x_low
    for b in range(nb):
        left = (high[:, b * size:(b + 1) * size], low[:, b * size:(b + 1) * size])
        first = b % na * size
        mirror[b // na][first:first + size, :] = product(left, right, contract=0)


def forward_kernel(plan, member, high, low, factor, mirror, *rest):
    lanes, size, depth = plan.lanes, plan.tile, plan.depth
    parts, rest = rest[:lanes], rest[lanes:]
    earlier, rest = rest[:lanes * bool(member)], rest[lanes * bool(member):]
    splits = plan.splits[member]
    totals, rest = rest[:splits], rest[splits:]
    cross, (total, whole) = rest[:lanes], rest[lanes:]
    right = [split(part[...]) for part in parts]
    for a in range(plan.na):
        rows = slice(a * size, (a + 1) * size)
        total[rows, :] = sum(
            product(
                (high[rows, i * depth:(i + 1) * depth], low[rows, i * depth:(i + 1) * depth]),
                right[i],
            )
            for i in range(lanes)
        )
    share = depth // splits
    on_diagonal = plan.on_diagonal()
    for i in range(splits):
        rows = slice(i * share, (i + 1) * share)
        totals[i][...] = total[rows, :] + jnp.where(on_diagonal, mirror[rows, :], 0.0)
    whole[...] = product(split(factor[...]), split(total[...]), contract=0)
    share = plan.width // lanes
    lane = lax.rem(lax.axis_index("row"), lanes)
    for i in range(lanes):
        first = pl.multiple_of(lax.rem(lane + i, lanes) * share, share)
        cross[i][member * share:, :] = whole[pl.ds(first, share), :]
        if member:
            cross[i][:member * share, :] = earlier[i][...]


def place_kernel(plan, member, tiles_ref, unit_ref, *rest):
    splits = plan.splits[member]
    sums, rest = rest[:2 * splits], rest[2 * splits:]
    out, stack, zeros, sems, zero_sems = rest[member > 0:]
    size, width = plan.tile, plan.width
    row, at_end = lax.axis_index("row"), plan.at_end()

    def zero_copies(act):
        for other in range(plan.members):
            for t in range(plan.row_tiles):
                taken = False
                for a in range(plan.na):
                    taken = taken | (
                        tiles_ref[other, row * plan.na + a] == row * plan.row_tiles + t
                    )
                copy = pltpu.make_async_copy(
                    zeros,
                    out.at[t * size:(t + 1) * size, other * width:(other + 1) * width],
                    zero_sems.at[other, t],
                )
                pl.when(jnp.logical_not(taken))(functools.partial(act, copy))

    if member == 0:
        zeros[...] = jnp.zeros_like(zeros)
        zero_copies(lambda copy: copy.start())
    right = split(unit_inverse(unit_ref, member))
    share = plan.depth // splits
    for i in range(splits):
        x = jnp.where(at_end, sums[2 * i + 1][...], sums[2 * i][...])
        stack[i * share:(i + 1) * share, :] = -product(split(x), right)
    copies = []
    for a in range(plan.na):
        t = jnp.clip(
            tiles_ref[member, row * plan.na + a] - row * plan.row_tiles, 0, plan.row_tiles - 1
        )
        copy = pltpu.make_async_copy(
            stack.at[a * size:(a + 1) * size, :],
            out.at[
                pl.ds(pl.multiple_of(t * size, size), size), member * width:(member + 1) * width
            ],
            sems.at[a],
        )
        copy.start()
        copies.append(copy)
    for copy in copies:
        copy.wait()
    if member == 0:
        zero_copies(lambda copy: copy.wait())


def diagonal_kernel(plan, pivot, unit_ref, *rest):
    parts, (out, cross) = rest[:plan.lanes], rest[plan.lanes:]
    width, lanes, members = plan.width, plan.lanes, plan.members
    lane = lax.rem(lax.axis_index("row"), lanes)
    count = 1 << plan.steps
    size = members * width // (lanes * count)
    for other in range(lanes):
        mine = plan.place_of(other)
        for place in range(count):
            first = pl.multiple_of((mine ^ place) * size, size)
            piece = parts[0][pl.ds(first, size), :]
            for i in range(1, lanes):
                piece = jnp.where(
                    lax.rem(lane + i, lanes) == other, parts[i][pl.ds(first, size), :], piece
                )
            cross[other, place * size:(place + 1) * size, :] = piece
    share = width // lanes
    row = lax.broadcasted_iota(jnp.int32, (width, width), 0)
    col = lax.broadcasted_iota(jnp.int32, (width, width), 1)
    for member in range(members):
        rows = slice(member * share, (member + 1) * share)
        x = jnp.concatenate([cross[other, rows, :] for other in range(lanes)])
        x = jnp.where(row == col, pivot[member:member + 1, :], 0.0) + x + x.T
        inverse = split(unit_inverse(unit_ref, member))
        half = product(split(x), inverse)
        out[member] = product(inverse, split(half), contract=0)


def reverse(pairs):
    return [(receiver, sender) for sender, receiver in pairs]


def shards(inverse_front, factor, unit_lower, pivot_inverse, tile_list, tile_valid):
    plan = Plan(inverse_front, factor, unit_lower, tile_list)
    width, depth, lanes, members, steps = plan.width, plan.depth, plan.lanes, plan.members, plan.steps
    both = ("row", "col")
    factors = [factor[:, member * width:(member + 1) * width] for member in range(members)]

    def lane_sum(parts):
        out = parts[0]
        for shift in range(1, lanes):
            out = out + plan.swap(parts[lanes - shift], shift)
        return out

    def gather(member):
        return pl.pallas_call(
            functools.partial(gather_kernel, plan, member),
            in_specs=smem(2) + [pl.BlockSpec(memory_space=pl.ANY)] + vmem(1),
            out_specs=vmem(2 + lanes),
            out_shape=[jax.ShapeDtypeStruct((depth, depth * lanes), BF16)] * 2
            + [jax.ShapeDtypeStruct((depth, width), F32)] * lanes,
            scratch_shapes=[
                pltpu.VMEM((plan.na, plan.nb, plan.tile, plan.tile), F32),
                pltpu.SemaphoreType.DMA((plan.na, plan.nb)),
            ],
            compiler_params=PARAMS,
            cost_estimate=COST,
            name="gather_mirror",
        )(tile_list, tile_valid, inverse_front, factors[member])

    def forward(member, high, low, mirror, held, earlier):
        parts = [held] + [plan.swap(held, shift) for shift in range(1, lanes)]
        splits = plan.splits[member]
        outs = pl.pallas_call(
            functools.partial(forward_kernel, plan, member),
            in_specs=vmem(4 + lanes + len(earlier)),
            out_specs=vmem(splits + lanes),
            out_shape=[jax.ShapeDtypeStruct((depth // splits, width), F32)] * splits
            + [jax.ShapeDtypeStruct(((member + 1) * width // lanes, width), F32)] * lanes,
            scratch_shapes=[
                pltpu.VMEM((depth, width), F32),
                pltpu.VMEM((width, width), F32),
            ],
            compiler_params=PARAMS,
            cost_estimate=COST,
            name="forward",
        )(high, low, factors[member], mirror, *parts, *earlier)
        return outs[:splits], outs[splits:]

    hops = plan.line_hops()

    def enter(x, after=()):
        if after:
            x, _ = lax.optimization_barrier((x, tuple(after)))
        return lax.ppermute(x, "col", hops[0])

    def run(x, got, ties=(), second=None):
        sent, brought = [], [got]
        for hop in range(1, len(hops)):
            x = plan.line_step(hop - 1, x, got)
            sent.append(x)
            tie = ties[hop - 1] if hop <= len(ties) else ()
            y = lax.optimization_barrier((x, tuple(tie)))[0] if tie else x
            if hop == 1 and second is not None:
                got = second
            else:
                got = lax.ppermute(y, "col", hops[hop])
            brought.append(got)
        if len(hops) == 1:
            got = x = x + got
        return x, got, sent, brought

    spread, collect = Chain(), Chain()
    count = members * steps
    tiles, held, mirror, chunks, entered = {}, {}, {}, [], {}
    after, cross, second = (), [], None
    for phase in range(count + 1):
        if phase < count:
            out, step = divmod(phase, steps)
            x = factors[out] if step == 0 else held[out]
            got_out, = spread.issue((x, both, plan.tree(step)), after=after)
        if phase:
            back, turn = divmod(phase - 1, steps)
            got_back, = collect.issue(
                (mirror[back], both, reverse(plan.tree(steps - 1 - turn))), after=after
            )
        if chunks and 0 not in entered:
            entered[0] = enter(chunks[0])
            entered[0], got_out, got_back = lax.optimization_barrier(
                (entered[0], got_out, got_back)
            )
            if len(hops) > 1 and len(chunks) > 1:
                second = lax.ppermute(plan.line_step(0, chunks[0], entered[0]), "col", hops[1])
                entered[1] = enter(chunks[1], (entered[0],))
        after = ()
        if phase % steps == 0 and phase < count:
            high, low, *parts = gather(out) if out == 0 else tiles[out]
            tiles[out] = (high, low)
            mirror[out] = lane_sum(parts)
        if phase % steps == 1 % steps and phase < count and out + 1 < members:
            tiles[out + 1] = gather(out + 1)
            after = (tiles[out + 1][0],)
        if phase < count:
            held[out] = jnp.where(plan.on_diagonal(), x, got_out) if step == 0 else x + got_out
        if phase:
            if turn < steps - 1:
                mirror[back] = mirror[back] + got_back
            else:
                x = mirror[back]
                if second is not None and len(chunks) == plan.splits[0]:
                    x, second, entered[1] = lax.optimization_barrier((x, second, entered[1]))
                sums, cross = forward(back, *tiles[back], x, held[back], cross)
                share = sums[0].shape[0]
                after = tuple(
                    part + got_back[i * share:(i + 1) * share] for i, part in enumerate(sums)
                )
                chunks += after

    x, _ = lax.optimization_barrier((lane_sum(cross), after))
    for step in range(steps):
        x = x.reshape(2, x.shape[0] // 2, x.shape[1])
        bit = plan.bit(step)
        send = lax.dynamic_index_in_dim(x, 1 - bit, 0, keepdims=False)
        keep = lax.dynamic_index_in_dim(x, bit, 0, keepdims=False)
        x = keep + lax.ppermute(send, both, plan.bit_pairs(step))
    update = x

    def place(member, column):
        sums, splits = [], plan.splits[member]
        first = sum(plan.splits[:member])
        for i in range(first, first + splits):
            sums += [chunks[i], ends[i]]
        return pl.pallas_call(
            functools.partial(place_kernel, plan, member),
            in_specs=smem(1) + vmem(1 + 2 * splits)
            + [pl.BlockSpec(memory_space=pl.ANY)] * (member > 0),
            out_specs=pl.BlockSpec(memory_space=pl.ANY),
            out_shape=jax.ShapeDtypeStruct((inverse_front.shape[0], factor.shape[1]), F32),
            scratch_shapes=[
                pltpu.VMEM((depth, width), F32),
                pltpu.VMEM((plan.tile, width), F32),
                pltpu.SemaphoreType.DMA((plan.na,)),
                pltpu.SemaphoreType.DMA((members, plan.row_tiles)),
            ],
            input_output_aliases={2 + 2 * splits: 0} if member else {},
            compiler_params=PARAMS,
            cost_estimate=COST,
            name="place",
        )(tile_list, unit_lower, *sums, *([column] if member else []))

    ends, sent, brought, column = {}, {}, {}, None
    last, middle = len(chunks) - 1, len(hops) - 1
    for i in range(last + 1):
        if i > 2:
            entered[i] = enter(chunks[i], (brought[i - 2][min(1, middle)],))
        if i == 1 and last > 1:
            entered[2] = enter(chunks[2], (ends[0],))
        ties = [()] * middle
        if i < 2 and i < last and middle:
            if 1 not in entered:
                entered[1] = enter(chunks[1], (entered[0],))
            ties[-1] = (entered[i + 1],)
        elif i > 1 and middle:
            ties = [
                (brought[i - 2][hop + 1],) if i > 2 else () for hop in range(1, middle)
            ]
            ties.append((brought[i - 1][-1],))
        chunks[i], ends[i], sent[i], brought[i] = run(
            chunks[i], entered[i], ties, second if i == 0 else None
        )
    column = place(0, column)
    ties = [(x,) for x in sent[last]]
    if middle:
        ties[-1] += (column,)
    update, got, _, _ = run(update, enter(update), ties)
    for member in range(1, members):
        column = place(member, column)

    x = update
    x = jnp.where(plan.at_end(), got, x)
    pieces = [x] + [lax.ppermute(x, both, plan.offset_pairs(r)) for r in range(1, 1 << steps)]
    x, _ = lax.optimization_barrier((jnp.concatenate(pieces), column))
    parts = [x] + [plan.swap(x, shift) for shift in range(1, lanes)]
    diagonal = pl.pallas_call(
        functools.partial(diagonal_kernel, plan),
        in_specs=vmem(2 + lanes),
        out_specs=vmem(1)[0],
        out_shape=jax.ShapeDtypeStruct(unit_lower.shape, F32),
        scratch_shapes=[pltpu.VMEM((lanes, members * width // lanes, width), F32)],
        compiler_params=PARAMS,
        cost_estimate=COST,
        name="diagonal",
    )(pivot_inverse, unit_lower, *parts)
    return (column, diagonal)


def solution(mesh):
    in_specs = (P("row", "col"), P("row", None), P(), P(), P(), P())
    out_specs = (P("row", None), P())
    return jax.shard_map(shards, mesh=mesh, in_specs=in_specs, out_specs=out_specs, check_vma=False)
```

```python
import functools

import jax
import jax.numpy as jnp
from jax import lax
from jax.experimental import pallas as pl
from jax.experimental.pallas import tpu as pltpu
from jax.sharding import PartitionSpec as P

F32 = jnp.float32
BF16 = jnp.bfloat16
VMEM = pltpu.MemorySpace.VMEM
SMEM = pltpu.MemorySpace.SMEM
COST = pl.CostEstimate(flops=1600 << 20, bytes_accessed=8 << 20, transcendentals=0)
PARAMS = pltpu.CompilerParams(vmem_limit_bytes=48 * 1024 * 1024)


def vmem(count):
    return [pl.BlockSpec(memory_space=VMEM)] * count


def smem(count):
    return [pl.BlockSpec(memory_space=SMEM)] * count


def split(x):
    high = x.astype(BF16)
    return high, (x - high.astype(F32)).astype(BF16)


def product(left, right, contract=1):
    def one(a, b):
        return lax.dot_general(a, b, (((contract,), (0,)), ((), ())), preferred_element_type=F32)

    return one(left[0], right[1]) + one(left[1], right[0]) + one(left[0], right[0])


def unit_inverse(ref, member):
    lower = ref[member]
    row = lax.broadcasted_iota(jnp.int32, lower.shape, 0)
    col = lax.broadcasted_iota(jnp.int32, lower.shape, 1)
    return jnp.where(row > col, lower, jnp.where(row == col, 1.0, 0.0).astype(F32))


class Plan:
    def __init__(self, front, factor, unit_lower, tile_list):
        self.rows, self.cols = lax.axis_size("row"), lax.axis_size("col")
        self.lanes = self.rows // self.cols
        self.members, self.width, _ = unit_lower.shape
        self.na = tile_list.shape[1] // self.rows
        self.tile = factor.shape[0] // self.na
        self.nb = self.na * self.lanes
        self.row_tiles = front.shape[0] // self.tile
        self.col_tiles = front.shape[1] // self.tile
        self.depth = factor.shape[0]
        bits = [1 << i for i in range((self.cols - 1).bit_length())]
        self.orders = [
            bits[lane % len(bits):] + bits[:lane % len(bits)] for lane in range(self.lanes)
        ]
        self.steps = len(bits)
        self.splits = [2] * self.members

    def device(self, chip, lane, col):
        return (chip * self.lanes + lane) * self.cols + col

    def tree(self, step):
        pairs = []
        for col in range(self.cols):
            for lane, order in enumerate(self.orders):
                held, later = [0], [0]
                for bit in order[:step]:
                    held = held + [x ^ bit for x in held]
                for bit in order[step + 1:]:
                    later = later + [x ^ bit for x in later]
                for offset in held:
                    child = col ^ offset ^ order[step]
                    if any(child ^ x > col for x in later):
                        pairs.append(
                            (self.device(col ^ offset, lane, col), self.device(child, lane, col))
                        )
        return pairs

    def swap(self, x, shift):
        pairs = []
        for row in range(self.rows):
            chip, lane = divmod(row, self.lanes)
            pairs.append((chip * self.lanes + (lane + shift) % self.lanes, row))
        return lax.ppermute(x, "row", pairs)

    def line_hops(self):
        count, half = self.cols, self.cols // 2
        inward = [[(i, i + 1), (count - 1 - i, count - 2 - i)] for i in range(half - 1)]
        outward = [
            [(half - 1 - i, half - 2 - i), (half + i, half + i + 1)] for i in range(half - 1)
        ]
        return inward + [[(half - 1, half), (half, half - 1)]] + outward

    def line_step(self, hop, x, got):
        half = self.cols // 2
        if hop < half:
            return x + got
        place, i = lax.axis_index("col"), hop - half
        return jnp.where((place == half - 2 - i) | (place == half + i + 1), got, x)

    def on_diagonal(self):
        return lax.axis_index("row") // self.lanes == lax.axis_index("col")

    def at_end(self):
        place = lax.axis_index("col")
        return (place == 0) | (place == self.cols - 1)

    def bit_pairs(self, step):
        return [
            (self.device(chip, lane, col), self.device(chip ^ order[step], lane, col))
            for chip in range(self.cols)
            for lane, order in enumerate(self.orders)
            for col in range(self.cols)
        ]

    def offset_pairs(self, offset):
        pairs = []
        for lane, order in enumerate(self.orders):
            flip = sum(
                bit for step, bit in enumerate(order) if offset >> (self.steps - 1 - step) & 1
            )
            for chip in range(self.cols):
                for col in range(self.cols):
                    pairs.append(
                        (self.device(chip, lane, col), self.device(chip ^ flip, lane, col))
                    )
        return pairs

    def place_of(self, lane):
        chip, place = lax.axis_index("row") // self.lanes, jnp.int32(0)
        for step, bit in enumerate(self.orders[lane]):
            place = jnp.where((chip & bit) != 0, place + (1 << (self.steps - 1 - step)), place)
        return place

    def bit(self, step):
        row = lax.axis_index("row")
        chip, value = row // self.lanes, jnp.int32(0)
        for lane, order in enumerate(self.orders):
            value = jnp.where((row % self.lanes == lane) & ((chip & order[step]) != 0), 1, value)
        return value


class Chain:
    def __init__(self):
        self.last = ()

    def issue(self, *requests, after=()):
        out = []
        for x, axis, pairs in requests:
            if self.last or after:
                x, _ = lax.optimization_barrier((x, self.last + tuple(after)))
            out.append(lax.ppermute(x, axis, pairs))
        self.last = tuple(out)
        return out


def gather_kernel(plan, member, tiles_ref, valid_ref, front, factor, high, low, *rest):
    mirror, (buffer, sems) = rest[:plan.lanes], rest[plan.lanes:]
    size, na, nb = plan.tile, plan.na, plan.nb
    row, col = lax.axis_index("row"), lax.axis_index("col")
    lane = lax.rem(row, plan.lanes)
    row_slots = [row * na + a for a in range(na)]
    col_slots = [
        col * nb + lax.rem(lane + b // na, plan.lanes) * na + b % na for b in range(nb)
    ]
    copies = []
    for a in range(na):
        for b in range(nb):
            i = jnp.clip(tiles_ref[member, row_slots[a]] - row * plan.row_tiles, 0, plan.row_tiles - 1)
            j = jnp.clip(tiles_ref[member, col_slots[b]] - col * plan.col_tiles, 0, plan.col_tiles - 1)
            copy = pltpu.make_async_copy(
                front.at[
                    pl.ds(pl.multiple_of(i * size, size), size),
                    pl.ds(pl.multiple_of(j * size, size), size),
                ],
                buffer.at[a, b],
                sems.at[a, b],
            )
            copy.start()
            copies.append(copy)
    right = split(factor[...])
    local_row = lax.broadcasted_iota(jnp.int32, (size, size), 0)
    local_col = lax.broadcasted_iota(jnp.int32, (size, size), 1)
    for a in range(na):
        for b in range(nb):
            copies[a * nb + b].wait()
            live = (valid_ref[member, row_slots[a]] > 0) & (valid_ref[member, col_slots[b]] > 0)
            ahead = (tiles_ref[member, row_slots[a]] - tiles_ref[member, col_slots[b]]) * size
            gap = local_row - local_col + ahead
            x = buffer[a, b]
            x = jnp.where(gap > 0, x, jnp.where(gap == 0, 0.5 * x, 0.0))
            x = jnp.where(live, x, 0.0)
            x_high, x_low = split(x)
            high[a * size:(a + 1) * size, b * size:(b + 1) * size] = x_high
            low[a * size:(a + 1) * size, b * size:(b + 1) * size] = x_low
    for b in range(nb):
        left = (high[:, b * size:(b + 1) * size], low[:, b * size:(b + 1) * size])
        first = b % na * size
        mirror[b // na][first:first + size, :] = product(left, right, contract=0)


def forward_kernel(plan, member, high, low, factor, mirror, *rest):
    lanes, size, depth = plan.lanes, plan.tile, plan.depth
    parts, rest = rest[:lanes], rest[lanes:]
    earlier, rest = rest[:lanes * bool(member)], rest[lanes * bool(member):]
    splits = plan.splits[member]
    totals, rest = rest[:splits], rest[splits:]
    cross, (total, whole) = rest[:lanes], rest[lanes:]
    right = [split(part[...]) for part in parts]
    for a in range(plan.na):
        rows = slice(a * size, (a + 1) * size)
        total[rows, :] = sum(
            product(
                (high[rows, i * depth:(i + 1) * depth], low[rows, i * depth:(i + 1) * depth]),
                right[i],
            )
            for i in range(lanes)
        )
    share = depth // splits
    on_diagonal = plan.on_diagonal()
    for i in range(splits):
        rows = slice(i * share, (i + 1) * share)
        totals[i][...] = total[rows, :] + jnp.where(on_diagonal, mirror[rows, :], 0.0)
    whole[...] = product(split(factor[...]), split(total[...]), contract=0)
    share = plan.width // lanes
    lane = lax.rem(lax.axis_index("row"), lanes)
    for i in range(lanes):
        first = pl.multiple_of(lax.rem(lane + i, lanes) * share, share)
        cross[i][member * share:, :] = whole[pl.ds(first, share), :]
        if member:
            cross[i][:member * share, :] = earlier[i][...]


def place_kernel(plan, member, tiles_ref, unit_ref, *rest):
    splits = plan.splits[member]
    sums, rest = rest[:2 * splits], rest[2 * splits:]
    out, stack, zeros, sems, zero_sems = rest[member > 0:]
    size, width = plan.tile, plan.width
    row, at_end = lax.axis_index("row"), plan.at_end()

    def zero_copies(act):
        for other in range(plan.members):
            for t in range(plan.row_tiles):
                taken = False
                for a in range(plan.na):
                    taken = taken | (
                        tiles_ref[other, row * plan.na + a] == row * plan.row_tiles + t
                    )
                copy = pltpu.make_async_copy(
                    zeros,
                    out.at[t * size:(t + 1) * size, other * width:(other + 1) * width],
                    zero_sems.at[other, t],
                )
                pl.when(jnp.logical_not(taken))(functools.partial(act, copy))

    if member == 0:
        zeros[...] = jnp.zeros_like(zeros)
        zero_copies(lambda copy: copy.start())
    right = split(unit_inverse(unit_ref, member))
    share = plan.depth // splits
    for i in range(splits):
        x = jnp.where(at_end, sums[2 * i + 1][...], sums[2 * i][...])
        stack[i * share:(i + 1) * share, :] = -product(split(x), right)
    copies = []
    for a in range(plan.na):
        t = jnp.clip(
            tiles_ref[member, row * plan.na + a] - row * plan.row_tiles, 0, plan.row_tiles - 1
        )
        copy = pltpu.make_async_copy(
            stack.at[a * size:(a + 1) * size, :],
            out.at[
                pl.ds(pl.multiple_of(t * size, size), size), member * width:(member + 1) * width
            ],
            sems.at[a],
        )
        copy.start()
        copies.append(copy)
    for copy in copies:
        copy.wait()
    if member == 0:
        zero_copies(lambda copy: copy.wait())


def diagonal_kernel(plan, pivot, unit_ref, *rest):
    parts, (out, cross) = rest[:plan.lanes], rest[plan.lanes:]
    width, lanes, members = plan.width, plan.lanes, plan.members
    lane = lax.rem(lax.axis_index("row"), lanes)
    count = 1 << plan.steps
    size = members * width // (lanes * count)
    for other in range(lanes):
        mine = plan.place_of(other)
        for place in range(count):
            first = pl.multiple_of((mine ^ place) * size, size)
            piece = parts[0][pl.ds(first, size), :]
            for i in range(1, lanes):
                piece = jnp.where(
                    lax.rem(lane + i, lanes) == other, parts[i][pl.ds(first, size), :], piece
                )
            cross[other, place * size:(place + 1) * size, :] = piece
    share = width // lanes
    row = lax.broadcasted_iota(jnp.int32, (width, width), 0)
    col = lax.broadcasted_iota(jnp.int32, (width, width), 1)
    for member in range(members):
        rows = slice(member * share, (member + 1) * share)
        x = jnp.concatenate([cross[other, rows, :] for other in range(lanes)])
        x = jnp.where(row == col, pivot[member:member + 1, :], 0.0) + x + x.T
        inverse = split(unit_inverse(unit_ref, member))
        half = product(split(x), inverse)
        out[member] = product(inverse, split(half), contract=0)


def reverse(pairs):
    return [(receiver, sender) for sender, receiver in pairs]


def shards(inverse_front, factor, unit_lower, pivot_inverse, tile_list, tile_valid):
    plan = Plan(inverse_front, factor, unit_lower, tile_list)
    width, depth, lanes, members, steps = plan.width, plan.depth, plan.lanes, plan.members, plan.steps
    both = ("row", "col")
    factors = [factor[:, member * width:(member + 1) * width] for member in range(members)]

    def lane_sum(parts):
        out = parts[0]
        for shift in range(1, lanes):
            out = out + plan.swap(parts[lanes - shift], shift)
        return out

    def gather(member):
        return pl.pallas_call(
            functools.partial(gather_kernel, plan, member),
            in_specs=smem(2) + [pl.BlockSpec(memory_space=pl.ANY)] + vmem(1),
            out_specs=vmem(2 + lanes),
            out_shape=[jax.ShapeDtypeStruct((depth, depth * lanes), BF16)] * 2
            + [jax.ShapeDtypeStruct((depth, width), F32)] * lanes,
            scratch_shapes=[
                pltpu.VMEM((plan.na, plan.nb, plan.tile, plan.tile), F32),
                pltpu.SemaphoreType.DMA((plan.na, plan.nb)),
            ],
            compiler_params=PARAMS,
            cost_estimate=COST,
            name="gather_mirror",
        )(tile_list, tile_valid, inverse_front, factors[member])

    def forward(member, high, low, mirror, held, earlier):
        parts = [held] + [plan.swap(held, shift) for shift in range(1, lanes)]
        splits = plan.splits[member]
        outs = pl.pallas_call(
            functools.partial(forward_kernel, plan, member),
            in_specs=vmem(4 + lanes + len(earlier)),
            out_specs=vmem(splits + lanes),
            out_shape=[jax.ShapeDtypeStruct((depth // splits, width), F32)] * splits
            + [jax.ShapeDtypeStruct(((member + 1) * width // lanes, width), F32)] * lanes,
            scratch_shapes=[
                pltpu.VMEM((depth, width), F32),
                pltpu.VMEM((width, width), F32),
            ],
            compiler_params=PARAMS,
            cost_estimate=COST,
            name="forward",
        )(high, low, factors[member], mirror, *parts, *earlier)
        return outs[:splits], outs[splits:], parts[-1]

    hops = plan.line_hops()

    def enter(x, after=()):
        if after:
            x, _ = lax.optimization_barrier((x, tuple(after)))
        return lax.ppermute(x, "col", hops[0])

    def run(x, got, ties=()):
        sent, brought = [], [got]
        for hop in range(1, len(hops)):
            x = plan.line_step(hop - 1, x, got)
            sent.append(x)
            tie = ties[hop - 1] if hop <= len(ties) else ()
            y = lax.optimization_barrier((x, tuple(tie)))[0] if tie else x
            got = lax.ppermute(y, "col", hops[hop])
            brought.append(got)
        if len(hops) == 1:
            got = x = x + got
        return x, got, sent, brought

    spread, collect = Chain(), Chain()
    count = members * steps
    tiles, held, mirror, chunks, entered = {}, {}, {}, [], {}
    after, cross, last_swap = (), [], ()
    for phase in range(count + 1):
        if phase < count:
            out, step = divmod(phase, steps)
            x = factors[out] if step == 0 else held[out]
            got_out, = spread.issue((x, both, plan.tree(step)), after=after)
        if phase:
            back, turn = divmod(phase - 1, steps)
            got_back, = collect.issue(
                (mirror[back], both, reverse(plan.tree(steps - 1 - turn))), after=after
            )
        if chunks and 0 not in entered:
            entered[0] = enter(chunks[0])
            entered[0], got_out, got_back = lax.optimization_barrier(
                (entered[0], got_out, got_back)
            )
        after = ()
        if phase % steps == 0 and phase < count:
            high, low, *parts = gather(out) if out == 0 else tiles[out]
            tiles[out] = (high, low)
            mirror[out] = lane_sum(parts)
        if phase % steps == 1 % steps and phase < count and out + 1 < members:
            tiles[out + 1] = gather(out + 1)
            after = (tiles[out + 1][0],)
        if phase < count:
            held[out] = jnp.where(plan.on_diagonal(), x, got_out) if step == 0 else x + got_out
        if phase:
            if turn < steps - 1:
                mirror[back] = mirror[back] + got_back
            else:
                sums, cross, last_swap = forward(back, *tiles[back], mirror[back], held[back], cross)
                share = sums[0].shape[0]
                after = tuple(
                    part + got_back[i * share:(i + 1) * share] for i, part in enumerate(sums)
                )
                chunks += after

    x, _ = lax.optimization_barrier((lane_sum(cross), after))
    for step in range(steps):
        x = x.reshape(2, x.shape[0] // 2, x.shape[1])
        bit = plan.bit(step)
        send = lax.dynamic_index_in_dim(x, 1 - bit, 0, keepdims=False)
        keep = lax.dynamic_index_in_dim(x, bit, 0, keepdims=False)
        x = keep + lax.ppermute(send, both, plan.bit_pairs(step))
    update = x

    def place(member, column):
        sums, splits = [], plan.splits[member]
        first = sum(plan.splits[:member])
        for i in range(first, first + splits):
            sums += [chunks[i], ends[i]]
        return pl.pallas_call(
            functools.partial(place_kernel, plan, member),
            in_specs=smem(1) + vmem(1 + 2 * splits)
            + [pl.BlockSpec(memory_space=pl.ANY)] * (member > 0),
            out_specs=pl.BlockSpec(memory_space=pl.ANY),
            out_shape=jax.ShapeDtypeStruct((inverse_front.shape[0], factor.shape[1]), F32),
            scratch_shapes=[
                pltpu.VMEM((depth, width), F32),
                pltpu.VMEM((plan.tile, width), F32),
                pltpu.SemaphoreType.DMA((plan.na,)),
                pltpu.SemaphoreType.DMA((members, plan.row_tiles)),
            ],
            input_output_aliases={2 + 2 * splits: 0} if member else {},
            compiler_params=PARAMS,
            cost_estimate=COST,
            name="place",
        )(tile_list, unit_lower, *sums, *([column] if member else []))

    ends, sent, brought, column = {}, {}, {}, None
    last, middle = len(chunks) - 1, len(hops) - 1
    for i in range(last + 1):
        if i > 2:
            entered[i] = enter(chunks[i], (brought[i - 2][min(1, middle)],))
        if i == 1 and last > 1:
            entered[2] = enter(chunks[2])
        ties = [()] * middle
        if i < 2 and i < last and middle:
            if i == 0:
                entered[1] = enter(chunks[1], (entered[0], last_swap))
            ties[-1] = (entered[i + 1],)
        elif i > 1 and middle:
            ties = [(brought[i - 2][hop + 1],) for hop in range(1, middle)]
            ties.append((brought[i - 1][-1],))
        chunks[i], ends[i], sent[i], brought[i] = run(chunks[i], entered[i], ties)
    column = place(0, column)
    ties = [(x,) for x in sent[last]]
    if middle:
        ties[-1] += (column,)
    update, got, _, _ = run(update, enter(update), ties)
    for member in range(1, members):
        column = place(member, column)

    x = update
    x = jnp.where(plan.at_end(), got, x)
    pieces = [x] + [lax.ppermute(x, both, plan.offset_pairs(r)) for r in range(1, 1 << steps)]
    x, _ = lax.optimization_barrier((jnp.concatenate(pieces), tuple(ends.values())))
    parts = [x] + [plan.swap(x, shift) for shift in range(1, lanes)]
    diagonal = pl.pallas_call(
        functools.partial(diagonal_kernel, plan),
        in_specs=vmem(2 + lanes),
        out_specs=vmem(1)[0],
        out_shape=jax.ShapeDtypeStruct(unit_lower.shape, F32),
        scratch_shapes=[pltpu.VMEM((lanes, members * width // lanes, width), F32)],
        compiler_params=PARAMS,
        cost_estimate=COST,
        name="diagonal",
    )(pivot_inverse, unit_lower, *parts)
    return (column, diagonal)


def solution(mesh):
    in_specs = (P("row", "col"), P("row", None), P(), P(), P(), P())
    out_specs = (P("row", None), P())
    return jax.shard_map(shards, mesh=mesh, in_specs=in_specs, out_specs=out_specs, check_vma=False)
```

```python
import functools

import jax
import jax.numpy as jnp
from jax import lax
from jax.experimental import pallas as pl
from jax.experimental.pallas import tpu as pltpu
from jax.sharding import PartitionSpec as P

F32 = jnp.float32
BF16 = jnp.bfloat16
VMEM = pltpu.MemorySpace.VMEM
SMEM = pltpu.MemorySpace.SMEM
COST = pl.CostEstimate(flops=1600 << 20, bytes_accessed=8 << 20, transcendentals=0)
PARAMS = pltpu.CompilerParams(vmem_limit_bytes=48 * 1024 * 1024)


def vmem(count):
    return [pl.BlockSpec(memory_space=VMEM)] * count


def smem(count):
    return [pl.BlockSpec(memory_space=SMEM)] * count


def split(x):
    high = x.astype(BF16)
    return high, (x - high.astype(F32)).astype(BF16)


def product(left, right, contract=1):
    def one(a, b):
        return lax.dot_general(a, b, (((contract,), (0,)), ((), ())), preferred_element_type=F32)

    return one(left[0], right[1]) + one(left[1], right[0]) + one(left[0], right[0])


def unit_inverse(ref, member):
    lower = ref[member]
    row = lax.broadcasted_iota(jnp.int32, lower.shape, 0)
    col = lax.broadcasted_iota(jnp.int32, lower.shape, 1)
    return jnp.where(row > col, lower, jnp.where(row == col, 1.0, 0.0).astype(F32))


class Plan:
    def __init__(self, front, factor, unit_lower, tile_list):
        self.rows, self.cols = lax.axis_size("row"), lax.axis_size("col")
        self.lanes = self.rows // self.cols
        self.members, self.width, _ = unit_lower.shape
        self.na = tile_list.shape[1] // self.rows
        self.tile = factor.shape[0] // self.na
        self.nb = self.na * self.lanes
        self.row_tiles = front.shape[0] // self.tile
        self.col_tiles = front.shape[1] // self.tile
        self.depth = factor.shape[0]
        bits = [1 << i for i in range((self.cols - 1).bit_length())]
        self.orders = [
            bits[lane % len(bits):] + bits[:lane % len(bits)] for lane in range(self.lanes)
        ]
        self.steps = len(bits)
        self.splits = [2] * self.members

    def device(self, chip, lane, col):
        return (chip * self.lanes + lane) * self.cols + col

    def tree(self, step):
        pairs = []
        for col in range(self.cols):
            for lane, order in enumerate(self.orders):
                held, later = [0], [0]
                for bit in order[:step]:
                    held = held + [x ^ bit for x in held]
                for bit in order[step + 1:]:
                    later = later + [x ^ bit for x in later]
                for offset in held:
                    child = col ^ offset ^ order[step]
                    if any(child ^ x > col for x in later):
                        pairs.append(
                            (self.device(col ^ offset, lane, col), self.device(child, lane, col))
                        )
        return pairs

    def swap(self, x, shift):
        pairs = []
        for row in range(self.rows):
            chip, lane = divmod(row, self.lanes)
            pairs.append((chip * self.lanes + (lane + shift) % self.lanes, row))
        return lax.ppermute(x, "row", pairs)

    def line_hops(self):
        count, half = self.cols, self.cols // 2
        inward = [[(i, i + 1), (count - 1 - i, count - 2 - i)] for i in range(half - 1)]
        outward = [
            [(half - 1 - i, half - 2 - i), (half + i, half + i + 1)] for i in range(half - 1)
        ]
        return inward + [[(half - 1, half), (half, half - 1)]] + outward

    def line_step(self, hop, x, got):
        half = self.cols // 2
        if hop < half:
            return x + got
        place, i = lax.axis_index("col"), hop - half
        return jnp.where((place == half - 2 - i) | (place == half + i + 1), got, x)

    def on_diagonal(self):
        return lax.axis_index("row") // self.lanes == lax.axis_index("col")

    def at_end(self):
        place = lax.axis_index("col")
        return (place == 0) | (place == self.cols - 1)

    def bit_pairs(self, step):
        return [
            (self.device(chip, lane, col), self.device(chip ^ order[step], lane, col))
            for chip in range(self.cols)
            for lane, order in enumerate(self.orders)
            for col in range(self.cols)
        ]

    def offset_pairs(self, offset):
        pairs = []
        for lane, order in enumerate(self.orders):
            flip = sum(
                bit for step, bit in enumerate(order) if offset >> (self.steps - 1 - step) & 1
            )
            for chip in range(self.cols):
                for col in range(self.cols):
                    pairs.append(
                        (self.device(chip, lane, col), self.device(chip ^ flip, lane, col))
                    )
        return pairs

    def place_of(self, lane):
        chip, place = lax.axis_index("row") // self.lanes, jnp.int32(0)
        for step, bit in enumerate(self.orders[lane]):
            place = jnp.where((chip & bit) != 0, place + (1 << (self.steps - 1 - step)), place)
        return place

    def bit(self, step):
        row = lax.axis_index("row")
        chip, value = row // self.lanes, jnp.int32(0)
        for lane, order in enumerate(self.orders):
            value = jnp.where((row % self.lanes == lane) & ((chip & order[step]) != 0), 1, value)
        return value


class Chain:
    def __init__(self):
        self.last = ()

    def issue(self, *requests, after=()):
        out = []
        for x, axis, pairs in requests:
            if self.last or after:
                x, _ = lax.optimization_barrier((x, self.last + tuple(after)))
            out.append(lax.ppermute(x, axis, pairs))
        self.last = tuple(out)
        return out


def gather_kernel(plan, member, tiles_ref, valid_ref, front, factor, high, low, *rest):
    mirror, (buffer, sems) = rest[:plan.lanes], rest[plan.lanes:]
    size, na, nb = plan.tile, plan.na, plan.nb
    row, col = lax.axis_index("row"), lax.axis_index("col")
    lane = lax.rem(row, plan.lanes)
    row_slots = [row * na + a for a in range(na)]
    col_slots = [
        col * nb + lax.rem(lane + b // na, plan.lanes) * na + b % na for b in range(nb)
    ]
    copies = []
    for a in range(na):
        for b in range(nb):
            i = jnp.clip(tiles_ref[member, row_slots[a]] - row * plan.row_tiles, 0, plan.row_tiles - 1)
            j = jnp.clip(tiles_ref[member, col_slots[b]] - col * plan.col_tiles, 0, plan.col_tiles - 1)
            copy = pltpu.make_async_copy(
                front.at[
                    pl.ds(pl.multiple_of(i * size, size), size),
                    pl.ds(pl.multiple_of(j * size, size), size),
                ],
                buffer.at[a, b],
                sems.at[a, b],
            )
            copy.start()
            copies.append(copy)
    right = split(factor[...])
    local_row = lax.broadcasted_iota(jnp.int32, (size, size), 0)
    local_col = lax.broadcasted_iota(jnp.int32, (size, size), 1)
    for a in range(na):
        for b in range(nb):
            copies[a * nb + b].wait()
            live = (valid_ref[member, row_slots[a]] > 0) & (valid_ref[member, col_slots[b]] > 0)
            ahead = (tiles_ref[member, row_slots[a]] - tiles_ref[member, col_slots[b]]) * size
            gap = local_row - local_col + ahead
            x = buffer[a, b]
            x = jnp.where(gap > 0, x, jnp.where(gap == 0, 0.5 * x, 0.0))
            x = jnp.where(live, x, 0.0)
            x_high, x_low = split(x)
            high[a * size:(a + 1) * size, b * size:(b + 1) * size] = x_high
            low[a * size:(a + 1) * size, b * size:(b + 1) * size] = x_low
    for b in range(nb):
        left = (high[:, b * size:(b + 1) * size], low[:, b * size:(b + 1) * size])
        first = b % na * size
        mirror[b // na][first:first + size, :] = product(left, right, contract=0)


def forward_kernel(plan, member, high, low, factor, mirror, *rest):
    lanes, size, depth = plan.lanes, plan.tile, plan.depth
    parts, rest = rest[:lanes], rest[lanes:]
    earlier, rest = rest[:lanes * bool(member)], rest[lanes * bool(member):]
    splits = plan.splits[member]
    totals, rest = rest[:splits], rest[splits:]
    cross, (total, whole) = rest[:lanes], rest[lanes:]
    right = [split(part[...]) for part in parts]
    for a in range(plan.na):
        rows = slice(a * size, (a + 1) * size)
        total[rows, :] = sum(
            product(
                (high[rows, i * depth:(i + 1) * depth], low[rows, i * depth:(i + 1) * depth]),
                right[i],
            )
            for i in range(lanes)
        )
    share = depth // splits
    on_diagonal = plan.on_diagonal()
    for i in range(splits):
        rows = slice(i * share, (i + 1) * share)
        totals[i][...] = total[rows, :] + jnp.where(on_diagonal, mirror[rows, :], 0.0)
    whole[...] = product(split(factor[...]), split(total[...]), contract=0)
    share = plan.width // lanes
    lane = lax.rem(lax.axis_index("row"), lanes)
    for i in range(lanes):
        first = pl.multiple_of(lax.rem(lane + i, lanes) * share, share)
        cross[i][member * share:, :] = whole[pl.ds(first, share), :]
        if member:
            cross[i][:member * share, :] = earlier[i][...]


def place_kernel(plan, member, tiles_ref, unit_ref, *rest):
    splits = plan.splits[member]
    sums, rest = rest[:2 * splits], rest[2 * splits:]
    out, stack, zeros, sems, zero_sems = rest[member > 0:]
    size, width = plan.tile, plan.width
    row, at_end = lax.axis_index("row"), plan.at_end()

    def zero_copies(act):
        for other in range(plan.members):
            for t in range(plan.row_tiles):
                taken = False
                for a in range(plan.na):
                    taken = taken | (
                        tiles_ref[other, row * plan.na + a] == row * plan.row_tiles + t
                    )
                copy = pltpu.make_async_copy(
                    zeros,
                    out.at[t * size:(t + 1) * size, other * width:(other + 1) * width],
                    zero_sems.at[other, t],
                )
                pl.when(jnp.logical_not(taken))(functools.partial(act, copy))

    if member == 0:
        zeros[...] = jnp.zeros_like(zeros)
        zero_copies(lambda copy: copy.start())
    right = split(unit_inverse(unit_ref, member))
    share = plan.depth // splits
    for i in range(splits):
        x = jnp.where(at_end, sums[2 * i + 1][...], sums[2 * i][...])
        left, part = split(x), width // 2
        rows = slice(i * share, (i + 1) * share)
        stack[rows, :part] = -product(left, tuple(y[:, :part] for y in right))
        stack[rows, part:] = -product(
            tuple(y[:, part:] for y in left), tuple(y[part:, part:] for y in right)
        )
    copies = []
    for a in range(plan.na):
        t = jnp.clip(
            tiles_ref[member, row * plan.na + a] - row * plan.row_tiles, 0, plan.row_tiles - 1
        )
        copy = pltpu.make_async_copy(
            stack.at[a * size:(a + 1) * size, :],
            out.at[
                pl.ds(pl.multiple_of(t * size, size), size), member * width:(member + 1) * width
            ],
            sems.at[a],
        )
        copy.start()
        copies.append(copy)
    for copy in copies:
        copy.wait()
    if member == 0:
        zero_copies(lambda copy: copy.wait())


def diagonal_kernel(plan, pivot, unit_ref, *rest):
    parts, (out, cross) = rest[:plan.lanes], rest[plan.lanes:]
    width, lanes, members = plan.width, plan.lanes, plan.members
    lane = lax.rem(lax.axis_index("row"), lanes)
    count = 1 << plan.steps
    size = members * width // (lanes * count)
    for other in range(lanes):
        mine = plan.place_of(other)
        for place in range(count):
            first = pl.multiple_of((mine ^ place) * size, size)
            piece = parts[0][pl.ds(first, size), :]
            for i in range(1, lanes):
                piece = jnp.where(
                    lax.rem(lane + i, lanes) == other, parts[i][pl.ds(first, size), :], piece
                )
            cross[other, place * size:(place + 1) * size, :] = piece
    share = width // lanes
    row = lax.broadcasted_iota(jnp.int32, (width, width), 0)
    col = lax.broadcasted_iota(jnp.int32, (width, width), 1)
    for member in range(members):
        rows = slice(member * share, (member + 1) * share)
        x = jnp.concatenate([cross[other, rows, :] for other in range(lanes)])
        x = jnp.where(row == col, pivot[member:member + 1, :], 0.0) + x + x.T
        inverse = split(unit_inverse(unit_ref, member))
        left, part = split(x), width // 2
        lower = tuple(y[part:, :part] for y in inverse)
        upper = tuple(y[:part, :part] for y in inverse)
        corner = tuple(y[part:, part:] for y in inverse)
        right = tuple(y[:, part:] for y in left)
        half = jnp.concatenate(
            [product(left, tuple(y[:, :part] for y in inverse)), product(right, corner)], axis=1
        )
        top, bottom = split(half[:part, :]), split(half[part:, :])
        out[member, :part, :] = product(upper, top, contract=0) + product(lower, bottom, contract=0)
        out[member, part:, :] = product(corner, bottom, contract=0)


def reverse(pairs):
    return [(receiver, sender) for sender, receiver in pairs]


def shards(inverse_front, factor, unit_lower, pivot_inverse, tile_list, tile_valid):
    plan = Plan(inverse_front, factor, unit_lower, tile_list)
    width, depth, lanes, members, steps = plan.width, plan.depth, plan.lanes, plan.members, plan.steps
    both = ("row", "col")
    factors = [factor[:, member * width:(member + 1) * width] for member in range(members)]

    def lane_sum(parts):
        out = parts[0]
        for shift in range(1, lanes):
            out = out + plan.swap(parts[lanes - shift], shift)
        return out

    def gather(member):
        return pl.pallas_call(
            functools.partial(gather_kernel, plan, member),
            in_specs=smem(2) + [pl.BlockSpec(memory_space=pl.ANY)] + vmem(1),
            out_specs=vmem(2 + lanes),
            out_shape=[jax.ShapeDtypeStruct((depth, depth * lanes), BF16)] * 2
            + [jax.ShapeDtypeStruct((depth, width), F32)] * lanes,
            scratch_shapes=[
                pltpu.VMEM((plan.na, plan.nb, plan.tile, plan.tile), F32),
                pltpu.SemaphoreType.DMA((plan.na, plan.nb)),
            ],
            compiler_params=PARAMS,
            cost_estimate=COST,
            name="gather_mirror",
        )(tile_list, tile_valid, inverse_front, factors[member])

    def forward(member, high, low, mirror, held, earlier):
        parts = [held] + [plan.swap(held, shift) for shift in range(1, lanes)]
        splits = plan.splits[member]
        outs = pl.pallas_call(
            functools.partial(forward_kernel, plan, member),
            in_specs=vmem(4 + lanes + len(earlier)),
            out_specs=vmem(splits + lanes),
            out_shape=[jax.ShapeDtypeStruct((depth // splits, width), F32)] * splits
            + [jax.ShapeDtypeStruct(((member + 1) * width // lanes, width), F32)] * lanes,
            scratch_shapes=[
                pltpu.VMEM((depth, width), F32),
                pltpu.VMEM((width, width), F32),
            ],
            compiler_params=PARAMS,
            cost_estimate=COST,
            name="forward",
        )(high, low, factors[member], mirror, *parts, *earlier)
        return outs[:splits], outs[splits:], parts[-1]

    hops = plan.line_hops()

    def enter(x, after=()):
        if after:
            x, _ = lax.optimization_barrier((x, tuple(after)))
        return lax.ppermute(x, "col", hops[0])

    def run(x, got, ties=()):
        sent, brought = [], [got]
        for hop in range(1, len(hops)):
            x = plan.line_step(hop - 1, x, got)
            sent.append(x)
            tie = ties[hop - 1] if hop <= len(ties) else ()
            y = lax.optimization_barrier((x, tuple(tie)))[0] if tie else x
            got = lax.ppermute(y, "col", hops[hop])
            brought.append(got)
        if len(hops) == 1:
            got = x = x + got
        return x, got, sent, brought

    spread, collect = Chain(), Chain()
    count = members * steps
    tiles, held, mirror, chunks, entered = {}, {}, {}, [], {}
    after, cross, last_swap = (), [], ()
    for phase in range(count + 1):
        if phase < count:
            out, step = divmod(phase, steps)
            x = factors[out] if step == 0 else held[out]
            got_out, = spread.issue((x, both, plan.tree(step)), after=after)
        if phase:
            back, turn = divmod(phase - 1, steps)
            got_back, = collect.issue(
                (mirror[back], both, reverse(plan.tree(steps - 1 - turn))), after=after
            )
        if chunks and 0 not in entered:
            entered[0] = enter(chunks[0])
            entered[0], got_out, got_back = lax.optimization_barrier(
                (entered[0], got_out, got_back)
            )
        after = ()
        if phase % steps == 0 and phase < count:
            high, low, *parts = gather(out) if out == 0 else tiles[out]
            tiles[out] = (high, low)
            mirror[out] = lane_sum(parts)
        if phase % steps == 1 % steps and phase < count and out + 1 < members:
            tiles[out + 1] = gather(out + 1)
            after = (tiles[out + 1][0],)
        if phase < count:
            held[out] = jnp.where(plan.on_diagonal(), x, got_out) if step == 0 else x + got_out
        if phase:
            if turn < steps - 1:
                mirror[back] = mirror[back] + got_back
            else:
                sums, cross, last_swap = forward(back, *tiles[back], mirror[back], held[back], cross)
                share = sums[0].shape[0]
                after = tuple(
                    part + got_back[i * share:(i + 1) * share] for i, part in enumerate(sums)
                )
                chunks += after

    x, _ = lax.optimization_barrier((lane_sum(cross), after))
    for step in range(steps):
        x = x.reshape(2, x.shape[0] // 2, x.shape[1])
        bit = plan.bit(step)
        send = lax.dynamic_index_in_dim(x, 1 - bit, 0, keepdims=False)
        keep = lax.dynamic_index_in_dim(x, bit, 0, keepdims=False)
        x = keep + lax.ppermute(send, both, plan.bit_pairs(step))
    update = x

    def place(member, column):
        sums, splits = [], plan.splits[member]
        first = sum(plan.splits[:member])
        for i in range(first, first + splits):
            sums += [chunks[i], ends[i]]
        return pl.pallas_call(
            functools.partial(place_kernel, plan, member),
            in_specs=smem(1) + vmem(1 + 2 * splits)
            + [pl.BlockSpec(memory_space=pl.ANY)] * (member > 0),
            out_specs=pl.BlockSpec(memory_space=pl.ANY),
            out_shape=jax.ShapeDtypeStruct((inverse_front.shape[0], factor.shape[1]), F32),
            scratch_shapes=[
                pltpu.VMEM((depth, width), F32),
                pltpu.VMEM((plan.tile, width), F32),
                pltpu.SemaphoreType.DMA((plan.na,)),
                pltpu.SemaphoreType.DMA((members, plan.row_tiles)),
            ],
            input_output_aliases={2 + 2 * splits: 0} if member else {},
            compiler_params=PARAMS,
            cost_estimate=COST,
            name="place",
        )(tile_list, unit_lower, *sums, *([column] if member else []))

    ends, sent, brought, column = {}, {}, {}, None
    last, middle = len(chunks) - 1, len(hops) - 1
    for i in range(last + 1):
        if i > 2:
            entered[i] = enter(chunks[i], (brought[i - 2][min(1, middle)],))
        if i == 1 and last > 1:
            entered[2] = enter(chunks[2])
        ties = [()] * middle
        if i < 2 and i < last and middle:
            if i == 0:
                entered[1] = enter(chunks[1], (entered[0], last_swap))
            ties[-1] = (entered[i + 1],)
        elif i > 1 and middle:
            ties = [(brought[i - 2][hop + 1],) for hop in range(1, middle)]
            ties.append((brought[i - 1][-1],))
        chunks[i], ends[i], sent[i], brought[i] = run(chunks[i], entered[i], ties)
    column = place(0, column)
    ties = [(x,) for x in sent[last]]
    if middle:
        ties[-1] += (column,)
    update, got, _, _ = run(update, enter(update), ties)
    for member in range(1, members):
        column = place(member, column)

    x = update
    x = jnp.where(plan.at_end(), got, x)
    pieces = [x] + [lax.ppermute(x, both, plan.offset_pairs(r)) for r in range(1, 1 << steps)]
    x, _ = lax.optimization_barrier((jnp.concatenate(pieces), tuple(ends.values())))
    parts = [x] + [plan.swap(x, shift) for shift in range(1, lanes)]
    diagonal = pl.pallas_call(
        functools.partial(diagonal_kernel, plan),
        in_specs=vmem(2 + lanes),
        out_specs=vmem(1)[0],
        out_shape=jax.ShapeDtypeStruct(unit_lower.shape, F32),
        scratch_shapes=[pltpu.VMEM((lanes, members * width // lanes, width), F32)],
        compiler_params=PARAMS,
        cost_estimate=COST,
        name="diagonal",
    )(pivot_inverse, unit_lower, *parts)
    return (column, diagonal)


def solution(mesh):
    in_specs = (P("row", "col"), P("row", None), P(), P(), P(), P())
    out_specs = (P("row", None), P())
    return jax.shard_map(shards, mesh=mesh, in_specs=in_specs, out_specs=out_specs, check_vma=False)
```
